32 devices in a mesh: dp: 16 (over z, y, core), mp: 2 (over x).
Axes of the slice: x: 2, y: 2, z: 4, core: 2. Of those that a mesh axis runs over, the one named last changes fastest.
Arguments:
- inputs: bfloat16 [26624, 1024], P(('dp', 'mp')), may hold values from -6 to 6
- qkv_weight: bfloat16 [1, 3, 1024, 1024], P(None, None, None, 'mp'), may hold values from -0.1875 to 0.1875
- qv_bias: float32 [1, 2, 1024], P(None, None, 'mp'), may hold values from -3 to 3
- out_weight: bfloat16 [1, 1024, 1024], P(None, 'mp'), may hold values from -1.5 to 1.5
- out_bias: float32 [1, 1024], replicated, may hold values from -3 to 3
- norm_gain: float32 [1, 2, 1024], replicated, may hold values from 0.1 to 1.9
- norm_shift: float32 [1, 2, 1024], replicated, may hold values from -3 to 3
- up_weight: bfloat16 [1, 1024, 4096], P(None, None, 'mp'), may hold values from -0.1875 to 0.1875
- up_bias: float32 [1, 4096], P(None, 'mp'), may hold values from -3 to 3
- down_weight: bfloat16 [1, 4096, 1024], P(None, 'mp'), may hold values from -0.09375 to 0.09375
- down_bias: float32 [1, 1024], replicated, may hold values from -3 to 3
- cotangent: bfloat16 [26624, 1024], P(('dp', 'mp')), may hold values from -6 to 6
Outputs:
- output: float32 [26624, 1024], P(('dp', 'mp'))
- input_grad: float32 [26624, 1024], P(('dp', 'mp'))
- qkv_weight_grad: float32 [1, 3, 1024, 1024], P(None, None, None, 'mp')
- qv_bias_grad: float32 [1, 2, 1024], P(None, None, 'mp')
- out_weight_grad: float32 [1, 1024, 1024], P(None, 'mp')
- out_bias_grad: float32 [1, 1024], replicated
- norm_gain_grad: float32 [1, 2, 1024], replicated
- norm_shift_grad: float32 [1, 2, 1024], replicated
- up_weight_grad: float32 [1, 1024, 4096], P(None, None, 'mp')
- up_bias_grad: float32 [1, 4096], P(None, 'mp')
- down_weight_grad: float32 [1, 4096, 1024], P(None, 'mp')
- down_bias_grad: float32 [1, 1024], replicated
The draws below stay inside these ranges and needn't reach their ends.
All inputs are finite; a program needn't handle non-finite values.
Results may differ from the reference program's by a relative error of at most 0.013.
The reference program's roundings to bfloat16 on the way count: a program that leaves them out, or rounds other values in their place, can miss the bound.
Values may be sent and summed in bfloat16 or wider, within the bound.
No kernel may reach another device: no remote copies, remote signals or barrier semaphores. Data moves between devices by JAX's collectives and lax.ppermute only.
A program may use at most 192 MiB of HBM per device.

```python
import jax
import jax.numpy as jnp
from jax import lax

D = 1024
HEADS = 16
HEAD = 64
FF = 4096
PAGE = 416
LAYERS = 1
PAGES_DEV = 4
TOKENS = 26624


def level_of(key, extent, split, smallest, largest):
    level = 1.0
    for position, blocks in split:
        draws = jax.random.uniform(jax.random.fold_in(jax.random.fold_in(key, 6), position), (blocks,), jnp.float32, smallest / len(split), largest / len(split))
        level = level * jnp.repeat(jnp.exp(draws), extent[position] // blocks).reshape((-1,) + (1,) * (len(extent) - 1 - position))
    return level


def scatter_about(rng, dims, deviation, bound, cuts=(), kind=jnp.bfloat16):
    gain = level_of(rng, dims, cuts, -0.22, 0.18) if cuts else 1.0
    entries = jax.random.normal(rng, dims, jnp.float32) * deviation * gain
    return jnp.minimum(jnp.maximum(entries, -bound), bound).astype(kind)


def setup_inputs(seed: int = 0) -> dict:
    splits = jax.random.split(jax.random.key(seed), 13)
    return {
        "inputs": scatter_about(splits[0], (TOKENS, D), 1.0, 6.0, ((0, 32),)),
        "qkv_weight": scatter_about(splits[1], (LAYERS, 3, D, D), D ** -0.5, 0.1875, ((3, 2),)),
        "qv_bias": scatter_about(splits[2], (LAYERS, 2, D), 0.5, 3.0, ((2, 2),), jnp.float32),
        "out_weight": scatter_about(splits[3], (LAYERS, D, D), (D // 64) ** -0.5, 1.5, ((1, 2),)),
        "out_bias": scatter_about(splits[4], (LAYERS, D), 0.5, 3.0, (), jnp.float32),
        "norm_gain": jnp.clip(1.0 + 0.18 * jax.random.normal(splits[5], (LAYERS, 2, D), jnp.float32), 0.1, 1.9),
        "norm_shift": scatter_about(splits[6], (LAYERS, 2, D), 0.5, 3.0, (), jnp.float32),
        "up_weight": scatter_about(splits[7], (LAYERS, D, FF), D ** -0.5, 0.1875, ((2, 2),)),
        "up_bias": scatter_about(splits[8], (LAYERS, FF), 0.5, 3.0, ((1, 2),), jnp.float32),
        "down_weight": scatter_about(splits[9], (LAYERS, FF, D), FF ** -0.5, 0.09375, ((1, 2),)),
        "down_bias": scatter_about(splits[10], (LAYERS, D), 0.5, 3.0, (), jnp.float32),
        "cotangent": scatter_about(splits[11], (TOKENS, D), 1.0, 6.0, ((0, 32),)),
    }


EPSILON = 1e-05
ACCURATE = lax.Precision.HIGHEST

@jax.custom_vjp
def low(v):
    return lax.optimization_barrier(v.astype(jnp.bfloat16)).astype(jnp.float32)

@jax.custom_vjp
def low_back(v):
    return v

def low_keep(v):
    return (low(v), None)

def low_pass(kept, grad):
    return (grad,)

def back_keep(v):
    return (v, None)

def back_low(kept, grad):
    return (low(grad),)
low.defvjp(low_keep, low_pass)
low_back.defvjp(back_keep, back_low)

def norm_rows(matrix, norm_scale, norm_offset):
    average = lax.optimization_barrier(jnp.mean(matrix, axis=-1, keepdims=True))
    centered = matrix - average
    variance = lax.optimization_barrier(jnp.mean(centered * centered, axis=-1, keepdims=True))
    return centered * lax.rsqrt(variance + EPSILON) * norm_scale + norm_offset

def layer_apply(matrix, weights):
    qkv_w, qv_b, out_w, out_b, gains, shifts, up_w, up_b, down_w, down_b = weights
    x_low = low(matrix)
    queries = low(low_back((jnp.dot(x_low, qkv_w[0], precision=ACCURATE) + qv_b[0]) * 0.125))
    key_rows = low(low_back(jnp.dot(x_low, qkv_w[1], precision=ACCURATE)))
    values = low(low_back(jnp.dot(x_low, qkv_w[2], precision=ACCURATE) + qv_b[1]))
    layout = (-1, PAGE, HEADS, HEAD)
    queries = queries.reshape(layout)
    key_rows = key_rows.reshape(layout)
    values = values.reshape(layout)
    scores = low_back(jnp.einsum('pqhd,pkhd->phqk', queries, key_rows, precision=ACCURATE))
    row_max = lax.optimization_barrier(jnp.max(scores, axis=-1, keepdims=True))
    exponent = jnp.exp(scores - row_max)
    probability = exponent / lax.optimization_barrier(jnp.sum(exponent, axis=-1, keepdims=True))
    weights_low = low(probability)
    attended = jnp.einsum('phqk,pkhd->pqhd', weights_low, values, precision=ACCURATE).reshape(matrix.shape)
    attended = low(low_back(attended))
    branch = low_back(jnp.dot(attended, out_w, precision=ACCURATE)) + out_b
    hidden = norm_rows(matrix + branch, gains[0], shifts[0])
    hidden_low = low(hidden)
    pre_gelu = low_back(jnp.dot(hidden_low, up_w, precision=ACCURATE) + up_b)
    active = low(jax.nn.gelu(pre_gelu, approximate=False))
    branch_two = low_back(jnp.dot(active, down_w, precision=ACCURATE)) + down_b
    return norm_rows(hidden + branch_two, gains[1], shifts[1])

def reference(inputs, qkv_weight, qv_bias, out_weight, out_bias, norm_gain, norm_shift, up_weight, up_bias, down_weight, down_bias, cotangent):
    params = (qkv_weight.astype(jnp.float32), qv_bias, out_weight.astype(jnp.float32), out_bias, norm_gain, norm_shift, up_weight.astype(jnp.float32), up_bias, down_weight.astype(jnp.float32), down_bias)

    def forward(rows_all, layer_params):
        grouped = rows_all.reshape(-1, PAGES_DEV * PAGE, D)

        def one_group(matrix):
            for layer_number in range(LAYERS):
                matrix = layer_apply(matrix, tuple((entry[layer_number] for entry in layer_params)))
            return matrix
        return lax.map(jax.checkpoint(one_group), grouped).reshape(rows_all.shape)
    output, pullback = jax.vjp(forward, inputs.astype(jnp.float32), params)
    input_grad, grads = pullback(cotangent.astype(jnp.float32))
    return (output, input_grad, grads[0], grads[1], grads[2], grads[3], grads[4], grads[5], grads[6], grads[7], grads[8], grads[9])
```

```python
import jax
import jax.numpy as jnp
from jax import lax
from jax.experimental import pallas as pl
from jax.experimental.pallas import tpu as pltpu
from jax.sharding import PartitionSpec as P

HEAD = 64
PAGE = 416
LANES = 128

EPSILON = 1e-05
F32 = jnp.float32
LOW = jnp.bfloat16

def norm_rows(matrix, norm_scale, norm_offset):
    average = jnp.mean(matrix, axis=-1, keepdims=True)
    centered = matrix - average
    variance = jnp.mean(centered * centered, axis=-1, keepdims=True)
    return centered * lax.rsqrt(variance + EPSILON) * norm_scale + norm_offset


def exact_gelu(matrix):
    return jax.nn.gelu(matrix, approximate=False)


def spread_rows(rows_low, project):
    return project(lax.all_gather(rows_low, "mp", axis=0, tiled=True), jnp.int32(0))


def sum_rows(term, shard_rows):
    return lax.psum_scatter(
        term(jnp.int32(0), lax.axis_size("mp") * shard_rows), "mp", scatter_dimension=0, tiled=True
    )


def grad_fold(portion, acts, weight):
    weight_grad = lax.dot_general(
        acts, portion, (((0,), (0,)), ((), ())), preferred_element_type=jnp.float32
    )
    product = lax.dot_general(
        portion, weight, (((1,), (1,)), ((), ())), preferred_element_type=jnp.float32
    )
    return (product, weight_grad)


def spread_grads(grad_low, acts, weight):
    return grad_fold(lax.all_gather(grad_low, "mp", axis=0, tiled=True), acts=acts, weight=weight)


def sum_grads(term, shard_rows):
    return lax.psum_scatter(
        term(jnp.int32(0), lax.axis_size("mp") * shard_rows), "mp", scatter_dimension=0, tiled=True
    )


def page_forward(page_items):
    queries, key_rows, values = page_items
    scores = jnp.einsum("qhd,khd->hqk", queries, key_rows, preferred_element_type=jnp.float32)
    row_max = jnp.max(scores, axis=-1, keepdims=True)
    exponent = jnp.exp(scores - row_max)
    denominator = jnp.sum(exponent, axis=-1, keepdims=True)
    weights_low = (exponent / denominator).astype(jnp.bfloat16)
    log_total = row_max + jnp.log(denominator)
    attended = jnp.einsum("hqk,khd->qhd", weights_low, values, preferred_element_type=jnp.float32)
    return (attended.astype(jnp.bfloat16), log_total)


def page_backward(page_items):
    queries, key_rows, values, log_total, grad_mix = page_items
    scores = jnp.einsum("qhd,khd->hqk", queries, key_rows, preferred_element_type=jnp.float32)
    probability = jnp.exp(scores - log_total)
    weights_low = probability.astype(jnp.bfloat16)
    grad_prob = jnp.einsum("qhd,khd->hqk", grad_mix, values, preferred_element_type=jnp.float32)
    inner_total = jnp.sum(probability * grad_prob, axis=-1, keepdims=True)
    grad_scores = (probability * (grad_prob - inner_total)).astype(jnp.bfloat16)
    grad_q = jnp.einsum("hqk,khd->qhd", grad_scores, key_rows, preferred_element_type=jnp.float32)
    grad_k = jnp.einsum("hqk,qhd->khd", grad_scores, queries, preferred_element_type=jnp.float32)
    grad_v = jnp.einsum("hqk,qhd->khd", weights_low, grad_mix, preferred_element_type=jnp.float32)
    return (grad_q.astype(jnp.bfloat16), grad_k.astype(jnp.bfloat16), grad_v.astype(jnp.bfloat16))


def layer_forward(x_shard, params):
    qkv_w, qv_b, out_w, out_b, gains, shifts, up_w, up_b, down_w, down_b = params
    shard_rows = x_shard.shape[0]

    def project_qkv(portion, offset):
        return (
            jnp.einsum("rd,kde->rke", portion, qkv_w, preferred_element_type=jnp.float32),
            portion,
        )

    qkv_all, x_all = spread_rows(x_shard.astype(jnp.bfloat16), project_qkv)
    token_count = qkv_all.shape[0]
    local_width = qkv_all.shape[2]
    layout = (token_count // PAGE, PAGE, local_width // HEAD, HEAD)
    queries = ((qkv_all[:, 0] + qv_b[0]) * 0.125).astype(jnp.bfloat16).reshape(layout)
    key_rows = qkv_all[:, 1].astype(jnp.bfloat16).reshape(layout)
    values = (qkv_all[:, 2] + qv_b[1]).astype(jnp.bfloat16).reshape(layout)
    attended, log_total = lax.map(jax.checkpoint(page_forward), (queries, key_rows, values))
    attended = attended.reshape(token_count, local_width)

    def project_out(offset, amount):
        return jnp.dot(attended, out_w, preferred_element_type=jnp.float32)

    pre_first = x_shard + sum_rows(project_out, shard_rows) + out_b
    hidden = norm_rows(pre_first, gains[0], shifts[0])

    def project_up(portion, offset):
        return (jnp.dot(portion, up_w, preferred_element_type=jnp.float32), portion)

    pre_gelu, hidden_all = spread_rows(hidden.astype(jnp.bfloat16), project_up)
    pre_gelu = pre_gelu + up_b
    active = exact_gelu(pre_gelu).astype(jnp.bfloat16)

    def project_down(offset, amount):
        return jnp.dot(active, down_w, preferred_element_type=jnp.float32)

    pre_second = hidden + sum_rows(project_down, shard_rows) + down_b
    layer_out = norm_rows(pre_second, gains[1], shifts[1])
    stored = (
        x_shard,
        x_all,
        queries,
        key_rows,
        values,
        log_total,
        attended,
        pre_first,
        hidden_all,
        pre_gelu,
        active,
        pre_second,
        out_w,
    )
    return (layer_out, stored)


def layer_backward(grad_out, stored, params):
    qkv_w, qv_b, out_w, out_b, gains, shifts, up_w, up_b, down_w, down_b = params
    (
        x_shard,
        x_all,
        queries,
        key_rows,
        values,
        log_total,
        attended,
        pre_first,
        hidden_all,
        pre_gelu,
        active,
        pre_second,
        out_full,
    ) = stored
    shard_rows = grad_out.shape[0]
    norm_result, norm_back = jax.vjp(norm_rows, pre_second, gains[1], shifts[1])
    grad_second, gain_two, shift_two = norm_back(grad_out)
    grad_down_bias = jnp.sum(grad_second, axis=0)
    grad_active, grad_down = spread_grads(grad_second.astype(jnp.bfloat16), active, down_w)
    gelu_result, gelu_back = jax.vjp(exact_gelu, pre_gelu)
    grad_pre_low = gelu_back(grad_active)[0].astype(jnp.bfloat16)
    grad_up_bias = jnp.sum(grad_pre_low.astype(jnp.float32), axis=0)
    grad_up = lax.dot_general(
        hidden_all, grad_pre_low, (((0,), (0,)), ((), ())), preferred_element_type=jnp.float32
    )

    def back_up(offset, amount):
        return lax.dot_general(
            grad_pre_low, up_w, (((1,), (1,)), ((), ())), preferred_element_type=jnp.float32
        )

    grad_hidden = grad_second + sum_grads(back_up, shard_rows)
    norm_result, norm_back = jax.vjp(norm_rows, pre_first, gains[0], shifts[0])
    grad_first, gain_one, shift_one = norm_back(grad_hidden)
    grad_out_bias = jnp.sum(grad_first, axis=0)
    grad_first_low = grad_first.astype(jnp.bfloat16)
    grad_attended, grad_out_w = spread_grads(grad_first_low, attended, out_w)
    token_count = grad_attended.shape[0]
    local_width = grad_attended.shape[1]
    grad_mix = grad_attended.astype(jnp.bfloat16).reshape(queries.shape)
    grad_q, grad_k, grad_v = lax.map(
        jax.checkpoint(page_backward), (queries, key_rows, values, log_total, grad_mix)
    )
    flat_q = grad_q.reshape(token_count, local_width) * 0.125
    flat_k = grad_k.reshape(token_count, local_width)
    flat_v = grad_v.reshape(token_count, local_width)
    grad_qkv = jnp.stack([flat_q, flat_k, flat_v], axis=1)
    grad_qv_bias = jnp.stack(
        [jnp.sum(flat_q.astype(jnp.float32), axis=0), jnp.sum(flat_v.astype(jnp.float32), axis=0)]
    )
    grad_qkv_w = jnp.einsum("rd,rke->kde", x_all, grad_qkv, preferred_element_type=jnp.float32)

    def back_qkv(offset, amount):
        return jnp.einsum("rke,kde->rd", grad_qkv, qkv_w, preferred_element_type=jnp.float32)

    grad_x = grad_first + sum_grads(back_qkv, shard_rows)
    split_grads = (grad_qkv_w, grad_qv_bias, grad_out_w, grad_up, grad_up_bias, grad_down)
    shared_grads = (
        grad_out_bias,
        jnp.stack([gain_one, gain_two]),
        jnp.stack([shift_one, shift_two]),
        grad_down_bias,
    )
    return (grad_x, split_grads, shared_grads)


def spread_body(
    inputs,
    qkv_weight,
    qv_bias,
    out_weight,
    out_bias,
    norm_gain,
    norm_shift,
    up_weight,
    up_bias,
    down_weight,
    down_bias,
    cotangent,
):
    layer_total = qkv_weight.shape[0]

    def params_of(layer_number):
        return (
            qkv_weight[layer_number],
            qv_bias[layer_number],
            out_weight[layer_number],
            out_bias[layer_number],
            norm_gain[layer_number],
            norm_shift[layer_number],
            up_weight[layer_number],
            up_bias[layer_number],
            down_weight[layer_number],
            down_bias[layer_number],
        )

    current = inputs.astype(jnp.float32)
    layer_number = 0
    layer_in = current
    current, stored = layer_forward(current, params_of(layer_number))
    kept_list = [layer_in]
    grad_rows = cotangent.astype(jnp.float32)
    split_list = []
    shared_list = []
    for layer_number in reversed(range(layer_total)):
        stored = layer_forward(kept_list[layer_number], params_of(layer_number))[1]
        grad_rows, split_grads, shared_grads = layer_backward(
            grad_rows, stored, params_of(layer_number)
        )
        qkv_part, bias_part, out_part, up_part, upb_part, down_part = split_grads
        split_grads = lax.psum((qkv_part, bias_part, out_part, up_part, upb_part, down_part), "dp")
        outb_part, gain_part, shift_part, downb_part = shared_grads
        shared_grads = lax.psum((outb_part, gain_part, shift_part, downb_part), ("dp", "mp"))
        split_list.insert(0, split_grads)
        shared_list.insert(0, shared_grads)
    split_all = tuple((jnp.stack([entry[member] for entry in split_list]) for member in range(6)))
    shared_all = tuple((jnp.stack([entry[member] for entry in shared_list]) for member in range(4)))
    return (
        current,
        grad_rows,
        split_all[0],
        split_all[1],
        split_all[2],
        shared_all[0],
        shared_all[1],
        shared_all[2],
        split_all[3],
        split_all[4],
        split_all[5],
        shared_all[3],
    )


RATE = 0.42
POLY = (
    0.23672758308126046,
    0.24094666497815675,
    0.18682847081810067,
    0.2932523313321973,
    -0.17452300094788806,
    0.4864472432641871,
    -0.34587320596419,
    0.0761939461469462,
)


def gelu_pair(u):
    magnitude = jnp.abs(u)
    t = 1.0 / (1.0 + (RATE * 0.5**0.5) * magnitude)
    total = jnp.full_like(u, 0.5 * POLY[-1])
    for factor in POLY[-2::-1]:
        total = total * t + 0.5 * factor
    bell = jnp.exp(u * u * -0.5)
    tail = total * t * bell
    below = jnp.where(u >= 0, 1.0 - tail, tail)
    return u * below, below + u * bell * 0.3989422804014327


def matmul(left, right, left_dim=1, right_dim=0):
    return lax.dot_general(
        left, right, (((left_dim,), (right_dim,)), ((), ())), preferred_element_type=F32
    )


def head_mask(which):
    lane = lax.broadcasted_iota(jnp.int32, (1, LANES), 1)
    return (lane // HEAD) == which


def attend_kernel(q_ref, k_ref, v_ref, o_ref, lse_ref):
    queries, key_rows, values = q_ref[...], k_ref[...], v_ref[...]
    values_t = values.T
    columns = []
    for which in range(LANES // HEAD):
        keys_one = jnp.where(head_mask(which), key_rows, jnp.zeros_like(key_rows))
        scores = matmul(keys_one, queries, 1, 1)
        peak = jnp.max(scores, axis=0, keepdims=True)
        exponent = jnp.exp(scores - peak)
        denominator = jnp.sum(exponent, axis=0, keepdims=True)
        weights_low = (exponent * (1.0 / denominator)).astype(LOW)
        columns.append(matmul(values_t[which * HEAD : (which + 1) * HEAD], weights_low))
        lse_ref[0, 0, which : which + 1, :] = peak + jnp.log(denominator)
    o_ref[...] = jnp.concatenate(columns, axis=0).T.astype(LOW)


def attend_back_kernel(q_ref, k_ref, v_ref, lse_ref, g_ref, dq_ref, dk_ref, dv_ref):
    queries, key_rows, values, grads = q_ref[...], k_ref[...], v_ref[...], g_ref[...]
    keys_t = key_rows.T
    columns, dk_parts, dv_parts = [], [], []
    for which in range(LANES // HEAD):
        mask = head_mask(which)
        keys_one = jnp.where(mask, key_rows, jnp.zeros_like(key_rows))
        scores = matmul(keys_one, queries, 1, 1)
        probability = jnp.exp(scores - lse_ref[0, 0, which : which + 1, :])
        values_one = jnp.where(mask, values, jnp.zeros_like(values))
        grad_prob = matmul(values_one, grads, 1, 1)
        inner = jnp.sum(probability * grad_prob, axis=0, keepdims=True)
        grad_scores = (probability * (grad_prob - inner)).astype(LOW)
        dv_parts.append(matmul(probability.astype(LOW), grads))
        dk_parts.append(matmul(grad_scores, queries))
        columns.append(matmul(keys_t[which * HEAD : (which + 1) * HEAD], grad_scores))
    first = head_mask(0)
    dv_ref[...] = jnp.where(first, dv_parts[0], dv_parts[1]).astype(LOW)
    dk_ref[...] = jnp.where(first, dk_parts[0], dk_parts[1]).astype(LOW)
    grad_q = jnp.concatenate(columns, axis=0).T.astype(LOW)
    dq_ref[...] = (grad_q.astype(F32) * 0.125).astype(LOW)


def head_specs(count):
    return [pl.BlockSpec((PAGE, LANES), lambda page, pair: (page, pair)) for _ in range(count)]


def lse_spec():
    return pl.BlockSpec((1, 1, LANES // HEAD, PAGE), lambda page, pair: (page, pair, 0, 0))


def attend(queries, key_rows, values):
    rows, width = queries.shape
    pages, pairs = rows // PAGE, width // LANES
    area = rows * PAGE * width
    return pl.pallas_call(
        attend_kernel,
        grid=(pages, pairs),
        in_specs=head_specs(3),
        out_specs=head_specs(1) + [lse_spec()],
        out_shape=[
            jax.ShapeDtypeStruct((rows, width), LOW),
            jax.ShapeDtypeStruct((pages, pairs, LANES // HEAD, PAGE), F32),
        ],
        compiler_params=pltpu.CompilerParams(vmem_limit_bytes=48 * 2**20),
        cost_estimate=pl.CostEstimate(
            flops=16 * area, bytes_accessed=8 * rows * width, transcendentals=area // HEAD
        ),
        name="attend",
    )(queries, key_rows, values)


def attend_back(queries, key_rows, values, lse, grads):
    rows, width = queries.shape
    pages, pairs = rows // PAGE, width // LANES
    area = rows * PAGE * width
    return pl.pallas_call(
        attend_back_kernel,
        grid=(pages, pairs),
        in_specs=head_specs(3) + [lse_spec()] + head_specs(1),
        out_specs=head_specs(3),
        out_shape=[jax.ShapeDtypeStruct((rows, width), LOW)] * 3,
        compiler_params=pltpu.CompilerParams(vmem_limit_bytes=48 * 2**20),
        cost_estimate=pl.CostEstimate(
            flops=40 * area, bytes_accessed=14 * rows * width, transcendentals=area // HEAD
        ),
        name="attend_back",
    )(queries, key_rows, values, lse, grads)


UNITS = 512


def expand_kernel(h_ref, w_ref, b_ref, active_ref, slope_ref):
    rows = h_ref.shape[0] // 4
    for part in range(4):
        span = slice(part * rows, (part + 1) * rows)
        value, slope = gelu_pair(matmul(h_ref[span, :], w_ref[...]) + b_ref[...])
        active_ref[span, :] = value.astype(LOW)
        slope_ref[span, :] = slope.astype(LOW)


def expand(hidden_low, weight, bias):
    rows, depth = hidden_low.shape
    units = weight.shape[1]
    column = pl.BlockSpec((rows, UNITS), lambda step: (0, step))
    return pl.pallas_call(
        expand_kernel,
        grid=(units // UNITS,),
        in_specs=[
            pl.BlockSpec((rows, depth), lambda step: (0, 0)),
            pl.BlockSpec((depth, UNITS), lambda step: (0, step)),
            pl.BlockSpec((1, UNITS), lambda step: (0, step)),
        ],
        out_specs=[column, column],
        out_shape=[jax.ShapeDtypeStruct((rows, units), LOW)] * 2,
        compiler_params=pltpu.CompilerParams(vmem_limit_bytes=48 * 2**20),
        cost_estimate=pl.CostEstimate(
            flops=4 * rows * depth * units,
            bytes_accessed=2 * depth * units + 4 * rows * units,
            transcendentals=2 * rows * units,
        ),
        name="expand",
    )(hidden_low, weight, bias)


def contract_back_kernel(g_ref, w_ref, slope_ref, out_ref, bias_ref):
    rows = g_ref.shape[0] // 4
    total = jnp.zeros(bias_ref.shape, F32)
    for part in range(4):
        span = slice(part * rows, (part + 1) * rows)
        grad = matmul(g_ref[span, :], w_ref[...], 1, 1) * slope_ref[span, :].astype(F32)
        grad_low = grad.astype(LOW)
        out_ref[span, :] = grad_low
        total = total + jnp.sum(grad_low.astype(F32), axis=0, keepdims=True)
    bias_ref[...] = total


def contract_back(grad_low, weight, slope):
    rows, depth = grad_low.shape
    units = weight.shape[0]
    column = pl.BlockSpec((rows, UNITS), lambda step: (0, step))
    return pl.pallas_call(
        contract_back_kernel,
        grid=(units // UNITS,),
        in_specs=[
            pl.BlockSpec((rows, depth), lambda step: (0, 0)),
            pl.BlockSpec((UNITS, depth), lambda step: (step, 0)),
            column,
        ],
        out_specs=[column, pl.BlockSpec((1, UNITS), lambda step: (0, step))],
        out_shape=[
            jax.ShapeDtypeStruct((rows, units), LOW),
            jax.ShapeDtypeStruct((1, units), F32),
        ],
        compiler_params=pltpu.CompilerParams(vmem_limit_bytes=48 * 2**20),
        cost_estimate=pl.CostEstimate(
            flops=2 * rows * depth * units,
            bytes_accessed=2 * depth * units + 4 * rows * units,
            transcendentals=0,
        ),
        name="contract_back",
    )(grad_low, weight, slope)


def swap(value, distance, axis="dp"):
    count = lax.axis_size(axis)
    return lax.ppermute(value, axis, [(place, place ^ distance) for place in range(count)])


def bit_of(place, distance):
    return (place // distance) % 2


def cut(value, number, count, axis):
    size = value.shape[axis] // count
    return lax.dynamic_slice_in_dim(value, number * size, size, axis)


def ordered(bit, mine, theirs, axis):
    return jnp.where(
        bit == 0,
        jnp.concatenate([mine, theirs], axis),
        jnp.concatenate([theirs, mine], axis),
    )


SHARERS = (1, 2, 4)


def fetch_other(weight, axis):
    place = lax.axis_index("dp")
    number = place % 8
    piece = swap(cut(weight, number, 8, axis), 1, "mp")
    beside = swap(piece, 2)
    above = swap(piece, 4)
    half = piece.shape[axis] // 2
    low_part = swap(lax.slice_in_dim(beside, 0, half, axis=axis), 4)
    high_part = swap(lax.slice_in_dim(above, half, 2 * half, axis=axis), 2)
    across = jnp.concatenate([low_part, high_part], axis)
    mine = jnp.concatenate([piece, beside, above, across], axis)
    both = jnp.concatenate([mine, swap(mine, 1)], axis)
    whole = both
    size = piece.shape[axis]
    for slot, relative in enumerate((0, 2, 4, 6, 1, 3, 5, 7)):
        whole = lax.dynamic_update_slice_in_dim(
            whole,
            lax.slice_in_dim(both, slot * size, (slot + 1) * size, axis=axis),
            (number ^ relative) * size,
            axis,
        )
    return whole


def reduce_gradient(own_keep, own_send, other_keep, other_send):
    place = lax.axis_index("dp")
    count = lax.axis_size("dp")
    from_other = swap(other_send.astype(LOW), 1)
    from_own = swap(own_send.astype(LOW), 1)
    crossing = swap((other_keep + from_other.astype(F32)).astype(LOW), 1, "mp")
    total = (own_keep + from_own.astype(F32) + crossing.astype(F32)).astype(LOW)
    distances = []
    distance = 2
    while distance < count:
        distances.append(distance)
        distance *= 2
    for distance in distances:
        bit = bit_of(place, distance)
        received = swap(cut(total, 1 - bit, 2, 0), distance)
        total = (cut(total, bit, 2, 0).astype(F32) + received.astype(F32)).astype(LOW)
    for distance in reversed(distances):
        total = ordered(bit_of(place, distance), total, swap(total, distance), 0)
    return total, swap(total, 1)


def whole_page_body(
    inputs,
    qkv_weight,
    qv_bias,
    out_weight,
    out_bias,
    norm_gain,
    norm_shift,
    up_weight,
    up_bias,
    down_weight,
    down_bias,
    cotangent,
):
    place = lax.axis_index("dp")
    column = lax.axis_index("mp")
    core = bit_of(place, 1)

    qkv_own, out_own, up_own, down_own = qkv_weight[0], out_weight[0], up_weight[0], down_weight[0]
    qkv_w = (qkv_own, fetch_other(qkv_own, 1))
    out_w = (out_own, fetch_other(out_own, 0))
    up_w = (up_own, fetch_other(up_own, 0))
    down_w = (down_own, fetch_other(down_own, 0))
    biases = jnp.concatenate([qv_bias[0].reshape(-1), up_bias[0]])
    biases = (biases, swap(biases, 1, "mp"))
    width = qv_bias.shape[2]
    q_b = [entry[:width] for entry in biases]
    v_b = [entry[width : 2 * width] for entry in biases]
    up_b = [entry[2 * width :].reshape(1, -1) for entry in biases]
    gains, shifts = norm_gain[0], norm_shift[0]

    x_low = inputs
    x_shard = inputs.astype(F32)
    heads = []
    for half in range(2):
        weight = qkv_w[half]
        queries = ((matmul(x_low, weight[0]) + q_b[half]) * 0.125).astype(LOW)
        key_rows = matmul(x_low, weight[1]).astype(LOW)
        values = (matmul(x_low, weight[2]) + v_b[half]).astype(LOW)
        attended, lse = attend(queries, key_rows, values)
        heads.append((queries, key_rows, values, lse, attended))
    pre_first = x_shard + out_bias[0]
    for half in range(2):
        pre_first = pre_first + matmul(heads[half][4], out_w[half])
    hidden = norm_rows(pre_first, gains[0], shifts[0])
    hidden_low = hidden.astype(LOW)
    units = [expand(hidden_low, up_w[half], up_b[half]) for half in range(2)]
    pre_second = hidden + down_bias[0]
    for half in range(2):
        pre_second = pre_second + matmul(units[half][0], down_w[half])
    layer_out, norm_back = jax.vjp(norm_rows, pre_second, gains[1], shifts[1])
    grad_second, gain_two, shift_two = norm_back(cotangent.astype(F32))

    def weight_gradient(left, right, axis):
        if axis == 0:
            return [matmul(part, right, 0, 0) for part in left]
        return [matmul(left, part, 0, 0) for part in right]

    def by_core(rows):
        return (cut(rows, core, 2, 1), cut(rows, 1 - core, 2, 1))

    grad_second_low = grad_second.astype(LOW)
    second_parts = by_core(grad_second_low)
    hidden_parts = by_core(hidden_low)
    input_parts = by_core(x_low)

    down_parts = [weight_gradient(units[half][0], second_parts, 1) for half in range(2)]
    down_sum = reduce_gradient(*down_parts[0], *down_parts[1])
    grad_down = ordered(core, down_sum[0], down_sum[1], 1).astype(F32)

    back = [contract_back(grad_second_low, down_w[half], units[half][1]) for half in range(2)]
    up_parts = [weight_gradient(hidden_parts, back[half][0], 0) for half in range(2)]
    up_sum = reduce_gradient(*up_parts[0], *up_parts[1])
    grad_up = ordered(core, up_sum[0], up_sum[1], 0).astype(F32)

    grad_hidden = grad_second
    for half in range(2):
        grad_hidden = grad_hidden + matmul(back[half][0], up_w[half], 1, 1)
    norm_result, norm_back = jax.vjp(norm_rows, pre_first, gains[0], shifts[0])
    grad_first, gain_one, shift_one = norm_back(grad_hidden)
    grad_first_low = grad_first.astype(LOW)
    first_parts = by_core(grad_first_low)
    out_parts = [weight_gradient(heads[half][4], first_parts, 1) for half in range(2)]
    out_sum = reduce_gradient(*out_parts[0], *out_parts[1])
    grad_out_w = ordered(core, out_sum[0], out_sum[1], 1).astype(F32)

    grad_x = grad_first
    qkv_parts = []
    qv_sums = []
    for half in (1, 0):
        queries, key_rows, values, lse, attended = heads[half]
        grad_mix = matmul(grad_first_low, out_w[half], 1, 1).astype(LOW)
        three = attend_back(queries, key_rows, values, lse, grad_mix)
        keep, send = (
            jnp.concatenate([matmul(part, entry, 0, 0) for entry in three])
            for part in input_parts
        )
        qkv_parts = [keep, send] + qkv_parts
        for member in range(3):
            grad_x = grad_x + matmul(three[member], qkv_w[half][member], 1, 1)
        qv_sums.insert(0, [jnp.sum(three[member].astype(F32), axis=0) for member in (0, 2)])
    qkv_sum = reduce_gradient(*qkv_parts)
    depth = qkv_own.shape[1] // 2
    grad_qkv = ordered(
        core,
        qkv_sum[0].reshape(3, depth, width),
        qkv_sum[1].reshape(3, depth, width),
        1,
    ).astype(F32)

    split_small = [
        jnp.concatenate(qv_sums[half] + [back[half][1].reshape(-1)]) for half in range(2)
    ]
    shared_small = jnp.concatenate(
        [
            jnp.sum(grad_first, axis=0),
            gain_one,
            gain_two,
            shift_one,
            shift_two,
            jnp.sum(grad_second, axis=0),
        ]
    )
    crossing = swap(jnp.concatenate([split_small[1], shared_small]), 1, "mp")
    small = jnp.concatenate([split_small[0], shared_small]) + crossing
    distance = 1
    while distance < lax.axis_size("dp"):
        small = small + swap(small, distance)
        distance *= 2
    split_width = split_small[0].shape[0]
    grad_qv_bias = small[: 2 * width].reshape(1, 2, width)
    grad_up_bias = small[2 * width : split_width].reshape(1, -1)
    shared = small[split_width:].reshape(6, -1)
    return (
        layer_out,
        grad_x,
        grad_qkv[None],
        grad_qv_bias,
        grad_out_w[None],
        shared[0:1],
        shared[1:3][None],
        shared[3:5][None],
        grad_up[None],
        grad_up_bias,
        grad_down[None],
        shared[5:6],
    )


def body(inputs, *others):
    rows = inputs.shape[0]
    shared = lax.axis_size("mp") == 2 and lax.axis_size("dp") in (8, 16, 32, 64)
    if rows % PAGE == 0 and shared:
        return whole_page_body(inputs, *others)
    return spread_body(inputs, *others)


def solution(mesh):
    placed = (
        P(("dp", "mp"), None),
        P(None, None, None, "mp"),
        P(None, None, "mp"),
        P(None, "mp", None),
        P(),
        P(),
        P(),
        P(None, None, "mp"),
        P(None, "mp"),
        P(None, "mp", None),
        P(),
        P(("dp", "mp"), None),
    )
    return jax.shard_map(
        body,
        mesh=mesh,
        in_specs=placed,
        out_specs=(
            P(("dp", "mp"), None),
            P(("dp", "mp"), None),
            P(None, None, None, "mp"),
            P(None, None, "mp"),
            P(None, "mp", None),
            P(),
            P(),
            P(),
            P(None, None, "mp"),
            P(None, "mp"),
            P(None, "mp", None),
            P(),
        ),
        check_vma=False,
    )
```

```python
import jax
import jax.numpy as jnp
from jax import lax
from jax.experimental import pallas as pl
from jax.experimental.pallas import tpu as pltpu
from jax.sharding import PartitionSpec as P

HEAD = 64
PAGE = 416
LANES = 128

EPSILON = 1e-05
F32 = jnp.float32
LOW = jnp.bfloat16

def norm_rows(matrix, norm_scale, norm_offset):
    average = jnp.mean(matrix, axis=-1, keepdims=True)
    centered = matrix - average
    variance = jnp.mean(centered * centered, axis=-1, keepdims=True)
    return centered * lax.rsqrt(variance + EPSILON) * norm_scale + norm_offset


def exact_gelu(matrix):
    return jax.nn.gelu(matrix, approximate=False)


def spread_rows(rows_low, project):
    return project(lax.all_gather(rows_low, "mp", axis=0, tiled=True), jnp.int32(0))


def sum_rows(term, shard_rows):
    return lax.psum_scatter(
        term(jnp.int32(0), lax.axis_size("mp") * shard_rows), "mp", scatter_dimension=0, tiled=True
    )


def grad_fold(portion, acts, weight):
    weight_grad = lax.dot_general(
        acts, portion, (((0,), (0,)), ((), ())), preferred_element_type=jnp.float32
    )
    product = lax.dot_general(
        portion, weight, (((1,), (1,)), ((), ())), preferred_element_type=jnp.float32
    )
    return (product, weight_grad)


def spread_grads(grad_low, acts, weight):
    return grad_fold(lax.all_gather(grad_low, "mp", axis=0, tiled=True), acts=acts, weight=weight)


def sum_grads(term, shard_rows):
    return lax.psum_scatter(
        term(jnp.int32(0), lax.axis_size("mp") * shard_rows), "mp", scatter_dimension=0, tiled=True
    )


def page_forward(page_items):
    queries, key_rows, values = page_items
    scores = jnp.einsum("qhd,khd->hqk", queries, key_rows, preferred_element_type=jnp.float32)
    row_max = jnp.max(scores, axis=-1, keepdims=True)
    exponent = jnp.exp(scores - row_max)
    denominator = jnp.sum(exponent, axis=-1, keepdims=True)
    weights_low = (exponent / denominator).astype(jnp.bfloat16)
    log_total = row_max + jnp.log(denominator)
    attended = jnp.einsum("hqk,khd->qhd", weights_low, values, preferred_element_type=jnp.float32)
    return (attended.astype(jnp.bfloat16), log_total)


def page_backward(page_items):
    queries, key_rows, values, log_total, grad_mix = page_items
    scores = jnp.einsum("qhd,khd->hqk", queries, key_rows, preferred_element_type=jnp.float32)
    probability = jnp.exp(scores - log_total)
    weights_low = probability.astype(jnp.bfloat16)
    grad_prob = jnp.einsum("qhd,khd->hqk", grad_mix, values, preferred_element_type=jnp.float32)
    inner_total = jnp.sum(probability * grad_prob, axis=-1, keepdims=True)
    grad_scores = (probability * (grad_prob - inner_total)).astype(jnp.bfloat16)
    grad_q = jnp.einsum("hqk,khd->qhd", grad_scores, key_rows, preferred_element_type=jnp.float32)
    grad_k = jnp.einsum("hqk,qhd->khd", grad_scores, queries, preferred_element_type=jnp.float32)
    grad_v = jnp.einsum("hqk,qhd->khd", weights_low, grad_mix, preferred_element_type=jnp.float32)
    return (grad_q.astype(jnp.bfloat16), grad_k.astype(jnp.bfloat16), grad_v.astype(jnp.bfloat16))


def layer_forward(x_shard, params):
    qkv_w, qv_b, out_w, out_b, gains, shifts, up_w, up_b, down_w, down_b = params
    shard_rows = x_shard.shape[0]

    def project_qkv(portion, offset):
        return (
            jnp.einsum("rd,kde->rke", portion, qkv_w, preferred_element_type=jnp.float32),
            portion,
        )

    qkv_all, x_all = spread_rows(x_shard.astype(jnp.bfloat16), project_qkv)
    token_count = qkv_all.shape[0]
    local_width = qkv_all.shape[2]
    layout = (token_count // PAGE, PAGE, local_width // HEAD, HEAD)
    queries = ((qkv_all[:, 0] + qv_b[0]) * 0.125).astype(jnp.bfloat16).reshape(layout)
    key_rows = qkv_all[:, 1].astype(jnp.bfloat16).reshape(layout)
    values = (qkv_all[:, 2] + qv_b[1]).astype(jnp.bfloat16).reshape(layout)
    attended, log_total = lax.map(jax.checkpoint(page_forward), (queries, key_rows, values))
    attended = attended.reshape(token_count, local_width)

    def project_out(offset, amount):
        return jnp.dot(attended, out_w, preferred_element_type=jnp.float32)

    pre_first = x_shard + sum_rows(project_out, shard_rows) + out_b
    hidden = norm_rows(pre_first, gains[0], shifts[0])

    def project_up(portion, offset):
        return (jnp.dot(portion, up_w, preferred_element_type=jnp.float32), portion)

    pre_gelu, hidden_all = spread_rows(hidden.astype(jnp.bfloat16), project_up)
    pre_gelu = pre_gelu + up_b
    active = exact_gelu(pre_gelu).astype(jnp.bfloat16)

    def project_down(offset, amount):
        return jnp.dot(active, down_w, preferred_element_type=jnp.float32)

    pre_second = hidden + sum_rows(project_down, shard_rows) + down_b
    layer_out = norm_rows(pre_second, gains[1], shifts[1])
    stored = (
        x_shard,
        x_all,
        queries,
        key_rows,
        values,
        log_total,
        attended,
        pre_first,
        hidden_all,
        pre_gelu,
        active,
        pre_second,
        out_w,
    )
    return (layer_out, stored)


def layer_backward(grad_out, stored, params):
    qkv_w, qv_b, out_w, out_b, gains, shifts, up_w, up_b, down_w, down_b = params
    (
        x_shard,
        x_all,
        queries,
        key_rows,
        values,
        log_total,
        attended,
        pre_first,
        hidden_all,
        pre_gelu,
        active,
        pre_second,
        out_full,
    ) = stored
    shard_rows = grad_out.shape[0]
    norm_result, norm_back = jax.vjp(norm_rows, pre_second, gains[1], shifts[1])
    grad_second, gain_two, shift_two = norm_back(grad_out)
    grad_down_bias = jnp.sum(grad_second, axis=0)
    grad_active, grad_down = spread_grads(grad_second.astype(jnp.bfloat16), active, down_w)
    gelu_result, gelu_back = jax.vjp(exact_gelu, pre_gelu)
    grad_pre_low = gelu_back(grad_active)[0].astype(jnp.bfloat16)
    grad_up_bias = jnp.sum(grad_pre_low.astype(jnp.float32), axis=0)
    grad_up = lax.dot_general(
        hidden_all, grad_pre_low, (((0,), (0,)), ((), ())), preferred_element_type=jnp.float32
    )

    def back_up(offset, amount):
        return lax.dot_general(
            grad_pre_low, up_w, (((1,), (1,)), ((), ())), preferred_element_type=jnp.float32
        )

    grad_hidden = grad_second + sum_grads(back_up, shard_rows)
    norm_result, norm_back = jax.vjp(norm_rows, pre_first, gains[0], shifts[0])
    grad_first, gain_one, shift_one = norm_back(grad_hidden)
    grad_out_bias = jnp.sum(grad_first, axis=0)
    grad_first_low = grad_first.astype(jnp.bfloat16)
    grad_attended, grad_out_w = spread_grads(grad_first_low, attended, out_w)
    token_count = grad_attended.shape[0]
    local_width = grad_attended.shape[1]
    grad_mix = grad_attended.astype(jnp.bfloat16).reshape(queries.shape)
    grad_q, grad_k, grad_v = lax.map(
        jax.checkpoint(page_backward), (queries, key_rows, values, log_total, grad_mix)
    )
    flat_q = grad_q.reshape(token_count, local_width) * 0.125
    flat_k = grad_k.reshape(token_count, local_width)
    flat_v = grad_v.reshape(token_count, local_width)
    grad_qkv = jnp.stack([flat_q, flat_k, flat_v], axis=1)
    grad_qv_bias = jnp.stack(
        [jnp.sum(flat_q.astype(jnp.float32), axis=0), jnp.sum(flat_v.astype(jnp.float32), axis=0)]
    )
    grad_qkv_w = jnp.einsum("rd,rke->kde", x_all, grad_qkv, preferred_element_type=jnp.float32)

    def back_qkv(offset, amount):
        return jnp.einsum("rke,kde->rd", grad_qkv, qkv_w, preferred_element_type=jnp.float32)

    grad_x = grad_first + sum_grads(back_qkv, shard_rows)
    split_grads = (grad_qkv_w, grad_qv_bias, grad_out_w, grad_up, grad_up_bias, grad_down)
    shared_grads = (
        grad_out_bias,
        jnp.stack([gain_one, gain_two]),
        jnp.stack([shift_one, shift_two]),
        grad_down_bias,
    )
    return (grad_x, split_grads, shared_grads)


def spread_body(
    inputs,
    qkv_weight,
    qv_bias,
    out_weight,
    out_bias,
    norm_gain,
    norm_shift,
    up_weight,
    up_bias,
    down_weight,
    down_bias,
    cotangent,
):
    layer_total = qkv_weight.shape[0]

    def params_of(layer_number):
        return (
            qkv_weight[layer_number],
            qv_bias[layer_number],
            out_weight[layer_number],
            out_bias[layer_number],
            norm_gain[layer_number],
            norm_shift[layer_number],
            up_weight[layer_number],
            up_bias[layer_number],
            down_weight[layer_number],
            down_bias[layer_number],
        )

    current = inputs.astype(jnp.float32)
    layer_number = 0
    layer_in = current
    current, stored = layer_forward(current, params_of(layer_number))
    kept_list = [layer_in]
    grad_rows = cotangent.astype(jnp.float32)
    split_list = []
    shared_list = []
    for layer_number in reversed(range(layer_total)):
        stored = layer_forward(kept_list[layer_number], params_of(layer_number))[1]
        grad_rows, split_grads, shared_grads = layer_backward(
            grad_rows, stored, params_of(layer_number)
        )
        qkv_part, bias_part, out_part, up_part, upb_part, down_part = split_grads
        split_grads = lax.psum((qkv_part, bias_part, out_part, up_part, upb_part, down_part), "dp")
        outb_part, gain_part, shift_part, downb_part = shared_grads
        shared_grads = lax.psum((outb_part, gain_part, shift_part, downb_part), ("dp", "mp"))
        split_list.insert(0, split_grads)
        shared_list.insert(0, shared_grads)
    split_all = tuple((jnp.stack([entry[member] for entry in split_list]) for member in range(6)))
    shared_all = tuple((jnp.stack([entry[member] for entry in shared_list]) for member in range(4)))
    return (
        current,
        grad_rows,
        split_all[0],
        split_all[1],
        split_all[2],
        shared_all[0],
        shared_all[1],
        shared_all[2],
        split_all[3],
        split_all[4],
        split_all[5],
        shared_all[3],
    )


RATE = 0.42
POLY = (
    0.23672758308126046,
    0.24094666497815675,
    0.18682847081810067,
    0.2932523313321973,
    -0.17452300094788806,
    0.4864472432641871,
    -0.34587320596419,
    0.0761939461469462,
)
LARGE = 58 * 2**20
SPEED = 30 * 1.1e9
HEAVY = 1
UNITS = 512
GROUP = 256


def gelu_pair(u):
    t = 1.0 / (1.0 + (RATE * 0.5**0.5) * jnp.abs(u))
    total = 0.5 * POLY[-1] * t + 0.5 * POLY[-2]
    for factor in POLY[-3::-1]:
        total = total * t + 0.5 * factor
    bell = jnp.exp(u * u * -0.5)
    tail = total * t * bell
    below = jnp.where(u >= 0, 1.0 - tail, tail)
    return u * below, below + u * bell * 0.3989422804014327


def matmul(left, right, left_dim=1, right_dim=0):
    return lax.dot_general(
        left, right, (((left_dim,), (right_dim,)), ((), ())), preferred_element_type=F32
    )


def head_mask(which):
    lane = lax.broadcasted_iota(jnp.int32, (1, LANES), 1)
    return (lane // HEAD) == which


def shaped(*dims, kind=F32):
    return jax.ShapeDtypeStruct(dims, kind)


def held(dims):
    return pl.BlockSpec(dims, lambda *place: (0,) * len(dims), pipeline_mode=pl.Buffered(1))


def scalar_spec():
    return pl.BlockSpec(memory_space=pltpu.SMEM)


TIMES = {
    "heads": 8,
    "heads_back": 26,
    "units": 20,
    "units_back": 22,
    "project": 7,
    "turn": 9,
    "first_back": 10,
    "combine": 2,
    "join_rows": 2,
    "take_blocks": 3,
    "split_blocks": 2,
    "join_depth": 3,
    "finish": 6,
}


def cost_of(name):
    return pl.CostEstimate(
        flops=int((TIMES[name] if TIMES[name] < 5 else TIMES[name] * HEAVY) * SPEED), bytes_accessed=1, transcendentals=0
    )


def run(kernel, name, grid, in_specs, out_specs, out_shape, operands, scratch=()):
    return pl.pallas_call(
        kernel,
        grid=grid,
        in_specs=in_specs,
        out_specs=out_specs,
        out_shape=out_shape,
        scratch_shapes=list(scratch),
        compiler_params=pltpu.CompilerParams(vmem_limit_bytes=LARGE),
        cost_estimate=cost_of(name),
        name=name,
    )(*operands)


def spans(pair):
    return [
        slice(start * GROUP + pair * LANES, start * GROUP + (pair + 1) * LANES)
        for start in range(3)
    ]


def gather_depth(order_ref, refs, target, by_column):
    for relative, ref in enumerate(refs):
        span = pl.ds(pl.multiple_of((order_ref[0] ^ relative) * QUARTER, QUARTER), QUARTER)
        if by_column:
            target[:, span] = ref[0]
        else:
            for member in range(3):
                target[span, member * GROUP : (member + 1) * GROUP] = ref[0, member]


QUARTER = 256


def qkv_specs(quarters, part):
    shape = (1, 3, QUARTER, GROUP)
    if len(quarters) == 1:
        return [
            pl.BlockSpec(
                shape,
                lambda page, number=number: (0, 0, number, part),
                pipeline_mode=pl.Buffered(1),
            )
            for number in range(4)
        ]
    return [held(shape)] * 4


def four_times(quarters):
    return list(quarters) * (4 // len(quarters))


def heads_kernel(order_ref, w0_ref, w1_ref, w2_ref, w3_ref, x_ref, b_ref, *refs):
    three_ref, o_ref, lse_ref, weight = refs[-4:]

    @pl.when(pl.program_id(0) == 0)
    def _():
        gather_depth(order_ref, (w0_ref, w1_ref, w2_ref, w3_ref), weight, False)

    scaled = matmul(x_ref[...], weight[...]) + b_ref[...]
    three_ref[:, :GROUP] = (scaled[:, :GROUP] * 0.125).astype(LOW)
    three_ref[:, GROUP:] = scaled[:, GROUP:].astype(LOW)
    for pair in range(GROUP // LANES):
        queries, key_rows, values = (three_ref[:, entry] for entry in spans(pair))
        values_t = values.T
        columns = []
        for which in range(LANES // HEAD):
            head = pair * (LANES // HEAD) + which
            keys_one = jnp.where(head_mask(which), key_rows, jnp.zeros_like(key_rows))
            scores = matmul(keys_one, queries, 1, 1)
            peak = jnp.max(scores, axis=0, keepdims=True)
            exponent = jnp.exp(scores - peak)
            denominator = jnp.sum(exponent, axis=0, keepdims=True)
            weights_low = (exponent * (1.0 / denominator)).astype(LOW)
            columns.append(matmul(values_t[which * HEAD : (which + 1) * HEAD], weights_low))
            lse_ref[0, 0, head : head + 1, :] = peak + jnp.log(denominator)
        o_ref[:, pair * LANES : (pair + 1) * LANES] = (
            jnp.concatenate(columns, axis=0).T.astype(LOW)
        )


def heads_forward(order, quarters, x_low, bias, part, parts, before=()):
    rows, depth = x_low.shape
    width = 3 * GROUP
    pages = rows // PAGE
    count = GROUP // HEAD
    return pl.pallas_call(
        heads_kernel,
        grid=(pages,),
        in_specs=[scalar_spec()]
        + qkv_specs(quarters, part)
        + [pl.BlockSpec((PAGE, depth), lambda page: (page, 0)), held((1, width))]
        + [pl.BlockSpec(memory_space=pl.ANY)] * len(before),
        out_specs=[
            pl.BlockSpec((PAGE, width), lambda page: (page, part)),
            pl.BlockSpec((PAGE, GROUP), lambda page: (page, part)),
            pl.BlockSpec((1, 1, count, PAGE), lambda page: (part, page, 0, 0)),
        ],
        out_shape=[
            shaped(rows, parts * width, kind=LOW),
            shaped(rows, parts * GROUP, kind=LOW),
            shaped(parts, pages, count, PAGE),
        ],
        scratch_shapes=[pltpu.VMEM((depth, width), LOW)],
        input_output_aliases={7 + number: number for number in range(len(before))},
        compiler_params=pltpu.CompilerParams(vmem_limit_bytes=LARGE),
        cost_estimate=cost_of("heads"),
        name="heads",
    )(order, *four_times(quarters), x_low, bias, *before)


def heads_back_kernel(core_ref, order_ref, x_ref, g_ref, before_ref, *refs):
    keep_ref, send_ref, gx_ref, sum_ref = refs[22:26]
    qkv_total, out_total, weight, out_weight = refs[26:]
    side, page = pl.program_id(0), pl.program_id(1)
    pages = pl.num_programs(1)
    core = core_ref[0]
    half = x_ref.shape[1] // 2

    def work(order, first_side, three_ref, lse_ref, att_ref, *weights):
        @pl.when(page == 0)
        def _():
            gather_depth(order, weights[:4], weight, False)
            gather_depth(order, weights[4:], out_weight, True)

        mix = matmul(g_ref[...], out_weight[...], 1, 1).astype(LOW)
        grads_three = [None] * (3 * (GROUP // LANES))
        for pair in range(GROUP // LANES):
            queries, key_rows, values = (three_ref[:, entry] for entry in spans(pair))
            grads = mix[:, pair * LANES : (pair + 1) * LANES]
            keys_t = key_rows.T
            columns, dk_parts, dv_parts = [], [], []
            for which in range(LANES // HEAD):
                head = pair * (LANES // HEAD) + which
                mask = head_mask(which)
                keys_one = jnp.where(mask, key_rows, jnp.zeros_like(key_rows))
                scores = matmul(keys_one, queries, 1, 1)
                probability = jnp.exp(scores - lse_ref[0, 0, head : head + 1, :])
                values_one = jnp.where(mask, values, jnp.zeros_like(values))
                grad_prob = matmul(values_one, grads, 1, 1)
                inner = jnp.sum(probability * grad_prob, axis=0, keepdims=True)
                grad_scores = (probability * (grad_prob - inner)).astype(LOW)
                dv_parts.append(matmul(probability.astype(LOW), grads))
                dk_parts.append(matmul(grad_scores, queries))
                columns.append(matmul(keys_t[which * HEAD : (which + 1) * HEAD], grad_scores))
            first = head_mask(0)
            grad_q = jnp.concatenate(columns, axis=0).T.astype(LOW)
            grads_three[pair] = (grad_q.astype(F32) * 0.125).astype(LOW)
            grads_three[2 + pair] = jnp.where(first, dk_parts[0], dk_parts[1]).astype(LOW)
            grads_three[4 + pair] = jnp.where(first, dv_parts[0], dv_parts[1]).astype(LOW)
        three = jnp.concatenate(grads_three, axis=1)
        start = page == 0
        sums = jnp.sum(three.astype(F32), axis=0, keepdims=True)
        sum_ref[0] = jnp.where(start, 0.0, sum_ref[0]) + sums
        product = matmul(x_ref[...], three, 0, 0)
        qkv_total[...] = jnp.where(start, 0.0, qkv_total[...]) + product
        product = matmul(att_ref[...], g_ref[...], 0, 0)
        out_total[...] = jnp.where(start, 0.0, out_total[...]) + product
        rows = pl.ds(pl.multiple_of(page * PAGE, PAGE), PAGE)
        before = before_ref[...] if first_side else gx_ref[rows, :]
        gx_ref[rows, :] = before + matmul(three, weight[...], 1, 1)

    @pl.when(side == 0)
    def _():
        work((0,), True, *refs[:11])

    @pl.when(side == 1)
    def _():
        work(order_ref, False, *refs[11:22])

    @pl.when(page == pages - 1)
    def _():
        for ref, number in ((keep_ref, core), (send_ref, 1 - core)):
            start = pl.multiple_of(number * half, half)
            for member in range(3):
                span = slice(member * GROUP, (member + 1) * GROUP)
                ref[member] = qkv_total[pl.ds(start, half), span].astype(LOW)
            for member in range(2):
                column = pl.ds(pl.multiple_of(number * half + member * GROUP, GROUP), GROUP)
                ref[3, member * GROUP : (member + 1) * GROUP, :] = out_total[:, column].astype(LOW)


def heads_back(core, order, saved, part, x_low, grad_low, qkv, out, before):
    rows, depth = x_low.shape
    width = 3 * GROUP
    pages = rows // PAGE
    count = GROUP // HEAD
    half = depth // 2
    block = pl.BlockSpec((4, half, GROUP), lambda side, page: (side, 0, 0))
    line = pl.BlockSpec((PAGE, depth), lambda side, page: (page, 0))
    once = pl.BlockSpec(
        (PAGE, depth), lambda side, page: (jnp.where(side == 0, page, pages - 1), 0)
    )
    in_specs, operands = [], []
    for number, side in enumerate(("own", "other")):

        def page_of(side, page, number=number):
            return jnp.where(side == number, page, 0 if number else pages - 1)

        def beside(side, page, page_of=page_of):
            return (page_of(side, page), part)

        def above(side, page, page_of=page_of):
            return (part, page_of(side, page), 0, 0)

        in_specs += [
            pl.BlockSpec((PAGE, width), beside),
            pl.BlockSpec((1, 1, count, PAGE), above),
            pl.BlockSpec((PAGE, GROUP), beside),
        ]
        for quarter in range(4):
            fixed = (0, 0, quarter, part) if side == "own" else (0, 0, 0, 0)
            in_specs.append(
                pl.BlockSpec(
                    (1, 3, QUARTER, GROUP),
                    lambda side, page, fixed=fixed: fixed,
                    pipeline_mode=pl.Buffered(1),
                )
            )
        for quarter in range(4):
            fixed = (0, part, quarter if side == "own" else 0)
            in_specs.append(
                pl.BlockSpec(
                    (1, GROUP, QUARTER),
                    lambda side, page, fixed=fixed: fixed,
                    pipeline_mode=pl.Buffered(1),
                )
            )
        three, attended, lse = saved[side]
        operands += [three, lse, attended, *four_times(qkv[side]), *four_times(out[side])]
    return run(
        heads_back_kernel,
        "heads_back",
        (2, pages),
        [scalar_spec(), scalar_spec(), line, line, once] + in_specs,
        [
            block,
            block,
            held((rows, depth)),
            pl.BlockSpec((1, 1, width), lambda side, page: (side, 0, 0)),
        ],
        [
            shaped(8, half, GROUP, kind=LOW),
            shaped(8, half, GROUP, kind=LOW),
            shaped(rows, depth),
            shaped(2, 1, width),
        ],
        (core, order, x_low, grad_low, before, *operands),
        [
            pltpu.VMEM((depth, width), F32),
            pltpu.VMEM((GROUP, depth), F32),
            pltpu.VMEM((depth, width), LOW),
            pltpu.VMEM((GROUP, depth), LOW),
        ],
    )


ROW_STEPS = 4


def pair_specs(pair, shape, axis, first=0):
    def place(step, number):
        return (0, number, step + first) if axis == 1 else (0, step + first, number)

    if len(pair) == 1:
        return [
            pl.BlockSpec((1,) + shape, lambda step, number=number: place(step, number))
            for number in range(2)
        ]
    return [pl.BlockSpec((1,) + shape, lambda step: place(step, 0)) for _ in range(2)]


def twice(pair):
    return list(pair) * (2 // len(pair))


def depth_spans(order_ref, half):
    return [
        pl.ds(pl.multiple_of((order_ref[0] ^ relative) * half, half), half)
        for relative in range(2)
    ]


def units_kernel(order_ref, h_ref, up_a, up_b, b_ref, down_a, down_b, *outs):
    active_ref, slope_ref, total_ref = outs
    rows = h_ref.shape[0] // ROW_STEPS
    first, second = depth_spans(order_ref, h_ref.shape[1] // 2)
    for part in range(ROW_STEPS):
        span = slice(part * rows, (part + 1) * rows)
        pre = matmul(h_ref[span, first], up_a[0]) + matmul(h_ref[span, second], up_b[0])
        value, slope = gelu_pair(pre + b_ref[...])
        value = value.astype(LOW)
        active_ref[span, :] = value
        slope_ref[span, :] = slope.astype(LOW)
        for place, weight in ((first, down_a), (second, down_b)):
            before = jnp.where(pl.program_id(0) == 0, 0.0, total_ref[span, place])
            total_ref[span, place] = before + matmul(value, weight[0])


def units_forward(order, hidden_low, up, bias, down):
    rows, depth = hidden_low.shape
    units = bias.shape[1]
    half = depth // 2
    column = pl.BlockSpec((rows, UNITS), lambda step: (0, step))
    return run(
        units_kernel,
        "units",
        (units // UNITS,),
        [scalar_spec(), held((rows, depth))]
        + pair_specs(up, (half, UNITS), 1)
        + [pl.BlockSpec((1, UNITS), lambda step: (0, step))]
        + pair_specs(down, (UNITS, half), 2),
        [column, column, held((rows, depth))],
        [shaped(rows, units, kind=LOW), shaped(rows, units, kind=LOW), shaped(rows, depth)],
        (order, hidden_low, *twice(up), bias, *twice(down)),
    )


def units_back_kernel(core_ref, order_ref, g_ref, h_ref, *refs):
    keep_ref, send_ref, total_ref, sum_ref = refs[-4:]
    core = core_ref[0]
    half = g_ref.shape[1] // 2
    step = pl.program_id(0)
    steps = pl.num_programs(0) // 2

    def work(order, active_ref, slope_ref, up_a, up_b, down_a, down_b):
        first, second = depth_spans(order, half)
        grad = matmul(g_ref[:, first], down_a[0], 1, 1)
        grad = grad + matmul(g_ref[:, second], down_b[0], 1, 1)
        grad_low = (grad * slope_ref[...].astype(F32)).astype(LOW)
        sum_ref[0] = jnp.sum(grad_low.astype(F32), axis=0, keepdims=True)
        for place, weight in ((first, up_a), (second, up_b)):
            before = jnp.where(step == 0, 0.0, total_ref[:, place])
            total_ref[:, place] = before + matmul(grad_low, weight[0], 1, 1)
        for ref, number in ((keep_ref, core), (send_ref, 1 - core)):
            span = pl.ds(pl.multiple_of(number * half, half), half)
            ref[0] = matmul(active_ref[...], g_ref[:, span], 0, 0).astype(LOW)
            ref[1] = matmul(h_ref[:, span], grad_low, 0, 0).astype(LOW)

    @pl.when(step < steps)
    def _():
        work((0,), *refs[:6])

    @pl.when(step >= steps)
    def _():
        work(order_ref, *refs[6:12])


def units_back(core, order, grad_low, hidden_low, units, up, down, part, parts):
    rows, depth = hidden_low.shape
    here = units["own"][0].shape[1] // parts
    half = depth // 2
    steps = here // UNITS
    first = part * steps
    in_specs, operands = [], []
    for side, least in (("own", 0), ("other", steps)):

        def number(step, least=least):
            return first + jnp.clip(step - least, 0, steps - 1)

        column = pl.BlockSpec((rows, UNITS), lambda step, number=number: (0, number(step)))
        in_specs += [column, column]
        for axis, pair, shape in ((1, up, (half, UNITS)), (2, down, (UNITS, half))):
            for which in range(2):
                fixed = which if side == "own" else 0

                def place(step, axis=axis, fixed=fixed, number=number):
                    moving = number(step)
                    return (0, fixed, moving) if axis == 1 else (0, moving, fixed)

                in_specs.append(pl.BlockSpec((1,) + shape, place))
        operands += [*units[side][:2], *twice(up[side]), *twice(down[side])]
    block = pl.BlockSpec((2, half, UNITS), lambda step: (step, 0, 0))
    return run(
        units_back_kernel,
        "units_back",
        (2 * steps,),
        [scalar_spec(), scalar_spec(), held((rows, depth)), held((rows, depth))] + in_specs,
        [
            block,
            block,
            held((rows, depth)),
            pl.BlockSpec((1, 1, UNITS), lambda step: (step, 0, 0)),
        ],
        [
            shaped(4 * steps, half, UNITS, kind=LOW),
            shaped(4 * steps, half, UNITS, kind=LOW),
            shaped(rows, depth),
            shaped(2 * steps, 1, UNITS),
        ],
        (core, order, grad_low, hidden_low, *operands),
    )


def normal_rows(matrix):
    average = jnp.mean(matrix, axis=-1, keepdims=True)
    centered = matrix - average
    variance = jnp.mean(centered * centered, axis=-1, keepdims=True)
    scale = lax.rsqrt(variance + EPSILON)
    return centered * scale, scale


def normal_back(normal, scale, gain, grad):
    scaled = gain * grad
    level = jnp.mean(scaled, axis=-1, keepdims=True)
    along = jnp.mean(scaled * normal, axis=-1, keepdims=True)
    return scale * (scaled - level - normal * along)


def add_rows(ref, matrix):
    total = jnp.sum(matrix, axis=0, keepdims=True)
    before = jnp.where(pl.program_id(0) == 0, 0.0, ref[...])
    ref[...] = before + total


STRIP = 208


def strip(columns):
    return pl.BlockSpec((STRIP, columns), lambda step: (step, 0))


def project_kernel(order_ref, a_ref, b_ref, wa_ref, w0, w1, w2, w3, x_ref, *refs):
    bias_ref, g_ref, s_ref, first_ref, hidden_ref, low_ref = refs
    first_ref[...] = x_ref[...].astype(F32) + bias_ref[...] + matmul(a_ref[...], wa_ref[0])
    for relative, weight in enumerate((w0, w1, w2, w3)):
        span = pl.ds(pl.multiple_of((order_ref[0] ^ relative) * QUARTER, QUARTER), QUARTER)
        first_ref[:, span] += matmul(b_ref[...], weight[0])
    hidden = normal_rows(first_ref[...])[0] * g_ref[...] + s_ref[...]
    hidden_ref[...] = hidden
    low_ref[...] = hidden.astype(LOW)


def project(order, sides, own, quarters, x_low, bias, gain, shift):
    rows, depth = x_low.shape
    line = held((1, depth))
    page = pl.BlockSpec((PAGE, depth), lambda step: (step, 0))
    side = pl.BlockSpec((PAGE, sides[0].shape[1]), lambda step: (step, 0))
    return run(
        project_kernel,
        "project",
        (rows // PAGE,),
        [scalar_spec(), side, side, held(own.shape)]
        + [held(entry.shape) for entry in quarters]
        + [page, line, line, line],
        [page] * 3,
        [shaped(rows, depth), shaped(rows, depth), shaped(rows, depth, kind=LOW)],
        (order, *sides, own, *quarters, x_low, bias, gain, shift),
    )


def turn_kernel(a_ref, b_ref, h_ref, c_ref, bias_ref, g_ref, s_ref, *outs):
    out_ref, grad_ref, low_ref, gain_ref, shift_ref, sum_ref = outs
    normal, scale = normal_rows(h_ref[...] + (a_ref[...] + b_ref[...]) + bias_ref[...])
    out_ref[...] = normal * g_ref[...] + s_ref[...]
    grad_out = c_ref[...].astype(F32)
    grad = normal_back(normal, scale, g_ref[...], grad_out)
    grad_ref[...] = grad
    low_ref[...] = grad.astype(LOW)
    add_rows(gain_ref, grad_out * normal)
    add_rows(shift_ref, grad_out)
    add_rows(sum_ref, grad)


def turn(sides, hidden, cotangent, bias, gain, shift):
    rows, depth = hidden.shape
    line = pl.BlockSpec((1, depth), lambda step: (0, 0))
    return run(
        turn_kernel,
        "turn",
        (rows // STRIP,),
        [strip(depth)] * 4 + [line] * 3,
        [strip(depth)] * 3 + [line] * 3,
        [shaped(rows, depth), shaped(rows, depth), shaped(rows, depth, kind=LOW)]
        + [shaped(1, depth)] * 3,
        (*sides, hidden, cotangent, bias, gain, shift),
    )


def first_back_kernel(*refs):
    *sides, second_ref, first_ref, g_ref = refs[:-5]
    grad_ref, low_ref, gain_ref, shift_ref, sum_ref = refs[-5:]
    total = second_ref[...]
    for side in sides:
        total = total + side[...]
    normal, scale = normal_rows(first_ref[...])
    grad = normal_back(normal, scale, g_ref[...], total)
    grad_ref[...] = grad
    low_ref[...] = grad.astype(LOW)
    add_rows(gain_ref, total * normal)
    add_rows(shift_ref, total)
    add_rows(sum_ref, grad)


def first_back(sides, grad_second, pre_first, gain):
    rows, depth = pre_first.shape
    line = pl.BlockSpec((1, depth), lambda step: (0, 0))
    return run(
        first_back_kernel,
        "first_back",
        (rows // STRIP,),
        [strip(depth)] * (len(sides) + 2) + [line],
        [strip(depth)] * 2 + [line] * 3,
        [shaped(rows, depth), shaped(rows, depth, kind=LOW)] + [shaped(1, depth)] * 3,
        (*sides, grad_second, pre_first, gain),
    )


def swap(value, distance, axis="dp"):
    count = lax.axis_size(axis)
    return lax.ppermute(value, axis, [(place, place ^ distance) for place in range(count)])


def bit_of(place, distance):
    return jnp.minimum(jnp.bitwise_and(place, distance), 1).astype(jnp.int32)


def cut(value, number, count, axis):
    size = value.shape[axis] // count
    return lax.dynamic_slice_in_dim(value, number * size, size, axis)


def ordered(bit, mine, theirs, axis):
    return jnp.where(
        bit == 0,
        jnp.concatenate([mine, theirs], axis),
        jnp.concatenate([theirs, mine], axis),
    )


def hold(value, *tokens):
    return lax.optimization_barrier((value,) + tokens)[0] if tokens else value


def take_blocks(words, sources):
    count = len(sources)

    def kernel(word_ref, *refs):
        for source, target in zip(refs[:count], refs[count:]):
            target[...] = source[...]

    return pl.pallas_call(
        kernel,
        grid_spec=pltpu.PrefetchScalarGridSpec(
            num_scalar_prefetch=1,
            grid=(1,),
            in_specs=[
                pl.BlockSpec(shape, lambda step, word, index=index: index(word))
                for _, shape, index in sources
            ],
            out_specs=[
                pl.BlockSpec(shape, lambda step, word, shape=shape: (0,) * len(shape))
                for _, shape, _ in sources
            ],
        ),
        out_shape=[shaped(*shape, kind=LOW) for _, shape, _ in sources],
        compiler_params=pltpu.CompilerParams(vmem_limit_bytes=LARGE),
        cost_estimate=cost_of("take_blocks"),
        name="take_blocks",
    )(words, *[array for array, _, _ in sources])


def split_blocks(first, second, axis):
    half = first.shape[axis] // 2
    shape = first.shape[:axis] + (half,) + first.shape[axis + 1 :]

    def kernel(first_ref, second_ref, low_ref, high_ref):
        if axis == 2:
            low_ref[...] = first_ref[:, :, :half]
            high_ref[...] = second_ref[:, :, half:]
        else:
            low_ref[...] = first_ref[:, :half]
            high_ref[...] = second_ref[:, half:]

    return run(
        kernel,
        "split_blocks",
        (1,),
        [held(first.shape), held(second.shape)],
        [held(shape), held(shape)],
        [shaped(*shape, kind=first.dtype)] * 2,
        (first, second),
    )


def join_depth(words, piece, beside, above, low_part, high_part, axis):
    size = piece.shape[axis]
    shape = piece.shape[:axis] + (4 * size,) + piece.shape[axis + 1 :]
    half = low_part.shape[3 - axis]

    def kernel(word_ref, piece_ref, beside_ref, above_ref, low_ref, high_ref, target):
        place = word_ref[2] % 4

        def span(number):
            return pl.ds(pl.multiple_of(number * size, size), size)

        for ref, number in ((piece_ref, place), (beside_ref, place ^ 2), (above_ref, place ^ 1)):
            if axis == 1:
                target[:, span(number)] = ref[...]
            else:
                target[:, :, span(number)] = ref[...]
        last = span(place ^ 3)
        if axis == 1:
            target[:, last, :half] = low_ref[...]
            target[:, last, half:] = high_ref[...]
        else:
            target[:, :half, last] = low_ref[...]
            target[:, half:, last] = high_ref[...]

    entries = [piece, beside, above, low_part, high_part]
    return run(
        kernel,
        "join_depth",
        (1,),
        [scalar_spec()] + [held(entry.shape) for entry in entries],
        held(shape),
        shaped(*shape, kind=piece.dtype),
        (words, *entries),
    )


class FetchQuarters:
    def __init__(self, clock, piece):
        self.clock = clock
        self.piece = swap(piece, 1, "mp")
        self.stages = [self.share, self.last]

    def step(self):
        self.stages.pop(0)()

    def share(self):
        self.piece = self.clock.hold(self.piece)
        self.clock.tick(self.piece)
        self.beside = swap(self.piece, 2)
        self.core_piece = swap(self.piece, 1)

    def last(self):
        self.beside = self.clock.hold(self.beside)
        self.clock.tick(self.beside)
        self.parts = (self.piece, self.beside, self.core_piece, swap(self.beside, 1))


class FetchHalves:
    def __init__(self, clock, words, piece, axis):
        self.clock, self.words, self.axis = clock, words, axis
        self.piece = swap(piece, 1, "mp")
        self.stages = [self.share, self.cross, self.join]

    def step(self):
        self.stages.pop(0)()

    def share(self):
        self.piece = self.clock.hold(self.piece)
        self.clock.tick(self.piece)
        self.near = [swap(self.piece, distance) for distance in (2, 4)]

    def cross(self):
        beside, above = self.near
        low_part, high_part = split_blocks(self.clock.hold(beside), above, 3 - self.axis)
        self.clock.tick(low_part, high_part)
        self.far = [swap(low_part, 4), swap(high_part, 2)]

    def join(self):
        beside, above = self.near
        mine = join_depth(
            self.words, self.clock.hold(self.piece), beside, above, *self.far, self.axis
        )
        self.clock.tick(mine)
        self.parts = (mine, swap(mine, 1))


class Clock:
    def __init__(self):
        self.tokens = ()

    def hold(self, value):
        return hold(value, *self.tokens)

    def tick(self, *values):
        self.tokens = values


def combine(words, sides, count, cut_by):
    terms = [term for side in sides for term in side]
    _, rows, columns = terms[0][0].shape
    ways = 2 if cut_by else 1
    size = rows // ways

    def kernel(word_ref, *refs):
        sources, targets = list(refs[: len(terms)]), list(refs[len(terms) :])
        leaving = [targets.pop(0) for _ in range(ways - 1)]
        place = (word_ref[0] // cut_by) % 2 if cut_by else 0
        for number, side in enumerate(sides):
            mine = [sources.pop(0) for _ in side]

            def total(relative):
                span = slice(None)
                if ways > 1:
                    span = pl.ds(pl.multiple_of((place ^ relative) * size, size), size)
                values = [ref[:, span, :].astype(F32) for ref in mine]
                return sum(values[1:], values[0]).astype(LOW)

            targets[number][...] = total(0)
            for relative, target in enumerate(leaving, 1):
                target[number * count : (number + 1) * count] = total(relative)

    def block(number):
        return pl.BlockSpec((count, rows, columns), lambda step: (number, 0, 0))

    shapes = [(count * len(sides), size, columns)] * (ways - 1) + [(count, size, columns)] * len(sides)
    return run(
        kernel,
        "combine",
        (1,),
        [scalar_spec()] + [block(number) for _, number in terms],
        [held(shape) for shape in shapes],
        [shaped(*shape, kind=LOW) for shape in shapes],
        (words, *[array for array, _ in terms]),
    )


def join_rows(words, entries, distance):
    ways = len(entries)
    count, size, columns = entries[0].shape
    shape = (count, ways * size, columns)

    def kernel(word_ref, *refs):
        target = refs[-1]
        place = (word_ref[0] // distance) % 2
        for relative, ref in enumerate(refs[:-1]):
            target[:, pl.ds(pl.multiple_of((place ^ relative) * size, size), size), :] = ref[...]

    return run(
        kernel,
        "join_rows",
        (1,),
        [scalar_spec()] + [held(entry.shape) for entry in entries],
        held(shape),
        shaped(*shape, kind=LOW),
        (words, *entries),
    )


class Piece:
    def __init__(self, clock, words, order, source, count):
        self.clock, self.words = clock, words
        self.order = list(order)
        self.back = [ways for ways in reversed(order) if ways != "x"]
        self.source = source
        self.count = count
        self.flight = None
        self.kept = None
        self.complete = False

    def add(self, sides):
        array, number = sides[0][0]
        sides[0][0] = (self.clock.hold(array), number)
        ways = self.order[0] if self.order else None
        sums = combine(self.words, sides, self.count, None if ways == "x" else ways)
        self.clock.tick(sums[0])
        if ways == "x":
            self.flight = [swap(sums[-1], 1, "mp")]
            self.kept = [[(entry, 0)] for entry in sums[:-1]]
        elif ways:
            self.flight = [swap(sums[0], ways)]
            self.kept = [[(entry, 0)] for entry in sums[1:]]
        else:
            self.total = sums[0]
            self.gather()

    def gather(self):
        self.flight = [swap(self.total, self.back[0] if self.back else 1)]

    def step(self):
        if self.flight is None:
            first = [(1,), (0, 1)][self.order[0] != "x"]
            self.add([self.source(side) for side in first])
            return
        if self.order:
            self.order.pop(0)
            sides = self.kept or [self.source(0)]
            for number, side in enumerate(sides):
                side += [(array, number) for array in self.flight]
            self.add(sides)
            return
        if not self.back:
            self.flight = [self.clock.hold(self.flight[0])]
            self.clock.tick(self.flight[0])
            self.complete = True
            return
        distance = self.back.pop(0)
        entries = [self.clock.hold(self.total)] + self.flight
        self.total = join_rows(self.words, entries, distance)
        self.clock.tick(self.total)
        self.gather()


def finish_units(core, ends):
    count, half, units = ends[0].shape
    entries = count // 2
    parts = len(ends) // 2

    def kernel(core_ref, *refs):
        down_ref, up_ref = refs[-2:]
        for part in range(parts):

            @pl.when(pl.program_id(0) // entries == part)
            def _():
                for ref, number in ((refs[2 * part], core_ref[0]), (refs[2 * part + 1], 1 - core_ref[0])):
                    span = pl.ds(pl.multiple_of(number * half, half), half)
                    down_ref[:, span] = ref[0].astype(F32)
                    up_ref[span, :] = ref[1].astype(F32)

    def block(part):
        return pl.BlockSpec(
            (2, half, units), lambda step: (jnp.clip(step - part * entries, 0, entries - 1), 0, 0)
        )

    total = entries * parts * units
    return run(
        kernel,
        "finish",
        (entries * parts,),
        [scalar_spec()] + [block(number // 2) for number in range(len(ends))],
        [
            pl.BlockSpec((half, 2 * half), lambda step: (step, 0)),
            pl.BlockSpec((2 * half, units), lambda step: (0, step)),
        ],
        [shaped(total, 2 * half), shaped(2 * half, total)],
        (core, *ends),
    )


def finish_heads(core, ends):
    _, half, group = ends[0].shape
    parts = len(ends) // 2

    def kernel(core_ref, *refs):
        qkv_ref, out_ref = refs[-2:]
        for part in range(parts):

            @pl.when(pl.program_id(0) == part)
            def _():
                for ref, number in ((refs[2 * part], core_ref[0]), (refs[2 * part + 1], 1 - core_ref[0])):
                    span = pl.ds(pl.multiple_of(number * half, half), half)
                    for member in range(3):
                        qkv_ref[member, span, :] = ref[member].astype(F32)
                    for member in range(half // group):
                        start = pl.multiple_of(number * half + member * group, group)
                        rows = slice(member * group, (member + 1) * group)
                        out_ref[:, pl.ds(start, group)] = ref[3, rows, :].astype(F32)

    return run(
        kernel,
        "finish",
        (parts,),
        [scalar_spec()] + [held(entry.shape) for entry in ends],
        [
            pl.BlockSpec((3, 2 * half, group), lambda step: (0, 0, step)),
            pl.BlockSpec((group, 2 * half), lambda step: (step, 0)),
        ],
        [shaped(3, 2 * half, parts * group), shaped(parts * group, 2 * half)],
        (core, *ends),
    )


MLP_ORDERS = (("x", 2, 4, 8), (2, "x", 4, 8))
HEAD_ORDERS = ((2, "x", 4, 8), (2, "x", 4, 8))
FORWARD = (
    ("own", 0),
    "a",
    ("own", 1),
    "b",
    "a",
    "out",
    "up",
    ("other", 0),
    "b",
    "out",
    "down",
    ("other", 1),
    "up",
    "project",
    "down",
    "up",
    "units",
    "down",
)
BACKWARD = (
    ("ub", 0),
    ("ub", 1),
    ("m", 0),
    ("fb",),
    ("m", 1),
    ("hb", 0),
    ("hb", 1),
    ("m", 0),
    ("m", 1),
    ("h", 0),
    ("h", 1),
    ("m", 0),
    ("m", 1),
    ("m", 0),
    ("h", 0),
    ("m", 1),
    ("m", 0),
    ("h", 1),
    ("h", 0),
    ("m", 1),
    ("m", 0),
    ("h", 1),
    ("h", 0),
    ("m", 1),
    ("m", 0),
    ("h", 1),
    ("h", 0),
    ("m", 1),
    ("h", 1),
    ("m", 0),
    ("h", 0),
    ("h", 1),
    ("m", 0),
    ("h", 0),
    ("m", 1),
    ("h", 1),
    ("m", 1),
    ("h", 0),
    ("h", 1),
    ("h", 0),
    ("h", 1),
)


def whole_page_body(
    inputs,
    qkv_weight,
    qv_bias,
    out_weight,
    out_bias,
    norm_gain,
    norm_shift,
    up_weight,
    up_bias,
    down_weight,
    down_bias,
    cotangent,
):
    place = lax.axis_index("dp")
    core, beside, above = (bit_of(place, distance) for distance in (1, 2, 4))
    words = jnp.stack([place, core * 2 + beside, core * 4 + beside * 2 + above, core])
    words = words.astype(jnp.int32)
    core_word, quarter_word = words[3:4], words[1:2]
    nothing = jnp.zeros((1,), jnp.int32)
    quarter_order = {"own": nothing, "other": quarter_word}
    half_order = {"own": nothing, "other": core_word}
    width = qv_bias.shape[2]
    parts = width // GROUP
    rows, depth = inputs.shape
    units_here = up_bias.shape[1]
    clock = Clock()

    def qkv_block(part):
        return (qkv_weight, (1, 3, QUARTER, GROUP), lambda word: (0, 0, word[1], part))

    pieces_now = take_blocks(words, [qkv_block(0), qkv_block(1)])
    clock.tick(pieces_now[0])
    fetch = {name: FetchQuarters(clock, piece) for name, piece in zip("ab", pieces_now)}
    pieces_now = take_blocks(
        words,
        [
            (clock.hold(out_weight), (1, width, QUARTER), lambda word: (0, 0, word[1])),
            (up_weight, (1, depth // 8, units_here), lambda word: (0, word[2], 0)),
            (down_weight, (1, units_here, depth // 8), lambda word: (0, 0, word[2])),
        ],
    )
    clock.tick(pieces_now[0])
    fetch["out"] = FetchQuarters(clock, pieces_now[0])
    fetch["up"] = FetchHalves(clock, words, pieces_now[1], 1)
    fetch["down"] = FetchHalves(clock, words, pieces_now[2], 2)
    biases = jnp.concatenate([qv_bias[0].reshape(-1), up_bias[0]])
    biases = {"own": biases, "other": swap(biases, 1, "mp")}
    gains, shifts = norm_gain[0], norm_shift[0]
    saved = {"own": (), "other": ()}
    qkv_w = {("own", part): (qkv_weight,) for part in range(parts)}
    up_w, down_w, out_w = {"own": (up_weight,)}, {"own": (down_weight,)}, {"own": (out_weight,)}
    units = {}

    def run_heads(side, part):
        values = biases[side] if side == "own" else clock.hold(biases[side])
        span = slice(part * GROUP, (part + 1) * GROUP)
        bias = jnp.concatenate(
            [values[:width][span], jnp.zeros((GROUP,), F32), values[width : 2 * width][span]]
        )
        if side == "other":
            qkv_w[side, part] = fetch["ab"[part]].parts
        saved[side] = heads_forward(
            quarter_order[side],
            qkv_w[side, part],
            clock.hold(inputs),
            bias[None],
            part,
            parts,
            saved[side],
        )
        clock.tick(saved[side][1])

    def run_units(side):
        bias = up_bias if side == "own" else clock.hold(biases[side])[None, 2 * width :]
        units[side] = units_forward(
            half_order[side], clock.hold(hidden_low), up_w[side], bias, down_w[side]
        )
        clock.tick(units[side][2])

    for action in FORWARD:
        if action == "project":
            out_w["other"] = fetch["out"].parts
            pre_first, hidden, hidden_low = project(
                quarter_word,
                (saved["own"][1], saved["other"][1]),
                out_weight,
                out_w["other"],
                clock.hold(inputs),
                out_bias,
                gains[0:1],
                shifts[0:1],
            )
            clock.tick(hidden_low)
        elif action == "units":
            run_units("own")
        elif isinstance(action, tuple):
            run_heads(*action)
        else:
            fetch[action].step()
    up_w["other"], down_w["other"] = fetch["up"].parts, fetch["down"].parts
    run_units("other")
    layer_out, grad_second, second_low, gain_two, shift_two, down_sum = turn(
        (units["own"][2], units["other"][2]),
        hidden,
        cotangent,
        down_bias,
        gains[1:2],
        shifts[1:2],
    )
    clock.tick(second_low)
    keep, received, totals, up_sums, head_sums = {}, {}, [], {}, {}
    state = {}

    def run_units_back(part):
        kept, sent, total, up_sums[part] = units_back(
            core_word,
            core_word,
            clock.hold(second_low),
            hidden_low,
            units,
            up_w,
            down_w,
            part,
            2,
        )
        keep["m", part], received["m", part] = kept, swap(sent, 1)
        totals.append(total)
        clock.tick(total)

    def run_first_back():
        state["first"] = first_back(totals, clock.hold(grad_second), pre_first, gains[0:1])
        state["grad_x"] = state["first"][0]
        clock.tick(state["first"][1])

    def run_heads_back(part):
        kept, sent, grad_x, head_sums[part] = heads_back(
            core_word,
            quarter_word,
            saved,
            part,
            inputs,
            clock.hold(state["first"][1]),
            {side: qkv_w[side, part] for side in ("own", "other")},
            out_w,
            state["grad_x"],
        )
        keep["h", part], received["h", part] = kept, swap(sent, 1)
        state["grad_x"] = grad_x
        clock.tick(grad_x)

    pieces = {}
    outcome = {}

    def run_piece(kind, number):
        key = (kind, number)
        if key not in pieces:
            orders = MLP_ORDERS if kind == "m" else HEAD_ORDERS

            def source(side):
                return [(keep[key], side), (received[key], side)]

            pieces[key] = Piece(clock, words, orders[number], source, 4)
        pieces[key].step()
        both = [pieces.get((kind, other)) for other in range(2)]
        if kind not in outcome and all(piece and piece.complete for piece in both):
            ends = [array for piece in both for array in (piece.total, piece.flight[0])]
            ends[0] = clock.hold(ends[0])
            outcome[kind] = finish_units(core_word, ends) if kind == "m" else finish_heads(core_word, ends)
            clock.tick(outcome[kind][0])

    for action in BACKWARD:
        name, *rest = action
        if name == "ub":
            run_units_back(*rest)
        elif name == "fb":
            run_first_back()
        elif name == "hb":
            run_heads_back(*rest)
        else:
            run_piece(*action)
    for kind in "mh":
        while kind not in outcome:
            for number in range(2):
                if not pieces[kind, number].complete:
                    run_piece(kind, number)
    grad_x = state["grad_x"]
    gain_one, shift_one, out_sum = state["first"][2:]
    grad_down, grad_up = outcome["m"]
    grad_qkv, grad_out_w = outcome["h"]

    def small_of(side):
        sums = [head_sums[part][side, 0] for part in range(parts)]
        entries = [entry[:GROUP] for entry in sums] + [entry[2 * GROUP :] for entry in sums]
        for part in range(2):
            steps = up_sums[part].shape[0] // 2
            entries.append(up_sums[part][side * steps : (side + 1) * steps].reshape(-1))
        return jnp.concatenate(entries)

    shared_small = jnp.concatenate(
        [entry[0] for entry in (out_sum, gain_one, gain_two, shift_one, shift_two, down_sum)]
    )
    own_small, other_small = small_of(0), small_of(1)
    split_width = own_small.shape[0]
    every = lax.all_gather(
        jnp.concatenate([own_small, other_small, shared_small]), ("dp", "mp"), axis=0
    ).reshape(lax.axis_size("dp"), 2, -1)
    same = jnp.sum(every, axis=0)
    column = lax.axis_index("mp")
    straight = same[0, :split_width] + same[1, split_width : 2 * split_width]
    turned = same[1, :split_width] + same[0, split_width : 2 * split_width]
    split_sum = jnp.where(column == 0, straight, turned)
    grad_qv_bias = split_sum[: 2 * width].reshape(1, 2, width)
    grad_up_bias = split_sum[2 * width :].reshape(1, -1)
    small = same[0] + same[1]
    split_width = 2 * split_width
    shared = small[split_width:].reshape(6, -1)
    return (
        layer_out,
        grad_x,
        grad_qkv[None],
        grad_qv_bias,
        grad_out_w[None],
        shared[0:1],
        shared[1:3][None],
        shared[3:5][None],
        grad_up[None],
        grad_up_bias,
        grad_down[None],
        shared[5:6],
    )


def body(inputs, *others):
    rows = inputs.shape[0]
    shared = lax.axis_size("mp") == 2 and lax.axis_size("dp") == 16
    if rows % PAGE == 0 and shared:
        return whole_page_body(inputs, *others)
    return spread_body(inputs, *others)


def solution(mesh):
    placed = (
        P(("dp", "mp"), None),
        P(None, None, None, "mp"),
        P(None, None, "mp"),
        P(None, "mp", None),
        P(),
        P(),
        P(),
        P(None, None, "mp"),
        P(None, "mp"),
        P(None, "mp", None),
        P(),
        P(("dp", "mp"), None),
    )
    return jax.shard_map(
        body,
        mesh=mesh,
        in_specs=placed,
        out_specs=(
            P(("dp", "mp"), None),
            P(("dp", "mp"), None),
            P(None, None, None, "mp"),
            P(None, None, "mp"),
            P(None, "mp", None),
            P(),
            P(),
            P(),
            P(None, None, "mp"),
            P(None, "mp"),
            P(None, "mp", None),
            P(),
        ),
        check_vma=False,
    )
```

```python
import jax
import jax.numpy as jnp
from jax import lax
from jax.experimental import pallas as pl
from jax.experimental.pallas import tpu as pltpu
from jax.sharding import PartitionSpec as P

HEAD = 64
PAGE = 416
LANES = 128

EPSILON = 1e-05
F32 = jnp.float32
LOW = jnp.bfloat16

def norm_rows(matrix, norm_scale, norm_offset):
    average = jnp.mean(matrix, axis=-1, keepdims=True)
    centered = matrix - average
    variance = jnp.mean(centered * centered, axis=-1, keepdims=True)
    return centered * lax.rsqrt(variance + EPSILON) * norm_scale + norm_offset


def exact_gelu(matrix):
    return jax.nn.gelu(matrix, approximate=False)


def spread_rows(rows_low, project):
    return project(lax.all_gather(rows_low, "mp", axis=0, tiled=True), jnp.int32(0))


def sum_rows(term, shard_rows):
    return lax.psum_scatter(
        term(jnp.int32(0), lax.axis_size("mp") * shard_rows), "mp", scatter_dimension=0, tiled=True
    )


def grad_fold(portion, acts, weight):
    weight_grad = lax.dot_general(
        acts, portion, (((0,), (0,)), ((), ())), preferred_element_type=jnp.float32
    )
    product = lax.dot_general(
        portion, weight, (((1,), (1,)), ((), ())), preferred_element_type=jnp.float32
    )
    return (product, weight_grad)


def spread_grads(grad_low, acts, weight):
    return grad_fold(lax.all_gather(grad_low, "mp", axis=0, tiled=True), acts=acts, weight=weight)


def sum_grads(term, shard_rows):
    return lax.psum_scatter(
        term(jnp.int32(0), lax.axis_size("mp") * shard_rows), "mp", scatter_dimension=0, tiled=True
    )


def page_forward(page_items):
    queries, key_rows, values = page_items
    scores = jnp.einsum("qhd,khd->hqk", queries, key_rows, preferred_element_type=jnp.float32)
    row_max = jnp.max(scores, axis=-1, keepdims=True)
    exponent = jnp.exp(scores - row_max)
    denominator = jnp.sum(exponent, axis=-1, keepdims=True)
    weights_low = (exponent / denominator).astype(jnp.bfloat16)
    log_total = row_max + jnp.log(denominator)
    attended = jnp.einsum("hqk,khd->qhd", weights_low, values, preferred_element_type=jnp.float32)
    return (attended.astype(jnp.bfloat16), log_total)


def page_backward(page_items):
    queries, key_rows, values, log_total, grad_mix = page_items
    scores = jnp.einsum("qhd,khd->hqk", queries, key_rows, preferred_element_type=jnp.float32)
    probability = jnp.exp(scores - log_total)
    weights_low = probability.astype(jnp.bfloat16)
    grad_prob = jnp.einsum("qhd,khd->hqk", grad_mix, values, preferred_element_type=jnp.float32)
    inner_total = jnp.sum(probability * grad_prob, axis=-1, keepdims=True)
    grad_scores = (probability * (grad_prob - inner_total)).astype(jnp.bfloat16)
    grad_q = jnp.einsum("hqk,khd->qhd", grad_scores, key_rows, preferred_element_type=jnp.float32)
    grad_k = jnp.einsum("hqk,qhd->khd", grad_scores, queries, preferred_element_type=jnp.float32)
    grad_v = jnp.einsum("hqk,qhd->khd", weights_low, grad_mix, preferred_element_type=jnp.float32)
    return (grad_q.astype(jnp.bfloat16), grad_k.astype(jnp.bfloat16), grad_v.astype(jnp.bfloat16))


def layer_forward(x_shard, params):
    qkv_w, qv_b, out_w, out_b, gains, shifts, up_w, up_b, down_w, down_b = params
    shard_rows = x_shard.shape[0]

    def project_qkv(portion, offset):
        return (
            jnp.einsum("rd,kde->rke", portion, qkv_w, preferred_element_type=jnp.float32),
            portion,
        )

    qkv_all, x_all = spread_rows(x_shard.astype(jnp.bfloat16), project_qkv)
    token_count = qkv_all.shape[0]
    local_width = qkv_all.shape[2]
    layout = (token_count // PAGE, PAGE, local_width // HEAD, HEAD)
    queries = ((qkv_all[:, 0] + qv_b[0]) * 0.125).astype(jnp.bfloat16).reshape(layout)
    key_rows = qkv_all[:, 1].astype(jnp.bfloat16).reshape(layout)
    values = (qkv_all[:, 2] + qv_b[1]).astype(jnp.bfloat16).reshape(layout)
    attended, log_total = lax.map(jax.checkpoint(page_forward), (queries, key_rows, values))
    attended = attended.reshape(token_count, local_width)

    def project_out(offset, amount):
        return jnp.dot(attended, out_w, preferred_element_type=jnp.float32)

    pre_first = x_shard + sum_rows(project_out, shard_rows) + out_b
    hidden = norm_rows(pre_first, gains[0], shifts[0])

    def project_up(portion, offset):
        return (jnp.dot(portion, up_w, preferred_element_type=jnp.float32), portion)

    pre_gelu, hidden_all = spread_rows(hidden.astype(jnp.bfloat16), project_up)
    pre_gelu = pre_gelu + up_b
    active = exact_gelu(pre_gelu).astype(jnp.bfloat16)

    def project_down(offset, amount):
        return jnp.dot(active, down_w, preferred_element_type=jnp.float32)

    pre_second = hidden + sum_rows(project_down, shard_rows) + down_b
    layer_out = norm_rows(pre_second, gains[1], shifts[1])
    stored = (
        x_shard,
        x_all,
        queries,
        key_rows,
        values,
        log_total,
        attended,
        pre_first,
        hidden_all,
        pre_gelu,
        active,
        pre_second,
        out_w,
    )
    return (layer_out, stored)


def layer_backward(grad_out, stored, params):
    qkv_w, qv_b, out_w, out_b, gains, shifts, up_w, up_b, down_w, down_b = params
    (
        x_shard,
        x_all,
        queries,
        key_rows,
        values,
        log_total,
        attended,
        pre_first,
        hidden_all,
        pre_gelu,
        active,
        pre_second,
        out_full,
    ) = stored
    shard_rows = grad_out.shape[0]
    norm_result, norm_back = jax.vjp(norm_rows, pre_second, gains[1], shifts[1])
    grad_second, gain_two, shift_two = norm_back(grad_out)
    grad_down_bias = jnp.sum(grad_second, axis=0)
    grad_active, grad_down = spread_grads(grad_second.astype(jnp.bfloat16), active, down_w)
    gelu_result, gelu_back = jax.vjp(exact_gelu, pre_gelu)
    grad_pre_low = gelu_back(grad_active)[0].astype(jnp.bfloat16)
    grad_up_bias = jnp.sum(grad_pre_low.astype(jnp.float32), axis=0)
    grad_up = lax.dot_general(
        hidden_all, grad_pre_low, (((0,), (0,)), ((), ())), preferred_element_type=jnp.float32
    )

    def back_up(offset, amount):
        return lax.dot_general(
            grad_pre_low, up_w, (((1,), (1,)), ((), ())), preferred_element_type=jnp.float32
        )

    grad_hidden = grad_second + sum_grads(back_up, shard_rows)
    norm_result, norm_back = jax.vjp(norm_rows, pre_first, gains[0], shifts[0])
    grad_first, gain_one, shift_one = norm_back(grad_hidden)
    grad_out_bias = jnp.sum(grad_first, axis=0)
    grad_first_low = grad_first.astype(jnp.bfloat16)
    grad_attended, grad_out_w = spread_grads(grad_first_low, attended, out_w)
    token_count = grad_attended.shape[0]
    local_width = grad_attended.shape[1]
    grad_mix = grad_attended.astype(jnp.bfloat16).reshape(queries.shape)
    grad_q, grad_k, grad_v = lax.map(
        jax.checkpoint(page_backward), (queries, key_rows, values, log_total, grad_mix)
    )
    flat_q = grad_q.reshape(token_count, local_width) * 0.125
    flat_k = grad_k.reshape(token_count, local_width)
    flat_v = grad_v.reshape(token_count, local_width)
    grad_qkv = jnp.stack([flat_q, flat_k, flat_v], axis=1)
    grad_qv_bias = jnp.stack(
        [jnp.sum(flat_q.astype(jnp.float32), axis=0), jnp.sum(flat_v.astype(jnp.float32), axis=0)]
    )
    grad_qkv_w = jnp.einsum("rd,rke->kde", x_all, grad_qkv, preferred_element_type=jnp.float32)

    def back_qkv(offset, amount):
        return jnp.einsum("rke,kde->rd", grad_qkv, qkv_w, preferred_element_type=jnp.float32)

    grad_x = grad_first + sum_grads(back_qkv, shard_rows)
    split_grads = (grad_qkv_w, grad_qv_bias, grad_out_w, grad_up, grad_up_bias, grad_down)
    shared_grads = (
        grad_out_bias,
        jnp.stack([gain_one, gain_two]),
        jnp.stack([shift_one, shift_two]),
        grad_down_bias,
    )
    return (grad_x, split_grads, shared_grads)


def spread_body(
    inputs,
    qkv_weight,
    qv_bias,
    out_weight,
    out_bias,
    norm_gain,
    norm_shift,
    up_weight,
    up_bias,
    down_weight,
    down_bias,
    cotangent,
):
    layer_total = qkv_weight.shape[0]

    def params_of(layer_number):
        return (
            qkv_weight[layer_number],
            qv_bias[layer_number],
            out_weight[layer_number],
            out_bias[layer_number],
            norm_gain[layer_number],
            norm_shift[layer_number],
            up_weight[layer_number],
            up_bias[layer_number],
            down_weight[layer_number],
            down_bias[layer_number],
        )

    current = inputs.astype(jnp.float32)
    layer_number = 0
    layer_in = current
    current, stored = layer_forward(current, params_of(layer_number))
    kept_list = [layer_in]
    grad_rows = cotangent.astype(jnp.float32)
    split_list = []
    shared_list = []
    for layer_number in reversed(range(layer_total)):
        stored = layer_forward(kept_list[layer_number], params_of(layer_number))[1]
        grad_rows, split_grads, shared_grads = layer_backward(
            grad_rows, stored, params_of(layer_number)
        )
        qkv_part, bias_part, out_part, up_part, upb_part, down_part = split_grads
        split_grads = lax.psum((qkv_part, bias_part, out_part, up_part, upb_part, down_part), "dp")
        outb_part, gain_part, shift_part, downb_part = shared_grads
        shared_grads = lax.psum((outb_part, gain_part, shift_part, downb_part), ("dp", "mp"))
        split_list.insert(0, split_grads)
        shared_list.insert(0, shared_grads)
    split_all = tuple((jnp.stack([entry[member] for entry in split_list]) for member in range(6)))
    shared_all = tuple((jnp.stack([entry[member] for entry in shared_list]) for member in range(4)))
    return (
        current,
        grad_rows,
        split_all[0],
        split_all[1],
        split_all[2],
        shared_all[0],
        shared_all[1],
        shared_all[2],
        split_all[3],
        split_all[4],
        split_all[5],
        shared_all[3],
    )


LARGE = 58 * 2**20
SPEED = 30 * 1.1e9
HEAVY = 1
UNITS = 512
GROUP = 256


def gelu_pair(u):
    below = 0.5 * lax.erf(u * 0.5**0.5) + 0.5
    return u * below, below + u * jnp.exp(u * u * -0.5) * 0.3989422804014327


def matmul(left, right, left_dim=1, right_dim=0):
    return lax.dot_general(
        left, right, (((left_dim,), (right_dim,)), ((), ())), preferred_element_type=F32
    )


def head_mask(which):
    lane = lax.broadcasted_iota(jnp.int32, (1, LANES), 1)
    return (lane // HEAD) == which


def shaped(*dims, kind=F32):
    return jax.ShapeDtypeStruct(dims, kind)


def held(dims):
    return pl.BlockSpec(dims, lambda *place: (0,) * len(dims), pipeline_mode=pl.Buffered(1))


def scalar_spec():
    return pl.BlockSpec(memory_space=pltpu.SMEM)


TIMES = {
    "heads": 8,
    "heads_back": 26,
    "units": 14,
    "units_back": 22,
    "project": 7,
    "turn": 9,
    "first_back": 10,
    "combine": 2,
    "join_rows": 2,
    "take_blocks": 3,
    "split_blocks": 2,
    "join_depth": 3,
    "finish": 6,
}


def cost_of(name):
    return pl.CostEstimate(
        flops=int((TIMES[name] if TIMES[name] < 5 else TIMES[name] * HEAVY) * SPEED), bytes_accessed=1, transcendentals=0
    )


def run(kernel, name, grid, in_specs, out_specs, out_shape, operands, scratch=()):
    return pl.pallas_call(
        kernel,
        grid=grid,
        in_specs=in_specs,
        out_specs=out_specs,
        out_shape=out_shape,
        scratch_shapes=list(scratch),
        compiler_params=pltpu.CompilerParams(vmem_limit_bytes=LARGE),
        cost_estimate=cost_of(name),
        name=name,
    )(*operands)


def spans(pair):
    return [
        slice(start * GROUP + pair * LANES, start * GROUP + (pair + 1) * LANES)
        for start in range(3)
    ]


def gather_depth(order_ref, refs, target, by_column):
    for relative, ref in enumerate(refs):
        span = pl.ds(pl.multiple_of((order_ref[0] ^ relative) * QUARTER, QUARTER), QUARTER)
        if by_column:
            target[:, span] = ref[0]
        else:
            for member in range(3):
                target[span, member * GROUP : (member + 1) * GROUP] = ref[0, member]


QUARTER = 256


def qkv_specs(quarters, part):
    shape = (1, 3, QUARTER, GROUP)
    if len(quarters) == 1:
        return [
            pl.BlockSpec(
                shape,
                lambda page, number=number: (0, 0, number, part),
                pipeline_mode=pl.Buffered(1),
            )
            for number in range(4)
        ]
    return [held(shape)] * 4


def four_times(quarters):
    return list(quarters) * (4 // len(quarters))


def heads_kernel(order_ref, w0_ref, w1_ref, w2_ref, w3_ref, x_ref, b_ref, *refs):
    three_ref, o_ref, lse_ref, weight = refs[-4:]

    @pl.when(pl.program_id(0) == 0)
    def _():
        gather_depth(order_ref, (w0_ref, w1_ref, w2_ref, w3_ref), weight, False)

    scaled = matmul(x_ref[...], weight[...]) + b_ref[...]
    three_ref[:, :GROUP] = (scaled[:, :GROUP] * 0.125).astype(LOW)
    three_ref[:, GROUP:] = scaled[:, GROUP:].astype(LOW)
    for pair in range(GROUP // LANES):
        queries, key_rows, values = (three_ref[:, entry] for entry in spans(pair))
        values_t = values.T
        columns = []
        for which in range(LANES // HEAD):
            head = pair * (LANES // HEAD) + which
            keys_one = jnp.where(head_mask(which), key_rows, jnp.zeros_like(key_rows))
            scores = matmul(keys_one, queries, 1, 1)
            peak = jnp.max(scores, axis=0, keepdims=True)
            exponent = jnp.exp(scores - peak)
            denominator = jnp.sum(exponent, axis=0, keepdims=True)
            weights_low = (exponent * (1.0 / denominator)).astype(LOW)
            columns.append(matmul(values_t[which * HEAD : (which + 1) * HEAD], weights_low))
            lse_ref[0, 0, head : head + 1, :] = peak + jnp.log(denominator)
        o_ref[:, pair * LANES : (pair + 1) * LANES] = (
            jnp.concatenate(columns, axis=0).T.astype(LOW)
        )


def heads_forward(order, quarters, x_low, bias, part, parts, before=()):
    rows, depth = x_low.shape
    width = 3 * GROUP
    pages = rows // PAGE
    count = GROUP // HEAD
    return pl.pallas_call(
        heads_kernel,
        grid=(pages,),
        in_specs=[scalar_spec()]
        + qkv_specs(quarters, part)
        + [pl.BlockSpec((PAGE, depth), lambda page: (page, 0)), held((1, width))]
        + [pl.BlockSpec(memory_space=pl.ANY)] * len(before),
        out_specs=[
            pl.BlockSpec((PAGE, width), lambda page: (page, part)),
            pl.BlockSpec((PAGE, GROUP), lambda page: (page, part)),
            pl.BlockSpec((1, 1, count, PAGE), lambda page: (part, page, 0, 0)),
        ],
        out_shape=[
            shaped(rows, parts * width, kind=LOW),
            shaped(rows, parts * GROUP, kind=LOW),
            shaped(parts, pages, count, PAGE),
        ],
        scratch_shapes=[pltpu.VMEM((depth, width), LOW)],
        input_output_aliases={7 + number: number for number in range(len(before))},
        compiler_params=pltpu.CompilerParams(vmem_limit_bytes=LARGE),
        cost_estimate=cost_of("heads"),
        name="heads",
    )(order, *four_times(quarters), x_low, bias, *before)


def heads_back_kernel(core_ref, order_ref, x_ref, g_ref, before_ref, *refs):
    keep_ref, send_ref, gx_ref, sum_ref = refs[22:26]
    qkv_total, out_total, weight, out_weight = refs[26:]
    side, page = pl.program_id(0), pl.program_id(1)
    pages = pl.num_programs(1)
    core = core_ref[0]
    half = x_ref.shape[1] // 2

    def work(order, first_side, three_ref, lse_ref, att_ref, *weights):
        @pl.when(page == 0)
        def _():
            gather_depth(order, weights[:4], weight, False)
            gather_depth(order, weights[4:], out_weight, True)

        mix = matmul(g_ref[...], out_weight[...], 1, 1).astype(LOW)
        grads_three = [None] * (3 * (GROUP // LANES))
        for pair in range(GROUP // LANES):
            queries, key_rows, values = (three_ref[:, entry] for entry in spans(pair))
            grads = mix[:, pair * LANES : (pair + 1) * LANES]
            keys_t = key_rows.T
            columns, dk_parts, dv_parts = [], [], []
            for which in range(LANES // HEAD):
                head = pair * (LANES // HEAD) + which
                mask = head_mask(which)
                keys_one = jnp.where(mask, key_rows, jnp.zeros_like(key_rows))
                scores = matmul(keys_one, queries, 1, 1)
                probability = jnp.exp(scores - lse_ref[0, 0, head : head + 1, :])
                values_one = jnp.where(mask, values, jnp.zeros_like(values))
                grad_prob = matmul(values_one, grads, 1, 1)
                inner = jnp.sum(probability * grad_prob, axis=0, keepdims=True)
                grad_scores = (probability * (grad_prob - inner)).astype(LOW)
                dv_parts.append(matmul(probability.astype(LOW), grads))
                dk_parts.append(matmul(grad_scores, queries))
                columns.append(matmul(keys_t[which * HEAD : (which + 1) * HEAD], grad_scores))
            first = head_mask(0)
            grad_q = jnp.concatenate(columns, axis=0).T.astype(LOW)
            grads_three[pair] = (grad_q.astype(F32) * 0.125).astype(LOW)
            grads_three[2 + pair] = jnp.where(first, dk_parts[0], dk_parts[1]).astype(LOW)
            grads_three[4 + pair] = jnp.where(first, dv_parts[0], dv_parts[1]).astype(LOW)
        three = jnp.concatenate(grads_three, axis=1)
        start = page == 0
        sums = jnp.sum(three.astype(F32), axis=0, keepdims=True)
        sum_ref[0] = jnp.where(start, 0.0, sum_ref[0]) + sums
        product = matmul(x_ref[...], three, 0, 0)
        qkv_total[...] = jnp.where(start, 0.0, qkv_total[...]) + product
        product = matmul(att_ref[...], g_ref[...], 0, 0)
        out_total[...] = jnp.where(start, 0.0, out_total[...]) + product
        rows = pl.ds(pl.multiple_of(page * PAGE, PAGE), PAGE)
        before = before_ref[...] if first_side else gx_ref[rows, :]
        gx_ref[rows, :] = before + matmul(three, weight[...], 1, 1)

    @pl.when(side == 0)
    def _():
        work((0,), True, *refs[:11])

    @pl.when(side == 1)
    def _():
        work(order_ref, False, *refs[11:22])

    @pl.when(page == pages - 1)
    def _():
        for ref, number in ((keep_ref, core), (send_ref, 1 - core)):
            start = pl.multiple_of(number * half, half)
            for member in range(3):
                span = slice(member * GROUP, (member + 1) * GROUP)
                ref[member] = qkv_total[pl.ds(start, half), span].astype(LOW)
            for member in range(2):
                column = pl.ds(pl.multiple_of(number * half + member * GROUP, GROUP), GROUP)
                ref[3, member * GROUP : (member + 1) * GROUP, :] = out_total[:, column].astype(LOW)


def heads_back(core, order, saved, part, x_low, grad_low, qkv, out, before):
    rows, depth = x_low.shape
    width = 3 * GROUP
    pages = rows // PAGE
    count = GROUP // HEAD
    half = depth // 2
    block = pl.BlockSpec((4, half, GROUP), lambda side, page: (side, 0, 0))
    line = pl.BlockSpec((PAGE, depth), lambda side, page: (page, 0))
    once = pl.BlockSpec(
        (PAGE, depth), lambda side, page: (jnp.where(side == 0, page, pages - 1), 0)
    )
    in_specs, operands = [], []
    for number, side in enumerate(("own", "other")):

        def page_of(side, page, number=number):
            return jnp.where(side == number, page, 0 if number else pages - 1)

        def beside(side, page, page_of=page_of):
            return (page_of(side, page), part)

        def above(side, page, page_of=page_of):
            return (part, page_of(side, page), 0, 0)

        in_specs += [
            pl.BlockSpec((PAGE, width), beside),
            pl.BlockSpec((1, 1, count, PAGE), above),
            pl.BlockSpec((PAGE, GROUP), beside),
        ]
        for quarter in range(4):
            fixed = (0, 0, quarter, part) if side == "own" else (0, 0, 0, 0)
            in_specs.append(
                pl.BlockSpec(
                    (1, 3, QUARTER, GROUP),
                    lambda side, page, fixed=fixed: fixed,
                    pipeline_mode=pl.Buffered(1),
                )
            )
        for quarter in range(4):
            fixed = (0, part, quarter if side == "own" else 0)
            in_specs.append(
                pl.BlockSpec(
                    (1, GROUP, QUARTER),
                    lambda side, page, fixed=fixed: fixed,
                    pipeline_mode=pl.Buffered(1),
                )
            )
        three, attended, lse = saved[side]
        operands += [three, lse, attended, *four_times(qkv[side]), *four_times(out[side])]
    return run(
        heads_back_kernel,
        "heads_back",
        (2, pages),
        [scalar_spec(), scalar_spec(), line, line, once] + in_specs,
        [
            block,
            block,
            held((rows, depth)),
            pl.BlockSpec((1, 1, width), lambda side, page: (side, 0, 0)),
        ],
        [
            shaped(8, half, GROUP, kind=LOW),
            shaped(8, half, GROUP, kind=LOW),
            shaped(rows, depth),
            shaped(2, 1, width),
        ],
        (core, order, x_low, grad_low, before, *operands),
        [
            pltpu.VMEM((depth, width), F32),
            pltpu.VMEM((GROUP, depth), F32),
            pltpu.VMEM((depth, width), LOW),
            pltpu.VMEM((GROUP, depth), LOW),
        ],
    )


ROW_STEPS = 1


def pair_specs(pair, shape, axis, first=0):
    def place(step, number):
        return (0, number, step + first) if axis == 1 else (0, step + first, number)

    if len(pair) == 1:
        return [
            pl.BlockSpec((1,) + shape, lambda step, number=number: place(step, number))
            for number in range(2)
        ]
    return [pl.BlockSpec((1,) + shape, lambda step: place(step, 0)) for _ in range(2)]


def twice(pair):
    return list(pair) * (2 // len(pair))


def depth_spans(order_ref, half):
    return [
        pl.ds(pl.multiple_of((order_ref[0] ^ relative) * half, half), half)
        for relative in range(2)
    ]


def units_kernel(order_ref, h_ref, up_a, up_b, b_ref, down_a, down_b, *outs):
    active_ref, slope_ref, total_ref = outs
    rows = h_ref.shape[0] // ROW_STEPS
    first, second = depth_spans(order_ref, h_ref.shape[1] // 2)
    for part in range(ROW_STEPS):
        span = slice(part * rows, (part + 1) * rows)
        pre = matmul(h_ref[span, first], up_a[0]) + matmul(h_ref[span, second], up_b[0])
        value, slope = gelu_pair(pre + b_ref[...])
        value = value.astype(LOW)
        active_ref[span, :] = value
        slope_ref[span, :] = slope.astype(LOW)
        for place, weight in ((first, down_a), (second, down_b)):
            before = jnp.where(pl.program_id(0) == 0, 0.0, total_ref[span, place])
            total_ref[span, place] = before + matmul(value, weight[0])


def units_forward(order, hidden_low, up, bias, down):
    rows, depth = hidden_low.shape
    units = bias.shape[1]
    half = depth // 2
    column = pl.BlockSpec((rows, UNITS), lambda step: (0, step))
    return run(
        units_kernel,
        "units",
        (units // UNITS,),
        [scalar_spec(), held((rows, depth))]
        + pair_specs(up, (half, UNITS), 1)
        + [pl.BlockSpec((1, UNITS), lambda step: (0, step))]
        + pair_specs(down, (UNITS, half), 2),
        [column, column, held((rows, depth))],
        [shaped(rows, units, kind=LOW), shaped(rows, units, kind=LOW), shaped(rows, depth)],
        (order, hidden_low, *twice(up), bias, *twice(down)),
    )


def units_back_kernel(core_ref, order_ref, g_ref, h_ref, *refs):
    keep_ref, send_ref, total_ref, sum_ref = refs[-4:]
    core = core_ref[0]
    half = g_ref.shape[1] // 2
    step = pl.program_id(0)
    steps = pl.num_programs(0) // 2

    def work(order, active_ref, slope_ref, up_a, up_b, down_a, down_b):
        first, second = depth_spans(order, half)
        grad = matmul(g_ref[:, first], down_a[0], 1, 1)
        grad = grad + matmul(g_ref[:, second], down_b[0], 1, 1)
        grad_low = (grad * slope_ref[...].astype(F32)).astype(LOW)
        sum_ref[0] = jnp.sum(grad_low.astype(F32), axis=0, keepdims=True)
        for place, weight in ((first, up_a), (second, up_b)):
            before = jnp.where(step == 0, 0.0, total_ref[:, place])
            total_ref[:, place] = before + matmul(grad_low, weight[0], 1, 1)
        for ref, number in ((keep_ref, core), (send_ref, 1 - core)):
            span = pl.ds(pl.multiple_of(number * half, half), half)
            ref[0] = matmul(active_ref[...], g_ref[:, span], 0, 0).astype(LOW)
            ref[1] = matmul(h_ref[:, span], grad_low, 0, 0).astype(LOW)

    @pl.when(step < steps)
    def _():
        work((0,), *refs[:6])

    @pl.when(step >= steps)
    def _():
        work(order_ref, *refs[6:12])


def units_back(core, order, grad_low, hidden_low, units, up, down, part, parts):
    rows, depth = hidden_low.shape
    here = units["own"][0].shape[1] // parts
    half = depth // 2
    steps = here // UNITS
    first = part * steps
    in_specs, operands = [], []
    for side, least in (("own", 0), ("other", steps)):

        def number(step, least=least):
            return first + jnp.clip(step - least, 0, steps - 1)

        column = pl.BlockSpec((rows, UNITS), lambda step, number=number: (0, number(step)))
        in_specs += [column, column]
        for axis, pair, shape in ((1, up, (half, UNITS)), (2, down, (UNITS, half))):
            for which in range(2):
                fixed = which if side == "own" else 0

                def place(step, axis=axis, fixed=fixed, number=number):
                    moving = number(step)
                    return (0, fixed, moving) if axis == 1 else (0, moving, fixed)

                in_specs.append(pl.BlockSpec((1,) + shape, place))
        operands += [*units[side][:2], *twice(up[side]), *twice(down[side])]
    block = pl.BlockSpec((2, half, UNITS), lambda step: (step, 0, 0))
    return run(
        units_back_kernel,
        "units_back",
        (2 * steps,),
        [scalar_spec(), scalar_spec(), held((rows, depth)), held((rows, depth))] + in_specs,
        [
            block,
            block,
            held((rows, depth)),
            pl.BlockSpec((1, 1, UNITS), lambda step: (step, 0, 0)),
        ],
        [
            shaped(4 * steps, half, UNITS, kind=LOW),
            shaped(4 * steps, half, UNITS, kind=LOW),
            shaped(rows, depth),
            shaped(2 * steps, 1, UNITS),
        ],
        (core, order, grad_low, hidden_low, *operands),
    )


def normal_rows(matrix):
    average = jnp.mean(matrix, axis=-1, keepdims=True)
    centered = matrix - average
    variance = jnp.mean(centered * centered, axis=-1, keepdims=True)
    scale = lax.rsqrt(variance + EPSILON)
    return centered * scale, scale


def normal_back(normal, scale, gain, grad):
    scaled = gain * grad
    level = jnp.mean(scaled, axis=-1, keepdims=True)
    along = jnp.mean(scaled * normal, axis=-1, keepdims=True)
    return scale * (scaled - level - normal * along)


def add_rows(ref, matrix):
    total = jnp.sum(matrix, axis=0, keepdims=True)
    before = jnp.where(pl.program_id(0) == 0, 0.0, ref[...])
    ref[...] = before + total


STRIP = 208


def strip(columns):
    return pl.BlockSpec((STRIP, columns), lambda step: (step, 0))


def project_kernel(order_ref, a_ref, b_ref, wa_ref, w0, w1, w2, w3, x_ref, *refs):
    bias_ref, g_ref, s_ref, first_ref, hidden_ref, low_ref = refs
    first_ref[...] = x_ref[...].astype(F32) + bias_ref[...] + matmul(a_ref[...], wa_ref[0])
    for relative, weight in enumerate((w0, w1, w2, w3)):
        span = pl.ds(pl.multiple_of((order_ref[0] ^ relative) * QUARTER, QUARTER), QUARTER)
        first_ref[:, span] += matmul(b_ref[...], weight[0])
    hidden = normal_rows(first_ref[...])[0] * g_ref[...] + s_ref[...]
    hidden_ref[...] = hidden
    low_ref[...] = hidden.astype(LOW)


def project(order, sides, own, quarters, x_low, bias, gain, shift):
    rows, depth = x_low.shape
    line = held((1, depth))
    page = pl.BlockSpec((PAGE, depth), lambda step: (step, 0))
    side = pl.BlockSpec((PAGE, sides[0].shape[1]), lambda step: (step, 0))
    return run(
        project_kernel,
        "project",
        (rows // PAGE,),
        [scalar_spec(), side, side, held(own.shape)]
        + [held(entry.shape) for entry in quarters]
        + [page, line, line, line],
        [page] * 3,
        [shaped(rows, depth), shaped(rows, depth), shaped(rows, depth, kind=LOW)],
        (order, *sides, own, *quarters, x_low, bias, gain, shift),
    )


def turn_kernel(a_ref, b_ref, h_ref, c_ref, bias_ref, g_ref, s_ref, *outs):
    out_ref, grad_ref, low_ref, gain_ref, shift_ref, sum_ref = outs
    normal, scale = normal_rows(h_ref[...] + (a_ref[...] + b_ref[...]) + bias_ref[...])
    out_ref[...] = normal * g_ref[...] + s_ref[...]
    grad_out = c_ref[...].astype(F32)
    grad = normal_back(normal, scale, g_ref[...], grad_out)
    grad_ref[...] = grad
    low_ref[...] = grad.astype(LOW)
    add_rows(gain_ref, grad_out * normal)
    add_rows(shift_ref, grad_out)
    add_rows(sum_ref, grad)


def turn(sides, hidden, cotangent, bias, gain, shift):
    rows, depth = hidden.shape
    line = pl.BlockSpec((1, depth), lambda step: (0, 0))
    return run(
        turn_kernel,
        "turn",
        (rows // STRIP,),
        [strip(depth)] * 4 + [line] * 3,
        [strip(depth)] * 3 + [line] * 3,
        [shaped(rows, depth), shaped(rows, depth), shaped(rows, depth, kind=LOW)]
        + [shaped(1, depth)] * 3,
        (*sides, hidden, cotangent, bias, gain, shift),
    )


def first_back_kernel(*refs):
    *sides, second_ref, first_ref, g_ref = refs[:-5]
    grad_ref, low_ref, gain_ref, shift_ref, sum_ref = refs[-5:]
    total = second_ref[...]
    for side in sides:
        total = total + side[...]
    normal, scale = normal_rows(first_ref[...])
    grad = normal_back(normal, scale, g_ref[...], total)
    grad_ref[...] = grad
    low_ref[...] = grad.astype(LOW)
    add_rows(gain_ref, total * normal)
    add_rows(shift_ref, total)
    add_rows(sum_ref, grad)


def first_back(sides, grad_second, pre_first, gain):
    rows, depth = pre_first.shape
    line = pl.BlockSpec((1, depth), lambda step: (0, 0))
    return run(
        first_back_kernel,
        "first_back",
        (rows // STRIP,),
        [strip(depth)] * (len(sides) + 2) + [line],
        [strip(depth)] * 2 + [line] * 3,
        [shaped(rows, depth), shaped(rows, depth, kind=LOW)] + [shaped(1, depth)] * 3,
        (*sides, grad_second, pre_first, gain),
    )


def swap(value, distance, axis="dp"):
    count = lax.axis_size(axis)
    return lax.ppermute(value, axis, [(place, place ^ distance) for place in range(count)])


def bit_of(place, distance):
    return jnp.minimum(jnp.bitwise_and(place, distance), 1).astype(jnp.int32)


def cut(value, number, count, axis):
    size = value.shape[axis] // count
    return lax.dynamic_slice_in_dim(value, number * size, size, axis)


def ordered(bit, mine, theirs, axis):
    return jnp.where(
        bit == 0,
        jnp.concatenate([mine, theirs], axis),
        jnp.concatenate([theirs, mine], axis),
    )


def hold(value, *tokens):
    return lax.optimization_barrier((value,) + tokens)[0] if tokens else value


def take_blocks(words, sources):
    count = len(sources)

    def kernel(word_ref, *refs):
        for source, target in zip(refs[:count], refs[count:]):
            target[...] = source[...]

    return pl.pallas_call(
        kernel,
        grid_spec=pltpu.PrefetchScalarGridSpec(
            num_scalar_prefetch=1,
            grid=(1,),
            in_specs=[
                pl.BlockSpec(shape, lambda step, word, index=index: index(word))
                for _, shape, index in sources
            ],
            out_specs=[
                pl.BlockSpec(shape, lambda step, word, shape=shape: (0,) * len(shape))
                for _, shape, _ in sources
            ],
        ),
        out_shape=[shaped(*shape, kind=LOW) for _, shape, _ in sources],
        compiler_params=pltpu.CompilerParams(vmem_limit_bytes=LARGE),
        cost_estimate=cost_of("take_blocks"),
        name="take_blocks",
    )(words, *[array for array, _, _ in sources])


def split_blocks(first, second, axis):
    half = first.shape[axis] // 2
    shape = first.shape[:axis] + (half,) + first.shape[axis + 1 :]

    def kernel(first_ref, second_ref, low_ref, high_ref):
        if axis == 2:
            low_ref[...] = first_ref[:, :, :half]
            high_ref[...] = second_ref[:, :, half:]
        else:
            low_ref[...] = first_ref[:, :half]
            high_ref[...] = second_ref[:, half:]

    return run(
        kernel,
        "split_blocks",
        (1,),
        [held(first.shape), held(second.shape)],
        [held(shape), held(shape)],
        [shaped(*shape, kind=first.dtype)] * 2,
        (first, second),
    )


def join_depth(words, piece, beside, above, low_part, high_part, axis):
    size = piece.shape[axis]
    shape = piece.shape[:axis] + (4 * size,) + piece.shape[axis + 1 :]
    half = low_part.shape[3 - axis]

    def kernel(word_ref, piece_ref, beside_ref, above_ref, low_ref, high_ref, target):
        place = word_ref[2] % 4

        def span(number):
            return pl.ds(pl.multiple_of(number * size, size), size)

        for ref, number in ((piece_ref, place), (beside_ref, place ^ 2), (above_ref, place ^ 1)):
            if axis == 1:
                target[:, span(number)] = ref[...]
            else:
                target[:, :, span(number)] = ref[...]
        last = span(place ^ 3)
        if axis == 1:
            target[:, last, :half] = low_ref[...]
            target[:, last, half:] = high_ref[...]
        else:
            target[:, :half, last] = low_ref[...]
            target[:, half:, last] = high_ref[...]

    entries = [piece, beside, above, low_part, high_part]
    return run(
        kernel,
        "join_depth",
        (1,),
        [scalar_spec()] + [held(entry.shape) for entry in entries],
        held(shape),
        shaped(*shape, kind=piece.dtype),
        (words, *entries),
    )


class FetchQuarters:
    def __init__(self, clock, piece):
        self.clock = clock
        self.piece = swap(piece, 1, "mp")
        self.stages = [self.share, self.last]

    def step(self):
        self.stages.pop(0)()

    def share(self):
        self.piece = self.clock.hold(self.piece)
        self.clock.tick(self.piece)
        self.beside = swap(self.piece, 2)
        self.core_piece = swap(self.piece, 1)

    def last(self):
        self.beside = self.clock.hold(self.beside)
        self.clock.tick(self.beside)
        self.parts = (self.piece, self.beside, self.core_piece, swap(self.beside, 1))


class FetchHalves:
    def __init__(self, clock, words, piece, axis):
        self.clock, self.words, self.axis = clock, words, axis
        self.piece = swap(piece, 1, "mp")
        self.stages = [self.share, self.cross, self.join]

    def step(self):
        self.stages.pop(0)()

    def share(self):
        self.piece = self.clock.hold(self.piece)
        self.clock.tick(self.piece)
        self.near = [swap(self.piece, distance) for distance in (2, 4)]

    def cross(self):
        beside, above = self.near
        low_part, high_part = split_blocks(self.clock.hold(beside), above, 3 - self.axis)
        self.clock.tick(low_part, high_part)
        self.far = [swap(low_part, 4), swap(high_part, 2)]

    def join(self):
        beside, above = self.near
        mine = join_depth(
            self.words, self.clock.hold(self.piece), beside, above, *self.far, self.axis
        )
        self.clock.tick(mine)
        self.parts = (mine, swap(mine, 1))


class Clock:
    def __init__(self):
        self.tokens = ()

    def hold(self, value):
        return hold(value, *self.tokens)

    def tick(self, *values):
        self.tokens = values


def combine(words, sides, count, cut_by):
    terms = [term for side in sides for term in side]
    _, rows, columns = terms[0][0].shape
    ways = 2 if cut_by else 1
    size = rows // ways

    def kernel(word_ref, *refs):
        sources, targets = list(refs[: len(terms)]), list(refs[len(terms) :])
        leaving = [targets.pop(0) for _ in range(ways - 1)]
        place = (word_ref[0] // cut_by) % 2 if cut_by else 0
        for number, side in enumerate(sides):
            mine = [sources.pop(0) for _ in side]

            def total(relative):
                span = slice(None)
                if ways > 1:
                    span = pl.ds(pl.multiple_of((place ^ relative) * size, size), size)
                values = [ref[:, span, :].astype(F32) for ref in mine]
                return sum(values[1:], values[0]).astype(LOW)

            targets[number][...] = total(0)
            for relative, target in enumerate(leaving, 1):
                target[number * count : (number + 1) * count] = total(relative)

    def block(number):
        return pl.BlockSpec((count, rows, columns), lambda step: (number, 0, 0))

    shapes = [(count * len(sides), size, columns)] * (ways - 1) + [(count, size, columns)] * len(sides)
    return run(
        kernel,
        "combine",
        (1,),
        [scalar_spec()] + [block(number) for _, number in terms],
        [held(shape) for shape in shapes],
        [shaped(*shape, kind=LOW) for shape in shapes],
        (words, *[array for array, _ in terms]),
    )


def join_rows(words, entries, distance):
    ways = len(entries)
    count, size, columns = entries[0].shape
    shape = (count, ways * size, columns)

    def kernel(word_ref, *refs):
        target = refs[-1]
        place = (word_ref[0] // distance) % 2
        for relative, ref in enumerate(refs[:-1]):
            target[:, pl.ds(pl.multiple_of((place ^ relative) * size, size), size), :] = ref[...]

    return run(
        kernel,
        "join_rows",
        (1,),
        [scalar_spec()] + [held(entry.shape) for entry in entries],
        held(shape),
        shaped(*shape, kind=LOW),
        (words, *entries),
    )


class Piece:
    def __init__(self, clock, words, order, source, count):
        self.clock, self.words = clock, words
        self.order = list(order)
        self.back = [ways for ways in reversed(order) if ways != "x"]
        self.source = source
        self.count = count
        self.flight = None
        self.kept = None
        self.complete = False

    def add(self, sides):
        array, number = sides[0][0]
        sides[0][0] = (self.clock.hold(array), number)
        ways = self.order[0] if self.order else None
        sums = combine(self.words, sides, self.count, None if ways == "x" else ways)
        self.clock.tick(sums[0])
        if ways == "x":
            self.flight = [swap(sums[-1], 1, "mp")]
            self.kept = [[(entry, 0)] for entry in sums[:-1]]
        elif ways:
            self.flight = [swap(sums[0], ways)]
            self.kept = [[(entry, 0)] for entry in sums[1:]]
        else:
            self.total = sums[0]
            self.gather()

    def gather(self):
        self.flight = [swap(self.total, self.back[0] if self.back else 1)]

    def step(self):
        if self.flight is None:
            first = [(1,), (0, 1)][self.order[0] != "x"]
            self.add([self.source(side) for side in first])
            return
        if self.order:
            self.order.pop(0)
            sides = self.kept or [self.source(0)]
            for number, side in enumerate(sides):
                side += [(array, number) for array in self.flight]
            self.add(sides)
            return
        if not self.back:
            self.flight = [self.clock.hold(self.flight[0])]
            self.clock.tick(self.flight[0])
            self.complete = True
            return
        distance = self.back.pop(0)
        entries = [self.clock.hold(self.total)] + self.flight
        self.total = join_rows(self.words, entries, distance)
        self.clock.tick(self.total)
        self.gather()


def finish_units(core, ends):
    count, half, units = ends[0].shape
    entries = count // 2
    parts = len(ends) // 2

    def kernel(core_ref, *refs):
        down_ref, up_ref = refs[-2:]
        for part in range(parts):

            @pl.when(pl.program_id(0) // entries == part)
            def _():
                for ref, number in ((refs[2 * part], core_ref[0]), (refs[2 * part + 1], 1 - core_ref[0])):
                    span = pl.ds(pl.multiple_of(number * half, half), half)
                    down_ref[:, span] = ref[0].astype(F32)
                    up_ref[span, :] = ref[1].astype(F32)

    def block(part):
        return pl.BlockSpec(
            (2, half, units), lambda step: (jnp.clip(step - part * entries, 0, entries - 1), 0, 0)
        )

    total = entries * parts * units
    return run(
        kernel,
        "finish",
        (entries * parts,),
        [scalar_spec()] + [block(number // 2) for number in range(len(ends))],
        [
            pl.BlockSpec((half, 2 * half), lambda step: (step, 0)),
            pl.BlockSpec((2 * half, units), lambda step: (0, step)),
        ],
        [shaped(total, 2 * half), shaped(2 * half, total)],
        (core, *ends),
    )


def finish_heads(core, ends):
    _, half, group = ends[0].shape
    parts = len(ends) // 2

    def kernel(core_ref, *refs):
        qkv_ref, out_ref = refs[-2:]
        for part in range(parts):

            @pl.when(pl.program_id(0) == part)
            def _():
                for ref, number in ((refs[2 * part], core_ref[0]), (refs[2 * part + 1], 1 - core_ref[0])):
                    span = pl.ds(pl.multiple_of(number * half, half), half)
                    for member in range(3):
                        qkv_ref[member, span, :] = ref[member].astype(F32)
                    for member in range(half // group):
                        start = pl.multiple_of(number * half + member * group, group)
                        rows = slice(member * group, (member + 1) * group)
                        out_ref[:, pl.ds(start, group)] = ref[3, rows, :].astype(F32)

    return run(
        kernel,
        "finish",
        (parts,),
        [scalar_spec()] + [held(entry.shape) for entry in ends],
        [
            pl.BlockSpec((3, 2 * half, group), lambda step: (0, 0, step)),
            pl.BlockSpec((group, 2 * half), lambda step: (step, 0)),
        ],
        [shaped(3, 2 * half, parts * group), shaped(parts * group, 2 * half)],
        (core, *ends),
    )


MLP_ORDERS = ((4, 8, 2, "x"), ("x", 2, 4, 8))
HEAD_ORDERS = ((4, "x", 2, 8), (4, 2, "x", 8))
FORWARD = (
    ("own", 0),
    "a",
    ("own", 1),
    "b",
    "a",
    "out",
    "up",
    ("other", 0),
    "b",
    "out",
    "down",
    ("other", 1),
    "up",
    "project",
    "down",
    "up",
    "units",
    "down",
)
BACKWARD = (
    ("ub", 0),
    ("ub", 1),
    ("m", 0),
    ("m", 1),
    ("fb",),
    ("hb", 0),
    ("m", 0),
    ("h", 0),
    ("m", 1),
    ("hb", 1),
    ("m", 1),
    ("h", 0),
    ("m", 0),
    ("h", 1),
    ("m", 1),
    ("h", 0),
    ("m", 0),
    ("h", 0),
    ("m", 1),
    ("m", 0),
    ("h", 1),
    ("h", 0),
    ("m", 0),
    ("m", 1),
    ("h", 0),
    ("h", 1),
    ("h", 0),
    ("m", 1),
    ("h", 1),
    ("m", 0),
    ("h", 0),
    ("small",),
    ("h", 1),
    ("h", 0),
    ("m", 1),
    ("h", 1),
    ("m", 0),
    ("m", 1),
    ("h", 1),
    ("m", 0),
    ("h", 1),
    ("h", 1),
)


def whole_page_body(
    inputs,
    qkv_weight,
    qv_bias,
    out_weight,
    out_bias,
    norm_gain,
    norm_shift,
    up_weight,
    up_bias,
    down_weight,
    down_bias,
    cotangent,
):
    place = lax.axis_index("dp")
    core, beside, above = (bit_of(place, distance) for distance in (1, 2, 4))
    words = jnp.stack([place, core * 2 + beside, core * 4 + beside * 2 + above, core])
    words = words.astype(jnp.int32)
    core_word, quarter_word = words[3:4], words[1:2]
    nothing = jnp.zeros((1,), jnp.int32)
    quarter_order = {"own": nothing, "other": quarter_word}
    half_order = {"own": nothing, "other": core_word}
    width = qv_bias.shape[2]
    parts = width // GROUP
    rows, depth = inputs.shape
    units_here = up_bias.shape[1]
    clock = Clock()

    def qkv_block(part):
        return (qkv_weight, (1, 3, QUARTER, GROUP), lambda word: (0, 0, word[1], part))

    pieces_now = take_blocks(words, [qkv_block(0), qkv_block(1)])
    clock.tick(pieces_now[0])
    fetch = {name: FetchQuarters(clock, piece) for name, piece in zip("ab", pieces_now)}
    pieces_now = take_blocks(
        words,
        [
            (clock.hold(out_weight), (1, width, QUARTER), lambda word: (0, 0, word[1])),
            (up_weight, (1, depth // 8, units_here), lambda word: (0, word[2], 0)),
            (down_weight, (1, units_here, depth // 8), lambda word: (0, 0, word[2])),
        ],
    )
    clock.tick(pieces_now[0])
    fetch["out"] = FetchQuarters(clock, pieces_now[0])
    fetch["up"] = FetchHalves(clock, words, pieces_now[1], 1)
    fetch["down"] = FetchHalves(clock, words, pieces_now[2], 2)
    biases = jnp.concatenate([qv_bias[0].reshape(-1), up_bias[0]])
    biases = {"own": biases, "other": swap(biases, 1, "mp")}
    gains, shifts = norm_gain[0], norm_shift[0]
    saved = {"own": (), "other": ()}
    qkv_w = {("own", part): (qkv_weight,) for part in range(parts)}
    up_w, down_w, out_w = {"own": (up_weight,)}, {"own": (down_weight,)}, {"own": (out_weight,)}
    units = {}

    def run_heads(side, part):
        values = biases[side] if side == "own" else clock.hold(biases[side])
        span = slice(part * GROUP, (part + 1) * GROUP)
        bias = jnp.concatenate(
            [values[:width][span], jnp.zeros((GROUP,), F32), values[width : 2 * width][span]]
        )
        if side == "other":
            qkv_w[side, part] = fetch["ab"[part]].parts
        saved[side] = heads_forward(
            quarter_order[side],
            qkv_w[side, part],
            clock.hold(inputs),
            bias[None],
            part,
            parts,
            saved[side],
        )
        clock.tick(saved[side][1])

    def run_units(side):
        bias = up_bias if side == "own" else clock.hold(biases[side])[None, 2 * width :]
        units[side] = units_forward(
            half_order[side], clock.hold(hidden_low), up_w[side], bias, down_w[side]
        )
        clock.tick(units[side][2])

    for action in FORWARD:
        if action == "project":
            out_w["other"] = fetch["out"].parts
            pre_first, hidden, hidden_low = project(
                quarter_word,
                (saved["own"][1], saved["other"][1]),
                out_weight,
                out_w["other"],
                clock.hold(inputs),
                out_bias,
                gains[0:1],
                shifts[0:1],
            )
            clock.tick(hidden_low)
        elif action == "units":
            run_units("own")
        elif isinstance(action, tuple):
            run_heads(*action)
        else:
            fetch[action].step()
    up_w["other"], down_w["other"] = fetch["up"].parts, fetch["down"].parts
    run_units("other")
    layer_out, grad_second, second_low, gain_two, shift_two, down_sum = turn(
        (units["own"][2], units["other"][2]),
        hidden,
        cotangent,
        down_bias,
        gains[1:2],
        shifts[1:2],
    )
    clock.tick(second_low)
    keep, received, totals, up_sums, head_sums = {}, {}, [], {}, {}
    state = {}

    def run_units_back(part):
        kept, sent, total, up_sums[part] = units_back(
            core_word,
            core_word,
            clock.hold(second_low),
            hidden_low,
            units,
            up_w,
            down_w,
            part,
            2,
        )
        keep["m", part], received["m", part] = kept, swap(sent, 1)
        totals.append(total)
        clock.tick(total)

    def run_first_back():
        state["first"] = first_back(totals, clock.hold(grad_second), pre_first, gains[0:1])
        state["grad_x"] = state["first"][0]
        clock.tick(state["first"][1])

    def run_heads_back(part):
        kept, sent, grad_x, head_sums[part] = heads_back(
            core_word,
            quarter_word,
            saved,
            part,
            inputs,
            clock.hold(state["first"][1]),
            {side: qkv_w[side, part] for side in ("own", "other")},
            out_w,
            state["grad_x"],
        )
        keep["h", part], received["h", part] = kept, swap(sent, 1)
        state["grad_x"] = grad_x
        clock.tick(grad_x)

    def gather_small():
        def small_of(side):
            sums = [head_sums[part][side, 0] for part in range(parts)]
            entries = [entry[:GROUP] for entry in sums] + [entry[2 * GROUP :] for entry in sums]
            for part in range(2):
                steps = up_sums[part].shape[0] // 2
                entries.append(up_sums[part][side * steps : (side + 1) * steps].reshape(-1))
            return jnp.concatenate(entries)

        gain_one, shift_one, out_sum = state["first"][2:]
        sums = (out_sum, gain_one, gain_two, shift_one, shift_two, down_sum)
        split = [small_of(0), small_of(1)]
        every = lax.all_gather(
            jnp.concatenate(split + [entry[0] for entry in sums]), ("dp", "mp"), axis=0
        )
        state["every"], state["split"] = every, split[0].shape[0]

    def add_small():
        every = clock.hold(state["every"]).reshape(lax.axis_size("dp"), 2, -1)
        split_width = state["split"]
        same = jnp.sum(every, axis=0)
        straight = same[0, :split_width] + same[1, split_width : 2 * split_width]
        turned = same[1, :split_width] + same[0, split_width : 2 * split_width]
        split_sum = jnp.where(lax.axis_index("mp") == 0, straight, turned)
        shared = (same[0] + same[1])[2 * split_width :].reshape(6, -1)
        clock.tick(split_sum, shared)
        state["small"] = (
            split_sum[: 2 * width].reshape(1, 2, width),
            split_sum[2 * width :].reshape(1, -1),
            shared,
        )

    pieces = {}
    outcome = {}

    def run_piece(kind, number):
        key = (kind, number)
        if key not in pieces:
            orders = MLP_ORDERS if kind == "m" else HEAD_ORDERS

            def source(side):
                return [(keep[key], side), (received[key], side)]

            pieces[key] = Piece(clock, words, orders[number], source, 4)
        pieces[key].step()
        both = [pieces.get((kind, other)) for other in range(2)]
        if kind not in outcome and all(piece and piece.complete for piece in both):
            ends = [array for piece in both for array in (piece.total, piece.flight[0])]
            ends[0] = clock.hold(ends[0])
            outcome[kind] = finish_units(core_word, ends) if kind == "m" else finish_heads(core_word, ends)
            clock.tick(outcome[kind][0])

    for action in BACKWARD:
        name, *rest = action
        if name == "ub":
            run_units_back(*rest)
        elif name == "fb":
            run_first_back()
        elif name == "hb":
            run_heads_back(*rest)
            if rest[0] == parts - 1:
                gather_small()
        elif name == "small":
            add_small()
        else:
            run_piece(*action)
    for kind in "mh":
        while kind not in outcome:
            for number in range(2):
                if not pieces[kind, number].complete:
                    run_piece(kind, number)
    grad_x = state["grad_x"]
    grad_down, grad_up = outcome["m"]
    grad_qkv, grad_out_w = outcome["h"]

    grad_qv_bias, grad_up_bias, shared = state["small"]
    return (
        layer_out,
        grad_x,
        grad_qkv[None],
        grad_qv_bias,
        grad_out_w[None],
        shared[0:1],
        shared[1:3][None],
        shared[3:5][None],
        grad_up[None],
        grad_up_bias,
        grad_down[None],
        shared[5:6],
    )


def body(inputs, *others):
    rows = inputs.shape[0]
    shared = lax.axis_size("mp") == 2 and lax.axis_size("dp") == 16
    if rows % PAGE == 0 and shared:
        return whole_page_body(inputs, *others)
    return spread_body(inputs, *others)


def solution(mesh):
    placed = (
        P(("dp", "mp"), None),
        P(None, None, None, "mp"),
        P(None, None, "mp"),
        P(None, "mp", None),
        P(),
        P(),
        P(),
        P(None, None, "mp"),
        P(None, "mp"),
        P(None, "mp", None),
        P(),
        P(("dp", "mp"), None),
    )
    return jax.shard_map(
        body,
        mesh=mesh,
        in_specs=placed,
        out_specs=(
            P(("dp", "mp"), None),
            P(("dp", "mp"), None),
            P(None, None, None, "mp"),
            P(None, None, "mp"),
            P(None, "mp", None),
            P(),
            P(),
            P(),
            P(None, None, "mp"),
            P(None, "mp"),
            P(None, "mp", None),
            P(),
        ),
        check_vma=False,
    )
```

```python
import jax
import jax.numpy as jnp
from jax import lax
from jax.experimental import pallas as pl
from jax.experimental.pallas import tpu as pltpu
from jax.sharding import PartitionSpec as P

HEAD = 64
PAGE = 416
LANES = 128

EPSILON = 1e-05
F32 = jnp.float32
LOW = jnp.bfloat16

def norm_rows(matrix, norm_scale, norm_offset):
    average = jnp.mean(matrix, axis=-1, keepdims=True)
    centered = matrix - average
    variance = jnp.mean(centered * centered, axis=-1, keepdims=True)
    return centered * lax.rsqrt(variance + EPSILON) * norm_scale + norm_offset


def exact_gelu(matrix):
    return jax.nn.gelu(matrix, approximate=False)


def spread_rows(rows_low, project):
    return project(lax.all_gather(rows_low, "mp", axis=0, tiled=True), jnp.int32(0))


def sum_rows(term, shard_rows):
    return lax.psum_scatter(
        term(jnp.int32(0), lax.axis_size("mp") * shard_rows), "mp", scatter_dimension=0, tiled=True
    )


def grad_fold(portion, acts, weight):
    weight_grad = lax.dot_general(
        acts, portion, (((0,), (0,)), ((), ())), preferred_element_type=jnp.float32
    )
    product = lax.dot_general(
        portion, weight, (((1,), (1,)), ((), ())), preferred_element_type=jnp.float32
    )
    return (product, weight_grad)


def spread_grads(grad_low, acts, weight):
    return grad_fold(lax.all_gather(grad_low, "mp", axis=0, tiled=True), acts=acts, weight=weight)


def sum_grads(term, shard_rows):
    return lax.psum_scatter(
        term(jnp.int32(0), lax.axis_size("mp") * shard_rows), "mp", scatter_dimension=0, tiled=True
    )


def page_forward(page_items):
    queries, key_rows, values = page_items
    scores = jnp.einsum("qhd,khd->hqk", queries, key_rows, preferred_element_type=jnp.float32)
    row_max = jnp.max(scores, axis=-1, keepdims=True)
    exponent = jnp.exp(scores - row_max)
    denominator = jnp.sum(exponent, axis=-1, keepdims=True)
    weights_low = (exponent / denominator).astype(jnp.bfloat16)
    log_total = row_max + jnp.log(denominator)
    attended = jnp.einsum("hqk,khd->qhd", weights_low, values, preferred_element_type=jnp.float32)
    return (attended.astype(jnp.bfloat16), log_total)


def page_backward(page_items):
    queries, key_rows, values, log_total, grad_mix = page_items
    scores = jnp.einsum("qhd,khd->hqk", queries, key_rows, preferred_element_type=jnp.float32)
    probability = jnp.exp(scores - log_total)
    weights_low = probability.astype(jnp.bfloat16)
    grad_prob = jnp.einsum("qhd,khd->hqk", grad_mix, values, preferred_element_type=jnp.float32)
    inner_total = jnp.sum(probability * grad_prob, axis=-1, keepdims=True)
    grad_scores = (probability * (grad_prob - inner_total)).astype(jnp.bfloat16)
    grad_q = jnp.einsum("hqk,khd->qhd", grad_scores, key_rows, preferred_element_type=jnp.float32)
    grad_k = jnp.einsum("hqk,qhd->khd", grad_scores, queries, preferred_element_type=jnp.float32)
    grad_v = jnp.einsum("hqk,qhd->khd", weights_low, grad_mix, preferred_element_type=jnp.float32)
    return (grad_q.astype(jnp.bfloat16), grad_k.astype(jnp.bfloat16), grad_v.astype(jnp.bfloat16))


def layer_forward(x_shard, params):
    qkv_w, qv_b, out_w, out_b, gains, shifts, up_w, up_b, down_w, down_b = params
    shard_rows = x_shard.shape[0]

    def project_qkv(portion, offset):
        return (
            jnp.einsum("rd,kde->rke", portion, qkv_w, preferred_element_type=jnp.float32),
            portion,
        )

    qkv_all, x_all = spread_rows(x_shard.astype(jnp.bfloat16), project_qkv)
    token_count = qkv_all.shape[0]
    local_width = qkv_all.shape[2]
    layout = (token_count // PAGE, PAGE, local_width // HEAD, HEAD)
    queries = ((qkv_all[:, 0] + qv_b[0]) * 0.125).astype(jnp.bfloat16).reshape(layout)
    key_rows = qkv_all[:, 1].astype(jnp.bfloat16).reshape(layout)
    values = (qkv_all[:, 2] + qv_b[1]).astype(jnp.bfloat16).reshape(layout)
    attended, log_total = lax.map(jax.checkpoint(page_forward), (queries, key_rows, values))
    attended = attended.reshape(token_count, local_width)

    def project_out(offset, amount):
        return jnp.dot(attended, out_w, preferred_element_type=jnp.float32)

    pre_first = x_shard + sum_rows(project_out, shard_rows) + out_b
    hidden = norm_rows(pre_first, gains[0], shifts[0])

    def project_up(portion, offset):
        return (jnp.dot(portion, up_w, preferred_element_type=jnp.float32), portion)

    pre_gelu, hidden_all = spread_rows(hidden.astype(jnp.bfloat16), project_up)
    pre_gelu = pre_gelu + up_b
    active = exact_gelu(pre_gelu).astype(jnp.bfloat16)

    def project_down(offset, amount):
        return jnp.dot(active, down_w, preferred_element_type=jnp.float32)

    pre_second = hidden + sum_rows(project_down, shard_rows) + down_b
    layer_out = norm_rows(pre_second, gains[1], shifts[1])
    stored = (
        x_shard,
        x_all,
        queries,
        key_rows,
        values,
        log_total,
        attended,
        pre_first,
        hidden_all,
        pre_gelu,
        active,
        pre_second,
        out_w,
    )
    return (layer_out, stored)


def layer_backward(grad_out, stored, params):
    qkv_w, qv_b, out_w, out_b, gains, shifts, up_w, up_b, down_w, down_b = params
    (
        x_shard,
        x_all,
        queries,
        key_rows,
        values,
        log_total,
        attended,
        pre_first,
        hidden_all,
        pre_gelu,
        active,
        pre_second,
        out_full,
    ) = stored
    shard_rows = grad_out.shape[0]
    norm_result, norm_back = jax.vjp(norm_rows, pre_second, gains[1], shifts[1])
    grad_second, gain_two, shift_two = norm_back(grad_out)
    grad_down_bias = jnp.sum(grad_second, axis=0)
    grad_active, grad_down = spread_grads(grad_second.astype(jnp.bfloat16), active, down_w)
    gelu_result, gelu_back = jax.vjp(exact_gelu, pre_gelu)
    grad_pre_low = gelu_back(grad_active)[0].astype(jnp.bfloat16)
    grad_up_bias = jnp.sum(grad_pre_low.astype(jnp.float32), axis=0)
    grad_up = lax.dot_general(
        hidden_all, grad_pre_low, (((0,), (0,)), ((), ())), preferred_element_type=jnp.float32
    )

    def back_up(offset, amount):
        return lax.dot_general(
            grad_pre_low, up_w, (((1,), (1,)), ((), ())), preferred_element_type=jnp.float32
        )

    grad_hidden = grad_second + sum_grads(back_up, shard_rows)
    norm_result, norm_back = jax.vjp(norm_rows, pre_first, gains[0], shifts[0])
    grad_first, gain_one, shift_one = norm_back(grad_hidden)
    grad_out_bias = jnp.sum(grad_first, axis=0)
    grad_first_low = grad_first.astype(jnp.bfloat16)
    grad_attended, grad_out_w = spread_grads(grad_first_low, attended, out_w)
    token_count = grad_attended.shape[0]
    local_width = grad_attended.shape[1]
    grad_mix = grad_attended.astype(jnp.bfloat16).reshape(queries.shape)
    grad_q, grad_k, grad_v = lax.map(
        jax.checkpoint(page_backward), (queries, key_rows, values, log_total, grad_mix)
    )
    flat_q = grad_q.reshape(token_count, local_width) * 0.125
    flat_k = grad_k.reshape(token_count, local_width)
    flat_v = grad_v.reshape(token_count, local_width)
    grad_qkv = jnp.stack([flat_q, flat_k, flat_v], axis=1)
    grad_qv_bias = jnp.stack(
        [jnp.sum(flat_q.astype(jnp.float32), axis=0), jnp.sum(flat_v.astype(jnp.float32), axis=0)]
    )
    grad_qkv_w = jnp.einsum("rd,rke->kde", x_all, grad_qkv, preferred_element_type=jnp.float32)

    def back_qkv(offset, amount):
        return jnp.einsum("rke,kde->rd", grad_qkv, qkv_w, preferred_element_type=jnp.float32)

    grad_x = grad_first + sum_grads(back_qkv, shard_rows)
    split_grads = (grad_qkv_w, grad_qv_bias, grad_out_w, grad_up, grad_up_bias, grad_down)
    shared_grads = (
        grad_out_bias,
        jnp.stack([gain_one, gain_two]),
        jnp.stack([shift_one, shift_two]),
        grad_down_bias,
    )
    return (grad_x, split_grads, shared_grads)


def spread_body(
    inputs,
    qkv_weight,
    qv_bias,
    out_weight,
    out_bias,
    norm_gain,
    norm_shift,
    up_weight,
    up_bias,
    down_weight,
    down_bias,
    cotangent,
):
    layer_total = qkv_weight.shape[0]

    def params_of(layer_number):
        return (
            qkv_weight[layer_number],
            qv_bias[layer_number],
            out_weight[layer_number],
            out_bias[layer_number],
            norm_gain[layer_number],
            norm_shift[layer_number],
            up_weight[layer_number],
            up_bias[layer_number],
            down_weight[layer_number],
            down_bias[layer_number],
        )

    current = inputs.astype(jnp.float32)
    layer_number = 0
    layer_in = current
    current, stored = layer_forward(current, params_of(layer_number))
    kept_list = [layer_in]
    grad_rows = cotangent.astype(jnp.float32)
    split_list = []
    shared_list = []
    for layer_number in reversed(range(layer_total)):
        stored = layer_forward(kept_list[layer_number], params_of(layer_number))[1]
        grad_rows, split_grads, shared_grads = layer_backward(
            grad_rows, stored, params_of(layer_number)
        )
        qkv_part, bias_part, out_part, up_part, upb_part, down_part = split_grads
        split_grads = lax.psum((qkv_part, bias_part, out_part, up_part, upb_part, down_part), "dp")
        outb_part, gain_part, shift_part, downb_part = shared_grads
        shared_grads = lax.psum((outb_part, gain_part, shift_part, downb_part), ("dp", "mp"))
        split_list.insert(0, split_grads)
        shared_list.insert(0, shared_grads)
    split_all = tuple((jnp.stack([entry[member] for entry in split_list]) for member in range(6)))
    shared_all = tuple((jnp.stack([entry[member] for entry in shared_list]) for member in range(4)))
    return (
        current,
        grad_rows,
        split_all[0],
        split_all[1],
        split_all[2],
        shared_all[0],
        shared_all[1],
        shared_all[2],
        split_all[3],
        split_all[4],
        split_all[5],
        shared_all[3],
    )


LARGE = 58 * 2**20
SPEED = 400 * 1.1e9
HEAVY = 1
UNITS = 512
GROUP = 256


def gelu_pair(u):
    below = 0.5 * lax.erf(u * 0.5**0.5) + 0.5
    return u * below, below + u * jnp.exp(u * u * -0.5) * 0.3989422804014327


def matmul(left, right, left_dim=1, right_dim=0):
    return lax.dot_general(
        left, right, (((left_dim,), (right_dim,)), ((), ())), preferred_element_type=F32
    )


def head_mask(which):
    lane = lax.broadcasted_iota(jnp.int32, (1, LANES), 1)
    return (lane // HEAD) == which


def shaped(*dims, kind=F32):
    return jax.ShapeDtypeStruct(dims, kind)


def held(dims):
    return pl.BlockSpec(dims, lambda *place: (0,) * len(dims), pipeline_mode=pl.Buffered(1))


def scalar_spec():
    return pl.BlockSpec(memory_space=pltpu.SMEM)


TIMES = {
    "heads": 8,
    "heads_back": 26,
    "units": 14,
    "units_back": 22,
    "project": 7,
    "turn": 9,
    "first_back": 10,
    "combine": 2,
    "join_rows": 2,
    "take_blocks": 3,
    "split_blocks": 2,
    "join_depth": 3,
    "finish": 6,
}


def cost_of(name):
    return pl.CostEstimate(
        flops=int((TIMES[name] if TIMES[name] < 5 else TIMES[name] * HEAVY) * SPEED), bytes_accessed=1, transcendentals=0
    )


def run(kernel, name, grid, in_specs, out_specs, out_shape, operands, scratch=()):
    return pl.pallas_call(
        kernel,
        grid=grid,
        in_specs=in_specs,
        out_specs=out_specs,
        out_shape=out_shape,
        scratch_shapes=list(scratch),
        compiler_params=pltpu.CompilerParams(vmem_limit_bytes=LARGE),
        cost_estimate=cost_of(name),
        name=name,
    )(*operands)


def spans(pair):
    return [
        slice(start * GROUP + pair * LANES, start * GROUP + (pair + 1) * LANES)
        for start in range(3)
    ]


def gather_depth(order_ref, refs, target, by_column):
    for relative, ref in enumerate(refs):
        span = pl.ds(pl.multiple_of((order_ref[0] ^ relative) * QUARTER, QUARTER), QUARTER)
        if by_column:
            target[:, span] = ref[0]
        else:
            for member in range(3):
                target[span, member * GROUP : (member + 1) * GROUP] = ref[0, member]


QUARTER = 256


def qkv_specs(quarters, part):
    shape = (1, 3, QUARTER, GROUP)
    if len(quarters) == 1:
        return [
            pl.BlockSpec(
                shape,
                lambda page, number=number: (0, 0, number, part),
                pipeline_mode=pl.Buffered(1),
            )
            for number in range(4)
        ]
    return [held(shape)] * 4


def four_times(quarters):
    return list(quarters) * (4 // len(quarters))


def heads_kernel(order_ref, w0_ref, w1_ref, w2_ref, w3_ref, x_ref, bq_ref, bv_ref, *refs):
    three_ref, o_ref, lse_ref, weight = refs[-4:]

    @pl.when(pl.program_id(0) == 0)
    def _():
        gather_depth(order_ref, (w0_ref, w1_ref, w2_ref, w3_ref), weight, False)

    product = matmul(x_ref[...], weight[...])
    three_ref[:, :GROUP] = ((product[:, :GROUP] + bq_ref[...]) * 0.125).astype(LOW)
    three_ref[:, GROUP : 2 * GROUP] = product[:, GROUP : 2 * GROUP].astype(LOW)
    three_ref[:, 2 * GROUP :] = (product[:, 2 * GROUP :] + bv_ref[...]).astype(LOW)
    for pair in range(GROUP // LANES):
        queries, key_rows, values = (three_ref[:, entry] for entry in spans(pair))
        values_t = values.T
        columns = []
        for which in range(LANES // HEAD):
            head = pair * (LANES // HEAD) + which
            keys_one = jnp.where(head_mask(which), key_rows, jnp.zeros_like(key_rows))
            scores = matmul(keys_one, queries, 1, 1)
            peak = jnp.max(scores, axis=0, keepdims=True)
            exponent = jnp.exp(scores - peak)
            denominator = jnp.sum(exponent, axis=0, keepdims=True)
            weights_low = (exponent * (1.0 / denominator)).astype(LOW)
            columns.append(matmul(values_t[which * HEAD : (which + 1) * HEAD], weights_low))
            lse_ref[0, 0, head : head + 1, :] = peak + jnp.log(denominator)
        o_ref[:, pair * LANES : (pair + 1) * LANES] = (
            jnp.concatenate(columns, axis=0).T.astype(LOW)
        )


def heads_forward(order, quarters, x_low, bias, part, parts, before=()):
    rows, depth = x_low.shape
    width = 3 * GROUP
    pages = rows // PAGE
    count = GROUP // HEAD
    return pl.pallas_call(
        heads_kernel,
        grid=(pages,),
        in_specs=[scalar_spec()]
        + qkv_specs(quarters, part)
        + [
            pl.BlockSpec((PAGE, depth), lambda page: (page, 0)),
            pl.BlockSpec((1, GROUP), lambda page: (0, part)),
            pl.BlockSpec((1, GROUP), lambda page: (0, parts + part)),
        ]
        + [pl.BlockSpec(memory_space=pl.ANY)] * len(before),
        out_specs=[
            pl.BlockSpec((PAGE, width), lambda page: (page, part)),
            pl.BlockSpec((PAGE, GROUP), lambda page: (page, part)),
            pl.BlockSpec((1, 1, count, PAGE), lambda page: (part, page, 0, 0)),
        ],
        out_shape=[
            shaped(rows, parts * width, kind=LOW),
            shaped(rows, parts * GROUP, kind=LOW),
            shaped(parts, pages, count, PAGE),
        ],
        scratch_shapes=[pltpu.VMEM((depth, width), LOW)],
        input_output_aliases={8 + number: number for number in range(len(before))},
        compiler_params=pltpu.CompilerParams(vmem_limit_bytes=LARGE),
        cost_estimate=cost_of("heads"),
        name="heads",
    )(order, *four_times(quarters), x_low, bias, bias, *before)


def heads_back_kernel(core_ref, order_ref, x_ref, g_ref, before_ref, *refs):
    keep_ref, send_ref, gx_ref, sum_ref = refs[22:26]
    qkv_total, out_total, weight, out_weight = refs[26:]
    side, page = pl.program_id(0), pl.program_id(1)
    pages = pl.num_programs(1)
    core = core_ref[0]
    half = x_ref.shape[1] // 2

    def work(order, first_side, three_ref, lse_ref, att_ref, *weights):
        @pl.when(page == 0)
        def _():
            gather_depth(order, weights[:4], weight, False)
            gather_depth(order, weights[4:], out_weight, True)

        mix = matmul(g_ref[...], out_weight[...], 1, 1).astype(LOW)
        grads_three = [None] * (3 * (GROUP // LANES))
        for pair in range(GROUP // LANES):
            queries, key_rows, values = (three_ref[:, entry] for entry in spans(pair))
            grads = mix[:, pair * LANES : (pair + 1) * LANES]
            keys_t = key_rows.T
            columns, dk_parts, dv_parts = [], [], []
            for which in range(LANES // HEAD):
                head = pair * (LANES // HEAD) + which
                mask = head_mask(which)
                keys_one = jnp.where(mask, key_rows, jnp.zeros_like(key_rows))
                scores = matmul(keys_one, queries, 1, 1)
                probability = jnp.exp(scores - lse_ref[0, 0, head : head + 1, :])
                values_one = jnp.where(mask, values, jnp.zeros_like(values))
                grad_prob = matmul(values_one, grads, 1, 1)
                inner = jnp.sum(probability * grad_prob, axis=0, keepdims=True)
                grad_scores = (probability * (grad_prob - inner)).astype(LOW)
                dv_parts.append(matmul(probability.astype(LOW), grads))
                dk_parts.append(matmul(grad_scores, queries))
                columns.append(matmul(keys_t[which * HEAD : (which + 1) * HEAD], grad_scores))
            first = head_mask(0)
            grad_q = jnp.concatenate(columns, axis=0).T.astype(LOW)
            grads_three[pair] = (grad_q.astype(F32) * 0.125).astype(LOW)
            grads_three[2 + pair] = jnp.where(first, dk_parts[0], dk_parts[1]).astype(LOW)
            grads_three[4 + pair] = jnp.where(first, dv_parts[0], dv_parts[1]).astype(LOW)
        three = jnp.concatenate(grads_three, axis=1)
        start = page == 0
        sums = jnp.sum(three.astype(F32), axis=0, keepdims=True)
        sum_ref[0] = jnp.where(start, 0.0, sum_ref[0]) + sums
        product = matmul(x_ref[...], three, 0, 0)
        qkv_total[...] = jnp.where(start, 0.0, qkv_total[...]) + product
        product = matmul(att_ref[...], g_ref[...], 0, 0)
        out_total[...] = jnp.where(start, 0.0, out_total[...]) + product
        rows = pl.ds(pl.multiple_of(page * PAGE, PAGE), PAGE)
        before = before_ref[...] if first_side else gx_ref[rows, :]
        gx_ref[rows, :] = before + matmul(three, weight[...], 1, 1)

    @pl.when(side == 0)
    def _():
        work((0,), True, *refs[:11])

    @pl.when(side == 1)
    def _():
        work(order_ref, False, *refs[11:22])

    @pl.when(page == pages - 1)
    def _():
        for ref, number in ((keep_ref, core), (send_ref, 1 - core)):
            start = pl.multiple_of(number * half, half)
            for member in range(3):
                span = slice(member * GROUP, (member + 1) * GROUP)
                ref[member] = qkv_total[pl.ds(start, half), span].astype(LOW)
            for member in range(2):
                column = pl.ds(pl.multiple_of(number * half + member * GROUP, GROUP), GROUP)
                ref[3, member * GROUP : (member + 1) * GROUP, :] = out_total[:, column].astype(LOW)


def heads_back(core, order, saved, part, x_low, grad_low, qkv, out, before):
    rows, depth = x_low.shape
    width = 3 * GROUP
    pages = rows // PAGE
    count = GROUP // HEAD
    half = depth // 2
    block = pl.BlockSpec((4, half, GROUP), lambda side, page: (side, 0, 0))
    line = pl.BlockSpec((PAGE, depth), lambda side, page: (page, 0))
    once = pl.BlockSpec(
        (PAGE, depth), lambda side, page: (jnp.where(side == 0, page, pages - 1), 0)
    )
    in_specs, operands = [], []
    for number, side in enumerate(("own", "other")):

        def page_of(side, page, number=number):
            return jnp.where(side == number, page, 0 if number else pages - 1)

        def beside(side, page, page_of=page_of):
            return (page_of(side, page), part)

        def above(side, page, page_of=page_of):
            return (part, page_of(side, page), 0, 0)

        in_specs += [
            pl.BlockSpec((PAGE, width), beside),
            pl.BlockSpec((1, 1, count, PAGE), above),
            pl.BlockSpec((PAGE, GROUP), beside),
        ]
        for quarter in range(4):
            fixed = (0, 0, quarter, part) if side == "own" else (0, 0, 0, 0)
            in_specs.append(
                pl.BlockSpec(
                    (1, 3, QUARTER, GROUP),
                    lambda side, page, fixed=fixed: fixed,
                    pipeline_mode=pl.Buffered(1),
                )
            )
        for quarter in range(4):
            fixed = (0, part, quarter if side == "own" else 0)
            in_specs.append(
                pl.BlockSpec(
                    (1, GROUP, QUARTER),
                    lambda side, page, fixed=fixed: fixed,
                    pipeline_mode=pl.Buffered(1),
                )
            )
        three, attended, lse = saved[side]
        operands += [three, lse, attended, *four_times(qkv[side]), *four_times(out[side])]
    return run(
        heads_back_kernel,
        "heads_back",
        (2, pages),
        [scalar_spec(), scalar_spec(), line, line, once] + in_specs,
        [
            block,
            block,
            held((rows, depth)),
            pl.BlockSpec((1, 1, width), lambda side, page: (side, 0, 0)),
        ],
        [
            shaped(8, half, GROUP, kind=LOW),
            shaped(8, half, GROUP, kind=LOW),
            shaped(rows, depth),
            shaped(2, 1, width),
        ],
        (core, order, x_low, grad_low, before, *operands),
        [
            pltpu.VMEM((depth, width), F32),
            pltpu.VMEM((GROUP, depth), F32),
            pltpu.VMEM((depth, width), LOW),
            pltpu.VMEM((GROUP, depth), LOW),
        ],
    )


ROW_STEPS = 1


def pair_specs(pair, shape, axis, first=0):
    def place(step, number):
        return (0, number, step + first) if axis == 1 else (0, step + first, number)

    if len(pair) == 1:
        return [
            pl.BlockSpec((1,) + shape, lambda step, number=number: place(step, number))
            for number in range(2)
        ]
    return [pl.BlockSpec((1,) + shape, lambda step: place(step, 0)) for _ in range(2)]


def twice(pair):
    return list(pair) * (2 // len(pair))


def depth_spans(order_ref, half):
    return [
        pl.ds(pl.multiple_of((order_ref[0] ^ relative) * half, half), half)
        for relative in range(2)
    ]


def units_kernel(order_ref, h_ref, up_a, up_b, b_ref, down_a, down_b, *outs):
    active_ref, slope_ref, total_ref = outs
    rows = h_ref.shape[0] // ROW_STEPS
    first, second = depth_spans(order_ref, h_ref.shape[1] // 2)
    for part in range(ROW_STEPS):
        span = slice(part * rows, (part + 1) * rows)
        pre = matmul(h_ref[span, first], up_a[0]) + matmul(h_ref[span, second], up_b[0])
        value, slope = gelu_pair(pre + b_ref[...])
        value = value.astype(LOW)
        active_ref[span, :] = value
        slope_ref[span, :] = slope.astype(LOW)
        for place, weight in ((first, down_a), (second, down_b)):
            before = jnp.where(pl.program_id(0) == 0, 0.0, total_ref[span, place])
            total_ref[span, place] = before + matmul(value, weight[0])


def units_forward(order, hidden_low, up, bias, down):
    rows, depth = hidden_low.shape
    units = down[0].shape[1]
    skip = (bias.shape[1] - units) // UNITS
    half = depth // 2
    column = pl.BlockSpec((rows, UNITS), lambda step: (0, step))
    return run(
        units_kernel,
        "units",
        (units // UNITS,),
        [scalar_spec(), held((rows, depth))]
        + pair_specs(up, (half, UNITS), 1)
        + [pl.BlockSpec((1, UNITS), lambda step: (0, step + skip))]
        + pair_specs(down, (UNITS, half), 2),
        [column, column, held((rows, depth))],
        [shaped(rows, units, kind=LOW), shaped(rows, units, kind=LOW), shaped(rows, depth)],
        (order, hidden_low, *twice(up), bias, *twice(down)),
    )


def units_back_kernel(core_ref, order_ref, g_ref, h_ref, *refs):
    keep_ref, send_ref, total_ref, sum_ref = refs[-4:]
    core = core_ref[0]
    half = g_ref.shape[1] // 2
    step = pl.program_id(0)
    steps = pl.num_programs(0) // 2

    def work(order, active_ref, slope_ref, up_a, up_b, down_a, down_b):
        first, second = depth_spans(order, half)
        grad = matmul(g_ref[:, first], down_a[0], 1, 1)
        grad = grad + matmul(g_ref[:, second], down_b[0], 1, 1)
        grad_low = (grad * slope_ref[...].astype(F32)).astype(LOW)
        sum_ref[0] = jnp.sum(grad_low.astype(F32), axis=0, keepdims=True)
        for place, weight in ((first, up_a), (second, up_b)):
            before = jnp.where(step == 0, 0.0, total_ref[:, place])
            total_ref[:, place] = before + matmul(grad_low, weight[0], 1, 1)
        for ref, number in ((keep_ref, core), (send_ref, 1 - core)):
            span = pl.ds(pl.multiple_of(number * half, half), half)
            ref[0] = matmul(active_ref[...], g_ref[:, span], 0, 0).astype(LOW)
            ref[1] = matmul(h_ref[:, span], grad_low, 0, 0).astype(LOW)

    @pl.when(step < steps)
    def _():
        work((0,), *refs[:6])

    @pl.when(step >= steps)
    def _():
        work(order_ref, *refs[6:12])


def units_back(core, order, grad_low, hidden_low, units, up, down, part, parts):
    rows, depth = hidden_low.shape
    here = units["own"][0].shape[1] // parts
    half = depth // 2
    steps = here // UNITS
    first = part * steps
    in_specs, operands = [], []
    for side, least in (("own", 0), ("other", steps)):

        def number(step, least=least):
            return first + jnp.clip(step - least, 0, steps - 1)

        column = pl.BlockSpec((rows, UNITS), lambda step, number=number: (0, number(step)))
        in_specs += [column, column]
        for axis, pair, shape in ((1, up, (half, UNITS)), (2, down, (UNITS, half))):
            for which in range(2):
                fixed = which if side == "own" else 0

                def place(step, axis=axis, fixed=fixed, number=number):
                    moving = number(step)
                    return (0, fixed, moving) if axis == 1 else (0, moving, fixed)

                in_specs.append(pl.BlockSpec((1,) + shape, place))
        operands += [*units[side][:2], *twice(up[side]), *twice(down[side])]
    block = pl.BlockSpec((2, half, UNITS), lambda step: (step, 0, 0))
    return run(
        units_back_kernel,
        "units_back",
        (2 * steps,),
        [scalar_spec(), scalar_spec(), held((rows, depth)), held((rows, depth))] + in_specs,
        [
            block,
            block,
            held((rows, depth)),
            pl.BlockSpec((1, 1, UNITS), lambda step: (step, 0, 0)),
        ],
        [
            shaped(4 * steps, half, UNITS, kind=LOW),
            shaped(4 * steps, half, UNITS, kind=LOW),
            shaped(rows, depth),
            shaped(2 * steps, 1, UNITS),
        ],
        (core, order, grad_low, hidden_low, *operands),
    )


def normal_rows(matrix):
    average = jnp.mean(matrix, axis=-1, keepdims=True)
    centered = matrix - average
    variance = jnp.mean(centered * centered, axis=-1, keepdims=True)
    scale = lax.rsqrt(variance + EPSILON)
    return centered * scale, scale


def normal_back(normal, scale, gain, grad):
    scaled = gain * grad
    level = jnp.mean(scaled, axis=-1, keepdims=True)
    along = jnp.mean(scaled * normal, axis=-1, keepdims=True)
    return scale * (scaled - level - normal * along)


def add_rows(ref, matrix):
    total = jnp.sum(matrix, axis=0, keepdims=True)
    before = jnp.where(pl.program_id(0) == 0, 0.0, ref[...])
    ref[...] = before + total


STRIP = 208


def strip(columns):
    return pl.BlockSpec((STRIP, columns), lambda step: (step, 0))


def project_kernel(order_ref, a_ref, b_ref, wa_ref, w0, w1, w2, w3, x_ref, *refs):
    bias_ref, g_ref, s_ref, first_ref, hidden_ref, low_ref = refs
    first_ref[...] = x_ref[...].astype(F32) + bias_ref[...] + matmul(a_ref[...], wa_ref[0])
    for relative, weight in enumerate((w0, w1, w2, w3)):
        span = pl.ds(pl.multiple_of((order_ref[0] ^ relative) * QUARTER, QUARTER), QUARTER)
        first_ref[:, span] += matmul(b_ref[...], weight[0])
    hidden = normal_rows(first_ref[...])[0] * g_ref[...] + s_ref[...]
    hidden_ref[...] = hidden
    low_ref[...] = hidden.astype(LOW)


def project(order, sides, own, quarters, x_low, bias, gain, shift):
    rows, depth = x_low.shape
    line = held((1, depth))
    page = pl.BlockSpec((PAGE, depth), lambda step: (step, 0))
    side = pl.BlockSpec((PAGE, sides[0].shape[1]), lambda step: (step, 0))
    return run(
        project_kernel,
        "project",
        (rows // PAGE,),
        [scalar_spec(), side, side, held(own.shape)]
        + [held(entry.shape) for entry in quarters]
        + [page, line, line, line],
        [page] * 3,
        [shaped(rows, depth), shaped(rows, depth), shaped(rows, depth, kind=LOW)],
        (order, *sides, own, *quarters, x_low, bias, gain, shift),
    )


def turn_kernel(a_ref, b_ref, h_ref, c_ref, bias_ref, g_ref, s_ref, *outs):
    out_ref, grad_ref, low_ref, gain_ref, shift_ref, sum_ref = outs
    normal, scale = normal_rows(h_ref[...] + (a_ref[...] + b_ref[...]) + bias_ref[...])
    out_ref[...] = normal * g_ref[...] + s_ref[...]
    grad_out = c_ref[...].astype(F32)
    grad = normal_back(normal, scale, g_ref[...], grad_out)
    grad_ref[...] = grad
    low_ref[...] = grad.astype(LOW)
    add_rows(gain_ref, grad_out * normal)
    add_rows(shift_ref, grad_out)
    add_rows(sum_ref, grad)


def turn(sides, hidden, cotangent, bias, gain, shift):
    rows, depth = hidden.shape
    line = pl.BlockSpec((1, depth), lambda step: (0, 0))
    return run(
        turn_kernel,
        "turn",
        (rows // STRIP,),
        [strip(depth)] * 4 + [line] * 3,
        [strip(depth)] * 3 + [line] * 3,
        [shaped(rows, depth), shaped(rows, depth), shaped(rows, depth, kind=LOW)]
        + [shaped(1, depth)] * 3,
        (*sides, hidden, cotangent, bias, gain, shift),
    )


def first_back_kernel(*refs):
    *sides, second_ref, first_ref, g_ref = refs[:-5]
    grad_ref, low_ref, gain_ref, shift_ref, sum_ref = refs[-5:]
    total = second_ref[...]
    for side in sides:
        total = total + side[...]
    normal, scale = normal_rows(first_ref[...])
    grad = normal_back(normal, scale, g_ref[...], total)
    grad_ref[...] = grad
    low_ref[...] = grad.astype(LOW)
    add_rows(gain_ref, total * normal)
    add_rows(shift_ref, total)
    add_rows(sum_ref, grad)


def first_back(sides, grad_second, pre_first, gain):
    rows, depth = pre_first.shape
    line = pl.BlockSpec((1, depth), lambda step: (0, 0))
    return run(
        first_back_kernel,
        "first_back",
        (rows // STRIP,),
        [strip(depth)] * (len(sides) + 2) + [line],
        [strip(depth)] * 2 + [line] * 3,
        [shaped(rows, depth), shaped(rows, depth, kind=LOW)] + [shaped(1, depth)] * 3,
        (*sides, grad_second, pre_first, gain),
    )


def swap(value, distance, axis="dp"):
    count = lax.axis_size(axis)
    return lax.ppermute(value, axis, [(place, place ^ distance) for place in range(count)])


def bit_of(place, distance):
    return jnp.minimum(jnp.bitwise_and(place, distance), 1).astype(jnp.int32)


def cut(value, number, count, axis):
    size = value.shape[axis] // count
    return lax.dynamic_slice_in_dim(value, number * size, size, axis)


def ordered(bit, mine, theirs, axis):
    return jnp.where(
        bit == 0,
        jnp.concatenate([mine, theirs], axis),
        jnp.concatenate([theirs, mine], axis),
    )


def hold(value, *tokens):
    return lax.optimization_barrier((value,) + tokens)[0] if tokens else value


def take_blocks(words, sources):
    count = len(sources)

    def kernel(word_ref, *refs):
        for source, target in zip(refs[:count], refs[count:]):
            target[...] = source[...]

    return pl.pallas_call(
        kernel,
        grid_spec=pltpu.PrefetchScalarGridSpec(
            num_scalar_prefetch=1,
            grid=(1,),
            in_specs=[
                pl.BlockSpec(shape, lambda step, word, index=index: index(word))
                for _, shape, index in sources
            ],
            out_specs=[
                pl.BlockSpec(shape, lambda step, word, shape=shape: (0,) * len(shape))
                for _, shape, _ in sources
            ],
        ),
        out_shape=[shaped(*shape, kind=LOW) for _, shape, _ in sources],
        compiler_params=pltpu.CompilerParams(vmem_limit_bytes=LARGE),
        cost_estimate=cost_of("take_blocks"),
        name="take_blocks",
    )(words, *[array for array, _, _ in sources])


def split_blocks(first, second, axis):
    half = first.shape[axis] // 2
    shape = first.shape[:axis] + (half,) + first.shape[axis + 1 :]

    def kernel(first_ref, second_ref, low_ref, high_ref):
        if axis == 2:
            low_ref[...] = first_ref[:, :, :half]
            high_ref[...] = second_ref[:, :, half:]
        else:
            low_ref[...] = first_ref[:, :half]
            high_ref[...] = second_ref[:, half:]

    return run(
        kernel,
        "split_blocks",
        (1,),
        [held(first.shape), held(second.shape)],
        [held(shape), held(shape)],
        [shaped(*shape, kind=first.dtype)] * 2,
        (first, second),
    )


def join_depth(words, piece, beside, above, low_part, high_part, axis):
    size = piece.shape[axis]
    shape = piece.shape[:axis] + (4 * size,) + piece.shape[axis + 1 :]
    half = low_part.shape[3 - axis]

    def kernel(word_ref, piece_ref, beside_ref, above_ref, low_ref, high_ref, target):
        place = word_ref[2] % 4

        def span(number):
            return pl.ds(pl.multiple_of(number * size, size), size)

        for ref, number in ((piece_ref, place), (beside_ref, place ^ 2), (above_ref, place ^ 1)):
            if axis == 1:
                target[:, span(number)] = ref[...]
            else:
                target[:, :, span(number)] = ref[...]
        last = span(place ^ 3)
        if axis == 1:
            target[:, last, :half] = low_ref[...]
            target[:, last, half:] = high_ref[...]
        else:
            target[:, :half, last] = low_ref[...]
            target[:, half:, last] = high_ref[...]

    entries = [piece, beside, above, low_part, high_part]
    return run(
        kernel,
        "join_depth",
        (1,),
        [scalar_spec()] + [held(entry.shape) for entry in entries],
        held(shape),
        shaped(*shape, kind=piece.dtype),
        (words, *entries),
    )


class FetchQuarters:
    def __init__(self, clock, piece):
        self.clock = clock
        self.piece = swap(piece, 1, "mp")
        self.stages = [self.share, self.last]

    def step(self):
        self.stages.pop(0)()

    def share(self):
        self.piece = self.clock.hold(self.piece)
        self.clock.tick(self.piece)
        self.beside = swap(self.piece, 2)
        self.core_piece = swap(self.piece, 1)

    def last(self):
        self.beside = self.clock.hold(self.beside)
        self.core_piece = self.clock.hold(self.core_piece)
        self.clock.tick(self.beside, self.core_piece)
        self.parts = (self.piece, self.beside, self.core_piece, swap(self.beside, 1))


class FetchHalves:
    def __init__(self, clock, words, piece, axis):
        self.clock, self.words, self.axis = clock, words, axis
        self.piece = swap(piece, 1, "mp")
        self.stages = [self.share, self.cross, self.join]

    def step(self):
        self.stages.pop(0)()

    def share(self):
        self.piece = self.clock.hold(self.piece)
        self.clock.tick(self.piece)
        self.near = [swap(self.piece, distance) for distance in (2, 4)]

    def cross(self):
        beside, above = self.near
        low_part, high_part = split_blocks(self.clock.hold(beside), above, 3 - self.axis)
        self.clock.tick(low_part, high_part)
        self.far = [swap(low_part, 4), swap(high_part, 2)]

    def join(self):
        beside, above = self.near
        mine = join_depth(
            self.words, self.clock.hold(self.piece), beside, above, *self.far, self.axis
        )
        self.clock.tick(mine)
        self.parts = (mine, swap(mine, 1))


class Clock:
    def __init__(self):
        self.tokens = ()

    def hold(self, value):
        return hold(value, *self.tokens)

    def tick(self, *values):
        self.tokens = values


def combine(words, sides, count, cut_by):
    terms = [term for side in sides for term in side]
    _, rows, columns = terms[0][0].shape
    ways = 2 if cut_by else 1
    size = rows // ways

    def kernel(word_ref, *refs):
        sources, targets = list(refs[: len(terms)]), list(refs[len(terms) :])
        leaving = [targets.pop(0) for _ in range(ways - 1)]
        place = (word_ref[0] // cut_by) % 2 if cut_by else 0
        for number, side in enumerate(sides):
            mine = [sources.pop(0) for _ in side]

            def total(relative):
                span = slice(None)
                if ways > 1:
                    span = pl.ds(pl.multiple_of((place ^ relative) * size, size), size)
                values = [ref[:, span, :].astype(F32) for ref in mine]
                return sum(values[1:], values[0]).astype(LOW)

            targets[number][...] = total(0)
            for relative, target in enumerate(leaving, 1):
                target[number * count : (number + 1) * count] = total(relative)

    def block(number):
        return pl.BlockSpec((count, rows, columns), lambda step: (number, 0, 0))

    shapes = [(count * len(sides), size, columns)] * (ways - 1) + [(count, size, columns)] * len(sides)
    return run(
        kernel,
        "combine",
        (1,),
        [scalar_spec()] + [block(number) for _, number in terms],
        [held(shape) for shape in shapes],
        [shaped(*shape, kind=LOW) for shape in shapes],
        (words, *[array for array, _ in terms]),
    )


def join_rows(words, entries, steps):
    ways = len(entries)
    outer = steps[1] if ways == 2 else 4
    count, size, columns = entries[0].shape
    shape = (count, ways * size, columns)

    def kernel(word_ref, *refs):
        target = refs[-1]
        for step, ref in zip(steps, refs[:-1]):
            place = ((word_ref[0] ^ step) // outer) % 2
            if ways == 4:
                place = place * 2 + ((word_ref[0] ^ step) // 8) % 2
            target[:, pl.ds(pl.multiple_of(place * size, size), size), :] = ref[...]

    return run(
        kernel,
        "join_rows",
        (1,),
        [scalar_spec()] + [held(entry.shape) for entry in entries],
        held(shape),
        shaped(*shape, kind=LOW),
        (words, *entries),
    )


class Piece:
    def __init__(self, clock, words, order, source, count, direct):
        self.clock, self.words = clock, words
        self.order = list(order)
        self.back = [(ways,) for ways in reversed(order) if ways != "x"]
        if direct:
            at = self.back.index((8,))
            self.back[at : at + 2] = [(8, 4, 12)]
        self.source = source
        self.count = count
        self.flight = None
        self.kept = None
        self.complete = False

    def add(self, sides):
        array, number = sides[0][0]
        sides[0][0] = (self.clock.hold(array), number)
        ways = self.order[0] if self.order else None
        sums = combine(self.words, sides, self.count, None if ways == "x" else ways)
        self.clock.tick(sums[0])
        if ways == "x":
            self.flight = [swap(sums[-1], 1, "mp")]
            self.kept = [[(entry, 0)] for entry in sums[:-1]]
        elif ways:
            self.flight = [swap(sums[0], ways)]
            self.kept = [[(entry, 0)] for entry in sums[1:]]
        else:
            self.total = sums[0]
            self.gather()

    def gather(self):
        steps = self.back[0] if self.back else (1,)
        self.flight = [swap(self.total, distance) for distance in steps]

    def step(self):
        if self.flight is None:
            first = [(1,), (0, 1)][self.order[0] != "x"]
            self.add([self.source(side) for side in first])
            return
        if self.order:
            self.order.pop(0)
            sides = self.kept or [self.source(0)]
            for number, side in enumerate(sides):
                side += [(array, number) for array in self.flight]
            self.add(sides)
            return
        if not self.back:
            self.flight = [self.clock.hold(self.flight[0])]
            self.clock.tick(self.flight[0])
            self.complete = True
            return
        steps = (0,) + self.back.pop(0)
        entries = [self.clock.hold(self.total)] + self.flight
        self.total = join_rows(self.words, entries, steps)
        self.clock.tick(self.total)
        self.gather()


def finish_units(core, ends):
    count, half, units = ends[0].shape
    entries = count // 2
    parts = len(ends) // 2

    def kernel(core_ref, *refs):
        down_ref, up_ref = refs[-2:]
        for part in range(parts):

            @pl.when(pl.program_id(0) // entries == part)
            def _():
                for ref, number in ((refs[2 * part], core_ref[0]), (refs[2 * part + 1], 1 - core_ref[0])):
                    span = pl.ds(pl.multiple_of(number * half, half), half)
                    down_ref[:, span] = ref[0].astype(F32)
                    up_ref[span, :] = ref[1].astype(F32)

    def block(part):
        return pl.BlockSpec(
            (2, half, units), lambda step: (jnp.clip(step - part * entries, 0, entries - 1), 0, 0)
        )

    total = entries * parts * units
    return run(
        kernel,
        "finish",
        (entries * parts,),
        [scalar_spec()] + [block(number // 2) for number in range(len(ends))],
        [
            pl.BlockSpec((half, 2 * half), lambda step: (step, 0)),
            pl.BlockSpec((2 * half, units), lambda step: (0, step)),
        ],
        [shaped(total, 2 * half), shaped(2 * half, total)],
        (core, *ends),
    )


def finish_heads(core, ends):
    _, half, group = ends[0].shape
    parts = len(ends) // 2

    def kernel(core_ref, *refs):
        qkv_ref, out_ref = refs[-2:]
        for part in range(parts):

            @pl.when(pl.program_id(0) == part)
            def _():
                for ref, number in ((refs[2 * part], core_ref[0]), (refs[2 * part + 1], 1 - core_ref[0])):
                    span = pl.ds(pl.multiple_of(number * half, half), half)
                    for member in range(3):
                        qkv_ref[member, span, :] = ref[member].astype(F32)
                    for member in range(half // group):
                        start = pl.multiple_of(number * half + member * group, group)
                        rows = slice(member * group, (member + 1) * group)
                        out_ref[:, pl.ds(start, group)] = ref[3, rows, :].astype(F32)

    return run(
        kernel,
        "finish",
        (parts,),
        [scalar_spec()] + [held(entry.shape) for entry in ends],
        [
            pl.BlockSpec((3, 2 * half, group), lambda step: (0, 0, step)),
            pl.BlockSpec((group, 2 * half), lambda step: (step, 0)),
        ],
        [shaped(3, 2 * half, parts * group), shaped(parts * group, 2 * half)],
        (core, *ends),
    )


DIRECT = ""
MLP_ORDERS = ((4, 8, 2, "x"), ("x", 2, 4, 8))
HEAD_ORDERS = ((4, "x", 2, 8), (4, 2, "x", 8))
FORWARD = (
    ("own", 0),
    "a",
    ("own", 1),
    "a",
    "biases",
    "b",
    "out",
    "up",
    ("other", 0),
    "b",
    "out",
    "down",
    ("other", 1),
    "up",
    "project",
    "down",
    "up",
    "units",
    "down",
)
BACKWARD = (
    ("ub", 0),
    ("ub", 1),
    ("m", 0),
    ("m", 1),
    ("fb",),
    ("hb", 0),
    ("m", 0),
    ("h", 0),
    ("m", 1),
    ("hb", 1),
    ("m", 1),
    ("h", 0),
    ("m", 0),
    ("h", 1),
    ("m", 1),
    ("h", 0),
    ("m", 0),
    ("h", 0),
    ("m", 1),
    ("m", 0),
    ("h", 1),
    ("h", 0),
    ("m", 0),
    ("m", 1),
    ("h", 0),
    ("h", 1),
    ("h", 0),
    ("m", 1),
    ("h", 1),
    ("m", 0),
    ("h", 0),
    ("small",),
    ("h", 1),
    ("h", 0),
    ("m", 1),
    ("h", 1),
    ("m", 0),
    ("m", 1),
    ("h", 1),
    ("m", 0),
    ("h", 1),
    ("h", 1),
)


def whole_page_body(
    inputs,
    qkv_weight,
    qv_bias,
    out_weight,
    out_bias,
    norm_gain,
    norm_shift,
    up_weight,
    up_bias,
    down_weight,
    down_bias,
    cotangent,
):
    place = lax.axis_index("dp")
    core, beside, above = (bit_of(place, distance) for distance in (1, 2, 4))
    words = jnp.stack([place, core * 2 + beside, core * 4 + beside * 2 + above, core])
    words = words.astype(jnp.int32)
    core_word, quarter_word = words[3:4], words[1:2]
    nothing = jnp.zeros((1,), jnp.int32)
    quarter_order = {"own": nothing, "other": quarter_word}
    half_order = {"own": nothing, "other": core_word}
    width = qv_bias.shape[2]
    parts = width // GROUP
    rows, depth = inputs.shape
    units_here = up_bias.shape[1]
    clock = Clock()

    def qkv_block(part):
        return (qkv_weight, (1, 3, QUARTER, GROUP), lambda word: (0, 0, word[1], part))

    pieces_now = take_blocks(words, [qkv_block(0), qkv_block(1)])
    clock.tick(pieces_now[0])
    fetch = {name: FetchQuarters(clock, piece) for name, piece in zip("ab", pieces_now)}
    pieces_now = take_blocks(
        words,
        [
            (clock.hold(out_weight), (1, width, QUARTER), lambda word: (0, 0, word[1])),
            (up_weight, (1, depth // 8, units_here), lambda word: (0, word[2], 0)),
            (down_weight, (1, units_here, depth // 8), lambda word: (0, 0, word[2])),
        ],
    )
    clock.tick(pieces_now[0])
    fetch["out"] = FetchQuarters(clock, pieces_now[0])
    fetch["up"] = FetchHalves(clock, words, pieces_now[1], 1)
    fetch["down"] = FetchHalves(clock, words, pieces_now[2], 2)
    biases = jnp.concatenate([qv_bias[:, 0], qv_bias[:, 1], up_bias], 1)
    biases = {"own": biases}
    gains, shifts = norm_gain[0], norm_shift[0]
    saved = {"own": (), "other": ()}
    qkv_w = {("own", part): (qkv_weight,) for part in range(parts)}
    up_w, down_w, out_w = {"own": (up_weight,)}, {"own": (down_weight,)}, {"own": (out_weight,)}
    units = {}

    def run_heads(side, part):
        bias = biases[side] if side == "own" else clock.hold(biases[side])
        if side == "other":
            qkv_w[side, part] = fetch["ab"[part]].parts
        saved[side] = heads_forward(
            quarter_order[side],
            qkv_w[side, part],
            clock.hold(inputs),
            bias,
            part,
            parts,
            saved[side],
        )
        clock.tick(saved[side][1])

    def run_units(side):
        bias = biases[side] if side == "own" else clock.hold(biases[side])
        units[side] = units_forward(
            half_order[side], clock.hold(hidden_low), up_w[side], bias, down_w[side]
        )
        clock.tick(units[side][2])

    for action in FORWARD:
        if action == "biases":
            biases["other"] = swap(clock.hold(biases["own"]), 1, "mp")
        elif action == "project":
            out_w["other"] = fetch["out"].parts
            pre_first, hidden, hidden_low = project(
                quarter_word,
                (saved["own"][1], saved["other"][1]),
                out_weight,
                out_w["other"],
                clock.hold(inputs),
                out_bias,
                gains[0:1],
                shifts[0:1],
            )
            clock.tick(hidden_low)
        elif action == "units":
            run_units("own")
        elif isinstance(action, tuple):
            run_heads(*action)
        else:
            fetch[action].step()
    up_w["other"], down_w["other"] = fetch["up"].parts, fetch["down"].parts
    run_units("other")
    layer_out, grad_second, second_low, gain_two, shift_two, down_sum = turn(
        (units["own"][2], units["other"][2]),
        hidden,
        cotangent,
        down_bias,
        gains[1:2],
        shifts[1:2],
    )
    clock.tick(second_low)
    keep, received, totals, up_sums, head_sums = {}, {}, [], {}, {}
    state = {}

    def run_units_back(part):
        kept, sent, total, up_sums[part] = units_back(
            core_word,
            core_word,
            clock.hold(second_low),
            hidden_low,
            units,
            up_w,
            down_w,
            part,
            2,
        )
        keep["m", part], received["m", part] = kept, swap(sent, 1)
        totals.append(total)
        clock.tick(total)

    def run_first_back():
        state["first"] = first_back(totals, clock.hold(grad_second), pre_first, gains[0:1])
        state["grad_x"] = state["first"][0]
        clock.tick(state["first"][1])

    def run_heads_back(part):
        kept, sent, grad_x, head_sums[part] = heads_back(
            core_word,
            quarter_word,
            saved,
            part,
            inputs,
            clock.hold(state["first"][1]),
            {side: qkv_w[side, part] for side in ("own", "other")},
            out_w,
            state["grad_x"],
        )
        keep["h", part], received["h", part] = kept, swap(sent, 1)
        state["grad_x"] = grad_x
        clock.tick(grad_x)

    def gather_small():
        def small_of(side):
            sums = [head_sums[part][side, 0] for part in range(parts)]
            entries = [entry[:GROUP] for entry in sums] + [entry[2 * GROUP :] for entry in sums]
            for part in range(2):
                steps = up_sums[part].shape[0] // 2
                entries.append(up_sums[part][side * steps : (side + 1) * steps].reshape(-1))
            return jnp.concatenate(entries)

        gain_one, shift_one, out_sum = state["first"][2:]
        sums = (out_sum, gain_one, gain_two, shift_one, shift_two, down_sum)
        split = [small_of(0), small_of(1)]
        every = lax.all_gather(
            jnp.concatenate(split + [entry[0] for entry in sums]), ("dp", "mp"), axis=0
        )
        state["every"], state["split"] = every, split[0].shape[0]

    def add_small():
        every = clock.hold(state["every"])
        split_width = state["split"]
        odd = (lax.broadcasted_iota(jnp.int32, (every.shape[0], 1), 0) % 2) == 1
        same = [
            jnp.sum(jnp.where(odd == (number == 1), every, 0.0), axis=0) for number in range(2)
        ]
        straight = same[0][:split_width] + same[1][split_width : 2 * split_width]
        turned = same[1][:split_width] + same[0][split_width : 2 * split_width]
        split_sum = jnp.where(lax.axis_index("mp") == 0, straight, turned)
        shared = (same[0] + same[1])[2 * split_width :].reshape(6, -1)
        clock.tick(split_sum, shared)
        state["small"] = (
            split_sum[: 2 * width].reshape(1, 2, width),
            split_sum[2 * width :].reshape(1, -1),
            shared,
        )

    pieces = {}
    outcome = {}

    def run_piece(kind, number):
        key = (kind, number)
        if key not in pieces:
            orders = MLP_ORDERS if kind == "m" else HEAD_ORDERS

            def source(side):
                return [(keep[key], side), (received[key], side)]

            pieces[key] = Piece(clock, words, orders[number], source, 4, kind in DIRECT)
        pieces[key].step()
        both = [pieces.get((kind, other)) for other in range(2)]
        if kind not in outcome and all(piece and piece.complete for piece in both):
            ends = [array for piece in both for array in (piece.total, piece.flight[0])]
            ends[0] = clock.hold(ends[0])
            outcome[kind] = finish_units(core_word, ends) if kind == "m" else finish_heads(core_word, ends)
            clock.tick(outcome[kind][0])

    for action in BACKWARD:
        name, *rest = action
        if name == "ub":
            run_units_back(*rest)
        elif name == "fb":
            run_first_back()
        elif name == "hb":
            run_heads_back(*rest)
            if rest[0] == parts - 1:
                gather_small()
        elif name == "small":
            add_small()
        else:
            run_piece(*action)
    for kind in "mh":
        while kind not in outcome:
            for number in range(2):
                if not pieces[kind, number].complete:
                    run_piece(kind, number)
    grad_x = state["grad_x"]
    grad_down, grad_up = outcome["m"]
    grad_qkv, grad_out_w = outcome["h"]

    grad_qv_bias, grad_up_bias, shared = state["small"]
    return (
        layer_out,
        grad_x,
        grad_qkv[None],
        grad_qv_bias,
        grad_out_w[None],
        shared[0:1],
        shared[1:3][None],
        shared[3:5][None],
        grad_up[None],
        grad_up_bias,
        grad_down[None],
        shared[5:6],
    )


def body(inputs, *others):
    rows = inputs.shape[0]
    shared = lax.axis_size("mp") == 2 and lax.axis_size("dp") == 16
    if rows % PAGE == 0 and shared:
        return whole_page_body(inputs, *others)
    return spread_body(inputs, *others)


def solution(mesh):
    placed = (
        P(("dp", "mp"), None),
        P(None, None, None, "mp"),
        P(None, None, "mp"),
        P(None, "mp", None),
        P(),
        P(),
        P(),
        P(None, None, "mp"),
        P(None, "mp"),
        P(None, "mp", None),
        P(),
        P(("dp", "mp"), None),
    )
    return jax.shard_map(
        body,
        mesh=mesh,
        in_specs=placed,
        out_specs=(
            P(("dp", "mp"), None),
            P(("dp", "mp"), None),
            P(None, None, None, "mp"),
            P(None, None, "mp"),
            P(None, "mp", None),
            P(),
            P(),
            P(),
            P(None, None, "mp"),
            P(None, "mp"),
            P(None, "mp", None),
            P(),
        ),
        check_vma=False,
    )
```

```python
import jax
import jax.numpy as jnp
from jax import lax
from jax.experimental import pallas as pl
from jax.experimental.pallas import tpu as pltpu
from jax.sharding import PartitionSpec as P

HEAD = 64
PAGE = 416
LANES = 128

EPSILON = 1e-05
F32 = jnp.float32
LOW = jnp.bfloat16

def norm_rows(matrix, norm_scale, norm_offset):
    average = jnp.mean(matrix, axis=-1, keepdims=True)
    centered = matrix - average
    variance = jnp.mean(centered * centered, axis=-1, keepdims=True)
    return centered * lax.rsqrt(variance + EPSILON) * norm_scale + norm_offset


def exact_gelu(matrix):
    return jax.nn.gelu(matrix, approximate=False)


def spread_rows(rows_low, project):
    return project(lax.all_gather(rows_low, "mp", axis=0, tiled=True), jnp.int32(0))


def sum_rows(term, shard_rows):
    return lax.psum_scatter(
        term(jnp.int32(0), lax.axis_size("mp") * shard_rows), "mp", scatter_dimension=0, tiled=True
    )


def grad_fold(portion, acts, weight):
    weight_grad = lax.dot_general(
        acts, portion, (((0,), (0,)), ((), ())), preferred_element_type=jnp.float32
    )
    product = lax.dot_general(
        portion, weight, (((1,), (1,)), ((), ())), preferred_element_type=jnp.float32
    )
    return (product, weight_grad)


def spread_grads(grad_low, acts, weight):
    return grad_fold(lax.all_gather(grad_low, "mp", axis=0, tiled=True), acts=acts, weight=weight)


def sum_grads(term, shard_rows):
    return lax.psum_scatter(
        term(jnp.int32(0), lax.axis_size("mp") * shard_rows), "mp", scatter_dimension=0, tiled=True
    )


def page_forward(page_items):
    queries, key_rows, values = page_items
    scores = jnp.einsum("qhd,khd->hqk", queries, key_rows, preferred_element_type=jnp.float32)
    row_max = jnp.max(scores, axis=-1, keepdims=True)
    exponent = jnp.exp(scores - row_max)
    denominator = jnp.sum(exponent, axis=-1, keepdims=True)
    weights_low = (exponent / denominator).astype(jnp.bfloat16)
    log_total = row_max + jnp.log(denominator)
    attended = jnp.einsum("hqk,khd->qhd", weights_low, values, preferred_element_type=jnp.float32)
    return (attended.astype(jnp.bfloat16), log_total)


def page_backward(page_items):
    queries, key_rows, values, log_total, grad_mix = page_items
    scores = jnp.einsum("qhd,khd->hqk", queries, key_rows, preferred_element_type=jnp.float32)
    probability = jnp.exp(scores - log_total)
    weights_low = probability.astype(jnp.bfloat16)
    grad_prob = jnp.einsum("qhd,khd->hqk", grad_mix, values, preferred_element_type=jnp.float32)
    inner_total = jnp.sum(probability * grad_prob, axis=-1, keepdims=True)
    grad_scores = (probability * (grad_prob - inner_total)).astype(jnp.bfloat16)
    grad_q = jnp.einsum("hqk,khd->qhd", grad_scores, key_rows, preferred_element_type=jnp.float32)
    grad_k = jnp.einsum("hqk,qhd->khd", grad_scores, queries, preferred_element_type=jnp.float32)
    grad_v = jnp.einsum("hqk,qhd->khd", weights_low, grad_mix, preferred_element_type=jnp.float32)
    return (grad_q.astype(jnp.bfloat16), grad_k.astype(jnp.bfloat16), grad_v.astype(jnp.bfloat16))


def layer_forward(x_shard, params):
    qkv_w, qv_b, out_w, out_b, gains, shifts, up_w, up_b, down_w, down_b = params
    shard_rows = x_shard.shape[0]

    def project_qkv(portion, offset):
        return (
            jnp.einsum("rd,kde->rke", portion, qkv_w, preferred_element_type=jnp.float32),
            portion,
        )

    qkv_all, x_all = spread_rows(x_shard.astype(jnp.bfloat16), project_qkv)
    token_count = qkv_all.shape[0]
    local_width = qkv_all.shape[2]
    layout = (token_count // PAGE, PAGE, local_width // HEAD, HEAD)
    queries = ((qkv_all[:, 0] + qv_b[0]) * 0.125).astype(jnp.bfloat16).reshape(layout)
    key_rows = qkv_all[:, 1].astype(jnp.bfloat16).reshape(layout)
    values = (qkv_all[:, 2] + qv_b[1]).astype(jnp.bfloat16).reshape(layout)
    attended, log_total = lax.map(jax.checkpoint(page_forward), (queries, key_rows, values))
    attended = attended.reshape(token_count, local_width)

    def project_out(offset, amount):
        return jnp.dot(attended, out_w, preferred_element_type=jnp.float32)

    pre_first = x_shard + sum_rows(project_out, shard_rows) + out_b
    hidden = norm_rows(pre_first, gains[0], shifts[0])

    def project_up(portion, offset):
        return (jnp.dot(portion, up_w, preferred_element_type=jnp.float32), portion)

    pre_gelu, hidden_all = spread_rows(hidden.astype(jnp.bfloat16), project_up)
    pre_gelu = pre_gelu + up_b
    active = exact_gelu(pre_gelu).astype(jnp.bfloat16)

    def project_down(offset, amount):
        return jnp.dot(active, down_w, preferred_element_type=jnp.float32)

    pre_second = hidden + sum_rows(project_down, shard_rows) + down_b
    layer_out = norm_rows(pre_second, gains[1], shifts[1])
    stored = (
        x_shard,
        x_all,
        queries,
        key_rows,
        values,
        log_total,
        attended,
        pre_first,
        hidden_all,
        pre_gelu,
        active,
        pre_second,
        out_w,
    )
    return (layer_out, stored)


def layer_backward(grad_out, stored, params):
    qkv_w, qv_b, out_w, out_b, gains, shifts, up_w, up_b, down_w, down_b = params
    (
        x_shard,
        x_all,
        queries,
        key_rows,
        values,
        log_total,
        attended,
        pre_first,
        hidden_all,
        pre_gelu,
        active,
        pre_second,
        out_full,
    ) = stored
    shard_rows = grad_out.shape[0]
    norm_result, norm_back = jax.vjp(norm_rows, pre_second, gains[1], shifts[1])
    grad_second, gain_two, shift_two = norm_back(grad_out)
    grad_down_bias = jnp.sum(grad_second, axis=0)
    grad_active, grad_down = spread_grads(grad_second.astype(jnp.bfloat16), active, down_w)
    gelu_result, gelu_back = jax.vjp(exact_gelu, pre_gelu)
    grad_pre_low = gelu_back(grad_active)[0].astype(jnp.bfloat16)
    grad_up_bias = jnp.sum(grad_pre_low.astype(jnp.float32), axis=0)
    grad_up = lax.dot_general(
        hidden_all, grad_pre_low, (((0,), (0,)), ((), ())), preferred_element_type=jnp.float32
    )

    def back_up(offset, amount):
        return lax.dot_general(
            grad_pre_low, up_w, (((1,), (1,)), ((), ())), preferred_element_type=jnp.float32
        )

    grad_hidden = grad_second + sum_grads(back_up, shard_rows)
    norm_result, norm_back = jax.vjp(norm_rows, pre_first, gains[0], shifts[0])
    grad_first, gain_one, shift_one = norm_back(grad_hidden)
    grad_out_bias = jnp.sum(grad_first, axis=0)
    grad_first_low = grad_first.astype(jnp.bfloat16)
    grad_attended, grad_out_w = spread_grads(grad_first_low, attended, out_w)
    token_count = grad_attended.shape[0]
    local_width = grad_attended.shape[1]
    grad_mix = grad_attended.astype(jnp.bfloat16).reshape(queries.shape)
    grad_q, grad_k, grad_v = lax.map(
        jax.checkpoint(page_backward), (queries, key_rows, values, log_total, grad_mix)
    )
    flat_q = grad_q.reshape(token_count, local_width) * 0.125
    flat_k = grad_k.reshape(token_count, local_width)
    flat_v = grad_v.reshape(token_count, local_width)
    grad_qkv = jnp.stack([flat_q, flat_k, flat_v], axis=1)
    grad_qv_bias = jnp.stack(
        [jnp.sum(flat_q.astype(jnp.float32), axis=0), jnp.sum(flat_v.astype(jnp.float32), axis=0)]
    )
    grad_qkv_w = jnp.einsum("rd,rke->kde", x_all, grad_qkv, preferred_element_type=jnp.float32)

    def back_qkv(offset, amount):
        return jnp.einsum("rke,kde->rd", grad_qkv, qkv_w, preferred_element_type=jnp.float32)

    grad_x = grad_first + sum_grads(back_qkv, shard_rows)
    split_grads = (grad_qkv_w, grad_qv_bias, grad_out_w, grad_up, grad_up_bias, grad_down)
    shared_grads = (
        grad_out_bias,
        jnp.stack([gain_one, gain_two]),
        jnp.stack([shift_one, shift_two]),
        grad_down_bias,
    )
    return (grad_x, split_grads, shared_grads)


def spread_body(
    inputs,
    qkv_weight,
    qv_bias,
    out_weight,
    out_bias,
    norm_gain,
    norm_shift,
    up_weight,
    up_bias,
    down_weight,
    down_bias,
    cotangent,
):
    layer_total = qkv_weight.shape[0]

    def params_of(layer_number):
        return (
            qkv_weight[layer_number],
            qv_bias[layer_number],
            out_weight[layer_number],
            out_bias[layer_number],
            norm_gain[layer_number],
            norm_shift[layer_number],
            up_weight[layer_number],
            up_bias[layer_number],
            down_weight[layer_number],
            down_bias[layer_number],
        )

    current = inputs.astype(jnp.float32)
    layer_number = 0
    layer_in = current
    current, stored = layer_forward(current, params_of(layer_number))
    kept_list = [layer_in]
    grad_rows = cotangent.astype(jnp.float32)
    split_list = []
    shared_list = []
    for layer_number in reversed(range(layer_total)):
        stored = layer_forward(kept_list[layer_number], params_of(layer_number))[1]
        grad_rows, split_grads, shared_grads = layer_backward(
            grad_rows, stored, params_of(layer_number)
        )
        qkv_part, bias_part, out_part, up_part, upb_part, down_part = split_grads
        split_grads = lax.psum((qkv_part, bias_part, out_part, up_part, upb_part, down_part), "dp")
        outb_part, gain_part, shift_part, downb_part = shared_grads
        shared_grads = lax.psum((outb_part, gain_part, shift_part, downb_part), ("dp", "mp"))
        split_list.insert(0, split_grads)
        shared_list.insert(0, shared_grads)
    split_all = tuple((jnp.stack([entry[member] for entry in split_list]) for member in range(6)))
    shared_all = tuple((jnp.stack([entry[member] for entry in shared_list]) for member in range(4)))
    return (
        current,
        grad_rows,
        split_all[0],
        split_all[1],
        split_all[2],
        shared_all[0],
        shared_all[1],
        shared_all[2],
        split_all[3],
        split_all[4],
        split_all[5],
        shared_all[3],
    )


LARGE = 58 * 2**20
SPEED = 400 * 1.1e9
HEAVY = 1
UNITS = 512
GROUP = 256


def gelu_pair(u):
    below = 0.5 * lax.erf(u * 0.5**0.5) + 0.5
    return u * below, below + u * jnp.exp(u * u * -0.5) * 0.3989422804014327


def matmul(left, right, left_dim=1, right_dim=0):
    return lax.dot_general(
        left, right, (((left_dim,), (right_dim,)), ((), ())), preferred_element_type=F32
    )


def head_mask(which):
    lane = lax.broadcasted_iota(jnp.int32, (1, LANES), 1)
    return (lane // HEAD) == which


def shaped(*dims, kind=F32):
    return jax.ShapeDtypeStruct(dims, kind)


def held(dims):
    return pl.BlockSpec(dims, lambda *place: (0,) * len(dims), pipeline_mode=pl.Buffered(1))


def scalar_spec():
    return pl.BlockSpec(memory_space=pltpu.SMEM)


TIMES = {
    "heads": 8,
    "heads_back": 26,
    "units": 14,
    "units_back": 22,
    "project": 7,
    "turn": 9,
    "first_back": 10,
    "combine": 2,
    "join_rows": 2,
    "take_blocks": 3,
    "split_blocks": 2,
    "join_depth": 3,
    "finish": 6,
}


def cost_of(name):
    return pl.CostEstimate(
        flops=int((TIMES[name] if TIMES[name] < 5 else TIMES[name] * HEAVY) * SPEED), bytes_accessed=1, transcendentals=0
    )


def run(kernel, name, grid, in_specs, out_specs, out_shape, operands, scratch=()):
    return pl.pallas_call(
        kernel,
        grid=grid,
        in_specs=in_specs,
        out_specs=out_specs,
        out_shape=out_shape,
        scratch_shapes=list(scratch),
        compiler_params=pltpu.CompilerParams(vmem_limit_bytes=LARGE),
        cost_estimate=cost_of(name),
        name=name,
    )(*operands)


def spans(pair):
    return [
        slice(start * GROUP + pair * LANES, start * GROUP + (pair + 1) * LANES)
        for start in range(3)
    ]


def gather_depth(order_ref, refs, target, by_column):
    for relative, ref in enumerate(refs):
        span = pl.ds(pl.multiple_of((order_ref[0] ^ relative) * QUARTER, QUARTER), QUARTER)
        if by_column:
            target[:, span] = ref[0]
        else:
            for member in range(3):
                target[span, member * GROUP : (member + 1) * GROUP] = ref[0, member]


QUARTER = 256


def qkv_specs(quarters, part):
    shape = (1, 3, QUARTER, GROUP)
    if len(quarters) == 1:
        return [
            pl.BlockSpec(
                shape,
                lambda page, number=number: (0, 0, number, part),
                pipeline_mode=pl.Buffered(1),
            )
            for number in range(4)
        ]
    return [held(shape)] * 4


def four_times(quarters):
    return list(quarters) * (4 // len(quarters))


def heads_kernel(order_ref, w0_ref, w1_ref, w2_ref, w3_ref, x_ref, bq_ref, bv_ref, *refs):
    three_ref, o_ref, lse_ref, weight = refs[-4:]

    @pl.when(pl.program_id(0) == 0)
    def _():
        gather_depth(order_ref, (w0_ref, w1_ref, w2_ref, w3_ref), weight, False)

    product = matmul(x_ref[...], weight[...])
    three_ref[:, :GROUP] = ((product[:, :GROUP] + bq_ref[...]) * 0.125).astype(LOW)
    three_ref[:, GROUP : 2 * GROUP] = product[:, GROUP : 2 * GROUP].astype(LOW)
    three_ref[:, 2 * GROUP :] = (product[:, 2 * GROUP :] + bv_ref[...]).astype(LOW)
    for pair in range(GROUP // LANES):
        queries, key_rows, values = (three_ref[:, entry] for entry in spans(pair))
        values_t = values.T
        columns = []
        for which in range(LANES // HEAD):
            head = pair * (LANES // HEAD) + which
            keys_one = jnp.where(head_mask(which), key_rows, jnp.zeros_like(key_rows))
            scores = matmul(keys_one, queries, 1, 1)
            peak = jnp.max(scores, axis=0, keepdims=True)
            exponent = jnp.exp(scores - peak)
            denominator = jnp.sum(exponent, axis=0, keepdims=True)
            weights_low = (exponent * (1.0 / denominator)).astype(LOW)
            columns.append(matmul(values_t[which * HEAD : (which + 1) * HEAD], weights_low))
            lse_ref[0, 0, head : head + 1, :] = peak + jnp.log(denominator)
        o_ref[:, pair * LANES : (pair + 1) * LANES] = (
            jnp.concatenate(columns, axis=0).T.astype(LOW)
        )


def heads_forward(order, quarters, x_low, bias, part, parts, before=()):
    rows, depth = x_low.shape
    width = 3 * GROUP
    pages = rows // PAGE
    count = GROUP // HEAD
    return pl.pallas_call(
        heads_kernel,
        grid=(pages,),
        in_specs=[scalar_spec()]
        + qkv_specs(quarters, part)
        + [
            pl.BlockSpec((PAGE, depth), lambda page: (page, 0)),
            pl.BlockSpec((1, GROUP), lambda page: (0, part)),
            pl.BlockSpec((1, GROUP), lambda page: (0, parts + part)),
        ]
        + [pl.BlockSpec(memory_space=pl.ANY)] * len(before),
        out_specs=[
            pl.BlockSpec((PAGE, width), lambda page: (page, part)),
            pl.BlockSpec((PAGE, GROUP), lambda page: (page, part)),
            pl.BlockSpec((1, 1, count, PAGE), lambda page: (part, page, 0, 0)),
        ],
        out_shape=[
            shaped(rows, parts * width, kind=LOW),
            shaped(rows, parts * GROUP, kind=LOW),
            shaped(parts, pages, count, PAGE),
        ],
        scratch_shapes=[pltpu.VMEM((depth, width), LOW)],
        input_output_aliases={8 + number: number for number in range(len(before))},
        compiler_params=pltpu.CompilerParams(vmem_limit_bytes=LARGE),
        cost_estimate=cost_of("heads"),
        name="heads",
    )(order, *four_times(quarters), x_low, bias, bias, *before)


def heads_back_kernel(core_ref, order_ref, x_ref, g_ref, before_ref, *refs):
    keep_ref, send_ref, gx_ref, sum_ref = refs[22:26]
    qkv_total, out_total, weight, out_weight = refs[26:]
    side, page = pl.program_id(0), pl.program_id(1)
    pages = pl.num_programs(1)
    core = core_ref[0]
    half = x_ref.shape[1] // 2

    def work(order, first_side, three_ref, lse_ref, att_ref, *weights):
        @pl.when(page == 0)
        def _():
            gather_depth(order, weights[:4], weight, False)
            gather_depth(order, weights[4:], out_weight, True)

        mix = matmul(g_ref[...], out_weight[...], 1, 1).astype(LOW)
        grads_three = [None] * (3 * (GROUP // LANES))
        for pair in range(GROUP // LANES):
            queries, key_rows, values = (three_ref[:, entry] for entry in spans(pair))
            grads = mix[:, pair * LANES : (pair + 1) * LANES]
            keys_t = key_rows.T
            columns, dk_parts, dv_parts = [], [], []
            for which in range(LANES // HEAD):
                head = pair * (LANES // HEAD) + which
                mask = head_mask(which)
                keys_one = jnp.where(mask, key_rows, jnp.zeros_like(key_rows))
                scores = matmul(keys_one, queries, 1, 1)
                probability = jnp.exp(scores - lse_ref[0, 0, head : head + 1, :])
                values_one = jnp.where(mask, values, jnp.zeros_like(values))
                grad_prob = matmul(values_one, grads, 1, 1)
                inner = jnp.sum(probability * grad_prob, axis=0, keepdims=True)
                grad_scores = (probability * (grad_prob - inner)).astype(LOW)
                dv_parts.append(matmul(probability.astype(LOW), grads))
                dk_parts.append(matmul(grad_scores, queries))
                columns.append(matmul(keys_t[which * HEAD : (which + 1) * HEAD], grad_scores))
            first = head_mask(0)
            grad_q = jnp.concatenate(columns, axis=0).T.astype(LOW)
            grads_three[pair] = (grad_q.astype(F32) * 0.125).astype(LOW)
            grads_three[2 + pair] = jnp.where(first, dk_parts[0], dk_parts[1]).astype(LOW)
            grads_three[4 + pair] = jnp.where(first, dv_parts[0], dv_parts[1]).astype(LOW)
        three = jnp.concatenate(grads_three, axis=1)
        start = page == 0
        sums = jnp.sum(three.astype(F32), axis=0, keepdims=True)
        sum_ref[0] = jnp.where(start, 0.0, sum_ref[0]) + sums
        product = matmul(x_ref[...], three, 0, 0)
        qkv_total[...] = jnp.where(start, 0.0, qkv_total[...]) + product
        product = matmul(att_ref[...], g_ref[...], 0, 0)
        out_total[...] = jnp.where(start, 0.0, out_total[...]) + product
        rows = pl.ds(pl.multiple_of(page * PAGE, PAGE), PAGE)
        before = before_ref[...] if first_side else gx_ref[rows, :]
        gx_ref[rows, :] = before + matmul(three, weight[...], 1, 1)

    @pl.when(side == 0)
    def _():
        work((0,), True, *refs[:11])

    @pl.when(side == 1)
    def _():
        work(order_ref, False, *refs[11:22])

    @pl.when(page == pages - 1)
    def _():
        for ref, number in ((keep_ref, core), (send_ref, 1 - core)):
            start = pl.multiple_of(number * half, half)
            for member in range(3):
                span = slice(member * GROUP, (member + 1) * GROUP)
                ref[member] = qkv_total[pl.ds(start, half), span].astype(LOW)
            for member in range(2):
                column = pl.ds(pl.multiple_of(number * half + member * GROUP, GROUP), GROUP)
                ref[3, member * GROUP : (member + 1) * GROUP, :] = out_total[:, column].astype(LOW)


def heads_back(core, order, saved, part, x_low, grad_low, qkv, out, before):
    rows, depth = x_low.shape
    width = 3 * GROUP
    pages = rows // PAGE
    count = GROUP // HEAD
    half = depth // 2
    block = pl.BlockSpec((4, half, GROUP), lambda side, page: (side, 0, 0))
    line = pl.BlockSpec((PAGE, depth), lambda side, page: (page, 0))
    once = pl.BlockSpec(
        (PAGE, depth), lambda side, page: (jnp.where(side == 0, page, pages - 1), 0)
    )
    in_specs, operands = [], []
    for number, side in enumerate(("own", "other")):

        def page_of(side, page, number=number):
            return jnp.where(side == number, page, 0 if number else pages - 1)

        def beside(side, page, page_of=page_of):
            return (page_of(side, page), part)

        def above(side, page, page_of=page_of):
            return (part, page_of(side, page), 0, 0)

        in_specs += [
            pl.BlockSpec((PAGE, width), beside),
            pl.BlockSpec((1, 1, count, PAGE), above),
            pl.BlockSpec((PAGE, GROUP), beside),
        ]
        for quarter in range(4):
            fixed = (0, 0, quarter, part) if side == "own" else (0, 0, 0, 0)
            in_specs.append(
                pl.BlockSpec(
                    (1, 3, QUARTER, GROUP),
                    lambda side, page, fixed=fixed: fixed,
                    pipeline_mode=pl.Buffered(1),
                )
            )
        for quarter in range(4):
            fixed = (0, part, quarter if side == "own" else 0)
            in_specs.append(
                pl.BlockSpec(
                    (1, GROUP, QUARTER),
                    lambda side, page, fixed=fixed: fixed,
                    pipeline_mode=pl.Buffered(1),
                )
            )
        three, attended, lse = saved[side]
        operands += [three, lse, attended, *four_times(qkv[side]), *four_times(out[side])]
    return run(
        heads_back_kernel,
        "heads_back",
        (2, pages),
        [scalar_spec(), scalar_spec(), line, line, once] + in_specs,
        [
            block,
            block,
            held((rows, depth)),
            pl.BlockSpec((1, 1, width), lambda side, page: (side, 0, 0)),
        ],
        [
            shaped(8, half, GROUP, kind=LOW),
            shaped(8, half, GROUP, kind=LOW),
            shaped(rows, depth),
            shaped(2, 1, width),
        ],
        (core, order, x_low, grad_low, before, *operands),
        [
            pltpu.VMEM((depth, width), F32),
            pltpu.VMEM((GROUP, depth), F32),
            pltpu.VMEM((depth, width), LOW),
            pltpu.VMEM((GROUP, depth), LOW),
        ],
    )


ROW_STEPS = 1


def pair_specs(pair, shape, axis, first=0):
    def place(step, number):
        return (0, number, step + first) if axis == 1 else (0, step + first, number)

    if len(pair) == 1:
        return [
            pl.BlockSpec((1,) + shape, lambda step, number=number: place(step, number))
            for number in range(2)
        ]
    return [pl.BlockSpec((1,) + shape, lambda step: place(step, 0)) for _ in range(2)]


def twice(pair):
    return list(pair) * (2 // len(pair))


def depth_spans(order_ref, half):
    return [
        pl.ds(pl.multiple_of((order_ref[0] ^ relative) * half, half), half)
        for relative in range(2)
    ]


def units_kernel(order_ref, h_ref, up_a, up_b, b_ref, down_a, down_b, *outs):
    active_ref, slope_ref, total_ref = outs
    rows = h_ref.shape[0] // ROW_STEPS
    first, second = depth_spans(order_ref, h_ref.shape[1] // 2)
    for part in range(ROW_STEPS):
        span = slice(part * rows, (part + 1) * rows)
        pre = matmul(h_ref[span, first], up_a[0]) + matmul(h_ref[span, second], up_b[0])
        value, slope = gelu_pair(pre + b_ref[...])
        value = value.astype(LOW)
        active_ref[span, :] = value
        slope_ref[span, :] = slope.astype(LOW)
        for place, weight in ((first, down_a), (second, down_b)):
            before = jnp.where(pl.program_id(0) == 0, 0.0, total_ref[span, place])
            total_ref[span, place] = before + matmul(value, weight[0])


def units_forward(order, hidden_low, up, bias, down):
    rows, depth = hidden_low.shape
    units = down[0].shape[1]
    skip = (bias.shape[1] - units) // UNITS
    half = depth // 2
    column = pl.BlockSpec((rows, UNITS), lambda step: (0, step))
    return run(
        units_kernel,
        "units",
        (units // UNITS,),
        [scalar_spec(), held((rows, depth))]
        + pair_specs(up, (half, UNITS), 1)
        + [pl.BlockSpec((1, UNITS), lambda step: (0, step + skip))]
        + pair_specs(down, (UNITS, half), 2),
        [column, column, held((rows, depth))],
        [shaped(rows, units, kind=LOW), shaped(rows, units, kind=LOW), shaped(rows, depth)],
        (order, hidden_low, *twice(up), bias, *twice(down)),
    )


def units_back_kernel(core_ref, order_ref, g_ref, h_ref, *refs):
    keep_ref, send_ref, total_ref, sum_ref = refs[-4:]
    core = core_ref[0]
    half = g_ref.shape[1] // 2
    step = pl.program_id(0)
    steps = pl.num_programs(0) // 2

    def work(order, active_ref, slope_ref, up_a, up_b, down_a, down_b):
        first, second = depth_spans(order, half)
        grad = matmul(g_ref[:, first], down_a[0], 1, 1)
        grad = grad + matmul(g_ref[:, second], down_b[0], 1, 1)
        grad_low = (grad * slope_ref[...].astype(F32)).astype(LOW)
        sum_ref[0] = jnp.sum(grad_low.astype(F32), axis=0, keepdims=True)
        for place, weight in ((first, up_a), (second, up_b)):
            before = jnp.where(step == 0, 0.0, total_ref[:, place])
            total_ref[:, place] = before + matmul(grad_low, weight[0], 1, 1)
        for ref, number in ((keep_ref, core), (send_ref, 1 - core)):
            span = pl.ds(pl.multiple_of(number * half, half), half)
            ref[0] = matmul(active_ref[...], g_ref[:, span], 0, 0).astype(LOW)
            ref[1] = matmul(h_ref[:, span], grad_low, 0, 0).astype(LOW)

    @pl.when(step < steps)
    def _():
        work((0,), *refs[:6])

    @pl.when(step >= steps)
    def _():
        work(order_ref, *refs[6:12])


def units_back(core, order, grad_low, hidden_low, units, up, down, part, parts):
    rows, depth = hidden_low.shape
    here = units["own"][0].shape[1] // parts
    half = depth // 2
    steps = here // UNITS
    first = part * steps
    in_specs, operands = [], []
    for side, least in (("own", 0), ("other", steps)):

        def number(step, least=least):
            return first + jnp.clip(step - least, 0, steps - 1)

        column = pl.BlockSpec((rows, UNITS), lambda step, number=number: (0, number(step)))
        in_specs += [column, column]
        for axis, pair, shape in ((1, up, (half, UNITS)), (2, down, (UNITS, half))):
            for which in range(2):
                fixed = which if side == "own" else 0

                def place(step, axis=axis, fixed=fixed, number=number):
                    moving = number(step)
                    return (0, fixed, moving) if axis == 1 else (0, moving, fixed)

                in_specs.append(pl.BlockSpec((1,) + shape, place))
        operands += [*units[side][:2], *twice(up[side]), *twice(down[side])]
    block = pl.BlockSpec((2, half, UNITS), lambda step: (step, 0, 0))
    return run(
        units_back_kernel,
        "units_back",
        (2 * steps,),
        [scalar_spec(), scalar_spec(), held((rows, depth)), held((rows, depth))] + in_specs,
        [
            block,
            block,
            held((rows, depth)),
            pl.BlockSpec((1, 1, UNITS), lambda step: (step, 0, 0)),
        ],
        [
            shaped(4 * steps, half, UNITS, kind=LOW),
            shaped(4 * steps, half, UNITS, kind=LOW),
            shaped(rows, depth),
            shaped(2 * steps, 1, UNITS),
        ],
        (core, order, grad_low, hidden_low, *operands),
    )


def normal_rows(matrix):
    average = jnp.mean(matrix, axis=-1, keepdims=True)
    centered = matrix - average
    variance = jnp.mean(centered * centered, axis=-1, keepdims=True)
    scale = lax.rsqrt(variance + EPSILON)
    return centered * scale, scale


def normal_back(normal, scale, gain, grad):
    scaled = gain * grad
    level = jnp.mean(scaled, axis=-1, keepdims=True)
    along = jnp.mean(scaled * normal, axis=-1, keepdims=True)
    return scale * (scaled - level - normal * along)


def add_rows(ref, matrix):
    total = jnp.sum(matrix, axis=0, keepdims=True)
    before = jnp.where(pl.program_id(0) == 0, 0.0, ref[...])
    ref[...] = before + total


STRIP = 208


def strip(columns):
    return pl.BlockSpec((STRIP, columns), lambda step: (step, 0))


def project_kernel(order_ref, a_ref, b_ref, wa_ref, w0, w1, w2, w3, x_ref, *refs):
    bias_ref, g_ref, s_ref, first_ref, hidden_ref, low_ref = refs
    first_ref[...] = x_ref[...].astype(F32) + bias_ref[...] + matmul(a_ref[...], wa_ref[0])
    for relative, weight in enumerate((w0, w1, w2, w3)):
        span = pl.ds(pl.multiple_of((order_ref[0] ^ relative) * QUARTER, QUARTER), QUARTER)
        first_ref[:, span] += matmul(b_ref[...], weight[0])
    hidden = normal_rows(first_ref[...])[0] * g_ref[...] + s_ref[...]
    hidden_ref[...] = hidden
    low_ref[...] = hidden.astype(LOW)


def project(order, sides, own, quarters, x_low, bias, gain, shift):
    rows, depth = x_low.shape
    line = held((1, depth))
    page = pl.BlockSpec((PAGE, depth), lambda step: (step, 0))
    side = pl.BlockSpec((PAGE, sides[0].shape[1]), lambda step: (step, 0))
    return run(
        project_kernel,
        "project",
        (rows // PAGE,),
        [scalar_spec(), side, side, held(own.shape)]
        + [held(entry.shape) for entry in quarters]
        + [page, line, line, line],
        [page] * 3,
        [shaped(rows, depth), shaped(rows, depth), shaped(rows, depth, kind=LOW)],
        (order, *sides, own, *quarters, x_low, bias, gain, shift),
    )


def turn_kernel(a_ref, b_ref, h_ref, c_ref, bias_ref, g_ref, s_ref, *outs):
    out_ref, grad_ref, low_ref, gain_ref, shift_ref, sum_ref = outs
    normal, scale = normal_rows(h_ref[...] + (a_ref[...] + b_ref[...]) + bias_ref[...])
    out_ref[...] = normal * g_ref[...] + s_ref[...]
    grad_out = c_ref[...].astype(F32)
    grad = normal_back(normal, scale, g_ref[...], grad_out)
    grad_ref[...] = grad
    low_ref[...] = grad.astype(LOW)
    add_rows(gain_ref, grad_out * normal)
    add_rows(shift_ref, grad_out)
    add_rows(sum_ref, grad)


def turn(sides, hidden, cotangent, bias, gain, shift):
    rows, depth = hidden.shape
    line = pl.BlockSpec((1, depth), lambda step: (0, 0))
    return run(
        turn_kernel,
        "turn",
        (rows // STRIP,),
        [strip(depth)] * 4 + [line] * 3,
        [strip(depth)] * 3 + [line] * 3,
        [shaped(rows, depth), shaped(rows, depth), shaped(rows, depth, kind=LOW)]
        + [shaped(1, depth)] * 3,
        (*sides, hidden, cotangent, bias, gain, shift),
    )


def first_back_kernel(*refs):
    *sides, second_ref, first_ref, g_ref = refs[:-5]
    grad_ref, low_ref, gain_ref, shift_ref, sum_ref = refs[-5:]
    total = second_ref[...]
    for side in sides:
        total = total + side[...]
    normal, scale = normal_rows(first_ref[...])
    grad = normal_back(normal, scale, g_ref[...], total)
    grad_ref[...] = grad
    low_ref[...] = grad.astype(LOW)
    add_rows(gain_ref, total * normal)
    add_rows(shift_ref, total)
    add_rows(sum_ref, grad)


def first_back(sides, grad_second, pre_first, gain):
    rows, depth = pre_first.shape
    line = pl.BlockSpec((1, depth), lambda step: (0, 0))
    return run(
        first_back_kernel,
        "first_back",
        (rows // STRIP,),
        [strip(depth)] * (len(sides) + 2) + [line],
        [strip(depth)] * 2 + [line] * 3,
        [shaped(rows, depth), shaped(rows, depth, kind=LOW)] + [shaped(1, depth)] * 3,
        (*sides, grad_second, pre_first, gain),
    )


def swap(value, distance, axis="dp"):
    count = lax.axis_size(axis)
    return lax.ppermute(value, axis, [(place, place ^ distance) for place in range(count)])


def bit_of(place, distance):
    return jnp.minimum(jnp.bitwise_and(place, distance), 1).astype(jnp.int32)


def cut(value, number, count, axis):
    size = value.shape[axis] // count
    return lax.dynamic_slice_in_dim(value, number * size, size, axis)


def ordered(bit, mine, theirs, axis):
    return jnp.where(
        bit == 0,
        jnp.concatenate([mine, theirs], axis),
        jnp.concatenate([theirs, mine], axis),
    )


def hold(value, *tokens):
    return lax.optimization_barrier((value,) + tokens)[0] if tokens else value


def take_blocks(words, sources):
    count = len(sources)

    def kernel(word_ref, *refs):
        for source, target in zip(refs[:count], refs[count:]):
            target[...] = source[...]

    return pl.pallas_call(
        kernel,
        grid_spec=pltpu.PrefetchScalarGridSpec(
            num_scalar_prefetch=1,
            grid=(1,),
            in_specs=[
                pl.BlockSpec(shape, lambda step, word, index=index: index(word))
                for _, shape, index in sources
            ],
            out_specs=[
                pl.BlockSpec(shape, lambda step, word, shape=shape: (0,) * len(shape))
                for _, shape, _ in sources
            ],
        ),
        out_shape=[shaped(*shape, kind=LOW) for _, shape, _ in sources],
        compiler_params=pltpu.CompilerParams(vmem_limit_bytes=LARGE),
        cost_estimate=cost_of("take_blocks"),
        name="take_blocks",
    )(words, *[array for array, _, _ in sources])


def split_blocks(first, second, axis):
    half = first.shape[axis] // 2
    shape = first.shape[:axis] + (half,) + first.shape[axis + 1 :]

    def kernel(first_ref, second_ref, low_ref, high_ref):
        if axis == 2:
            low_ref[...] = first_ref[:, :, :half]
            high_ref[...] = second_ref[:, :, half:]
        else:
            low_ref[...] = first_ref[:, :half]
            high_ref[...] = second_ref[:, half:]

    return run(
        kernel,
        "split_blocks",
        (1,),
        [held(first.shape), held(second.shape)],
        [held(shape), held(shape)],
        [shaped(*shape, kind=first.dtype)] * 2,
        (first, second),
    )


def join_depth(words, piece, beside, above, low_part, high_part, axis):
    size = piece.shape[axis]
    shape = piece.shape[:axis] + (4 * size,) + piece.shape[axis + 1 :]
    half = low_part.shape[3 - axis]

    def kernel(word_ref, piece_ref, beside_ref, above_ref, low_ref, high_ref, target):
        place = word_ref[2] % 4

        def span(number):
            return pl.ds(pl.multiple_of(number * size, size), size)

        for ref, number in ((piece_ref, place), (beside_ref, place ^ 2), (above_ref, place ^ 1)):
            if axis == 1:
                target[:, span(number)] = ref[...]
            else:
                target[:, :, span(number)] = ref[...]
        last = span(place ^ 3)
        if axis == 1:
            target[:, last, :half] = low_ref[...]
            target[:, last, half:] = high_ref[...]
        else:
            target[:, :half, last] = low_ref[...]
            target[:, half:, last] = high_ref[...]

    entries = [piece, beside, above, low_part, high_part]
    return run(
        kernel,
        "join_depth",
        (1,),
        [scalar_spec()] + [held(entry.shape) for entry in entries],
        held(shape),
        shaped(*shape, kind=piece.dtype),
        (words, *entries),
    )


class FetchQuarters:
    def __init__(self, clock, piece):
        self.clock = clock
        self.piece = swap(piece, 1, "mp")
        self.stages = [self.share, self.last]

    def step(self):
        self.stages.pop(0)()

    def share(self):
        self.piece = self.clock.hold(self.piece)
        self.clock.tick(self.piece)
        self.beside = swap(self.piece, 2)
        self.core_piece = swap(self.piece, 1)

    def last(self):
        self.beside = self.clock.hold(self.beside)
        self.core_piece = self.clock.hold(self.core_piece)
        self.clock.tick(self.beside, self.core_piece)
        self.parts = (self.piece, self.beside, self.core_piece, swap(self.beside, 1))


class FetchHalves:
    def __init__(self, clock, words, piece, axis):
        self.clock, self.words, self.axis = clock, words, axis
        self.piece = swap(piece, 1, "mp")
        self.stages = [self.share, self.cross, self.join]

    def step(self):
        self.stages.pop(0)()

    def share(self):
        self.piece = self.clock.hold(self.piece)
        self.clock.tick(self.piece)
        self.near = [swap(self.piece, distance) for distance in (2, 4)]

    def cross(self):
        beside, above = self.near
        low_part, high_part = split_blocks(self.clock.hold(beside), above, 3 - self.axis)
        self.clock.tick(low_part, high_part)
        self.far = [swap(low_part, 4), swap(high_part, 2)]

    def join(self):
        beside, above = self.near
        mine = join_depth(
            self.words, self.clock.hold(self.piece), beside, above, *self.far, self.axis
        )
        self.clock.tick(mine)
        self.parts = (mine, swap(mine, 1))


class Clock:
    def __init__(self):
        self.tokens = ()

    def hold(self, value):
        return hold(value, *self.tokens)

    def tick(self, *values):
        self.tokens = values


def combine(words, sides, count, cut_by):
    terms = [term for side in sides for term in side]
    _, rows, columns = terms[0][0].shape
    ways = 2 if cut_by else 1
    size = rows // ways

    def kernel(word_ref, *refs):
        sources, targets = list(refs[: len(terms)]), list(refs[len(terms) :])
        leaving = [targets.pop(0) for _ in range(ways - 1)]
        place = (word_ref[0] // cut_by) % 2 if cut_by else 0
        for number, side in enumerate(sides):
            mine = [sources.pop(0) for _ in side]

            def total(relative):
                span = slice(None)
                if ways > 1:
                    span = pl.ds(pl.multiple_of((place ^ relative) * size, size), size)
                values = [ref[:, span, :].astype(F32) for ref in mine]
                return sum(values[1:], values[0]).astype(LOW)

            targets[number][...] = total(0)
            for relative, target in enumerate(leaving, 1):
                target[number * count : (number + 1) * count] = total(relative)

    def block(number):
        return pl.BlockSpec((count, rows, columns), lambda step: (number, 0, 0))

    shapes = [(count * len(sides), size, columns)] * (ways - 1) + [(count, size, columns)] * len(sides)
    return run(
        kernel,
        "combine",
        (1,),
        [scalar_spec()] + [block(number) for _, number in terms],
        [held(shape) for shape in shapes],
        [shaped(*shape, kind=LOW) for shape in shapes],
        (words, *[array for array, _ in terms]),
    )


def join_rows(words, entries, steps):
    ways = len(entries)
    outer = steps[1] if ways == 2 else 4
    count, size, columns = entries[0].shape
    shape = (count, ways * size, columns)

    def kernel(word_ref, *refs):
        target = refs[-1]
        for step, ref in zip(steps, refs[:-1]):
            place = ((word_ref[0] ^ step) // outer) % 2
            if ways == 4:
                place = place * 2 + ((word_ref[0] ^ step) // 8) % 2
            target[:, pl.ds(pl.multiple_of(place * size, size), size), :] = ref[...]

    return run(
        kernel,
        "join_rows",
        (1,),
        [scalar_spec()] + [held(entry.shape) for entry in entries],
        held(shape),
        shaped(*shape, kind=LOW),
        (words, *entries),
    )


class Piece:
    def __init__(self, clock, words, order, source, count, direct):
        self.clock, self.words = clock, words
        self.order = list(order)
        self.back = [(ways,) for ways in reversed(order) if ways != "x"]
        if direct:
            at = self.back.index((8,))
            self.back[at : at + 2] = [(8, 4, 12)]
        self.source = source
        self.count = count
        self.flight = None
        self.kept = None
        self.complete = False

    def add(self, sides):
        array, number = sides[0][0]
        sides[0][0] = (self.clock.hold(array), number)
        ways = self.order[0] if self.order else None
        sums = combine(self.words, sides, self.count, None if ways == "x" else ways)
        self.clock.tick(sums[0])
        if ways == "x":
            self.flight = [swap(sums[-1], 1, "mp")]
            self.kept = [[(entry, 0)] for entry in sums[:-1]]
        elif ways:
            self.flight = [swap(sums[0], ways)]
            self.kept = [[(entry, 0)] for entry in sums[1:]]
        else:
            self.total = sums[0]
            self.gather()

    def gather(self):
        steps = self.back[0] if self.back else (1,)
        self.flight = [swap(self.total, distance) for distance in steps]

    def step(self):
        if self.flight is None:
            first = [(1,), (0, 1)][self.order[0] != "x"]
            self.add([self.source(side) for side in first])
            return
        if self.order:
            self.order.pop(0)
            sides = self.kept or [self.source(0)]
            for number, side in enumerate(sides):
                side += [(array, number) for array in self.flight]
            self.add(sides)
            return
        if not self.back:
            self.flight = [self.clock.hold(self.flight[0])]
            self.clock.tick(self.flight[0])
            self.complete = True
            return
        steps = (0,) + self.back.pop(0)
        entries = [self.clock.hold(self.total)] + self.flight
        self.total = join_rows(self.words, entries, steps)
        self.clock.tick(self.total)
        self.gather()


def finish_units(core, ends):
    count, half, units = ends[0].shape
    entries = count // 2
    parts = len(ends) // 2

    def kernel(core_ref, *refs):
        down_ref, up_ref = refs[-2:]
        for part in range(parts):

            @pl.when(pl.program_id(0) // entries == part)
            def _():
                for ref, number in ((refs[2 * part], core_ref[0]), (refs[2 * part + 1], 1 - core_ref[0])):
                    span = pl.ds(pl.multiple_of(number * half, half), half)
                    down_ref[:, span] = ref[0].astype(F32)
                    up_ref[span, :] = ref[1].astype(F32)

    def block(part):
        return pl.BlockSpec(
            (2, half, units), lambda step: (jnp.clip(step - part * entries, 0, entries - 1), 0, 0)
        )

    total = entries * parts * units
    return run(
        kernel,
        "finish",
        (entries * parts,),
        [scalar_spec()] + [block(number // 2) for number in range(len(ends))],
        [
            pl.BlockSpec((half, 2 * half), lambda step: (step, 0)),
            pl.BlockSpec((2 * half, units), lambda step: (0, step)),
        ],
        [shaped(total, 2 * half), shaped(2 * half, total)],
        (core, *ends),
    )


def finish_heads(core, ends):
    _, half, group = ends[0].shape
    parts = len(ends) // 2

    def kernel(core_ref, *refs):
        qkv_ref, out_ref = refs[-2:]
        for part in range(parts):

            @pl.when(pl.program_id(0) == part)
            def _():
                for ref, number in ((refs[2 * part], core_ref[0]), (refs[2 * part + 1], 1 - core_ref[0])):
                    span = pl.ds(pl.multiple_of(number * half, half), half)
                    for member in range(3):
                        qkv_ref[member, span, :] = ref[member].astype(F32)
                    for member in range(half // group):
                        start = pl.multiple_of(number * half + member * group, group)
                        rows = slice(member * group, (member + 1) * group)
                        out_ref[:, pl.ds(start, group)] = ref[3, rows, :].astype(F32)

    return run(
        kernel,
        "finish",
        (parts,),
        [scalar_spec()] + [held(entry.shape) for entry in ends],
        [
            pl.BlockSpec((3, 2 * half, group), lambda step: (0, 0, step)),
            pl.BlockSpec((group, 2 * half), lambda step: (step, 0)),
        ],
        [shaped(3, 2 * half, parts * group), shaped(parts * group, 2 * half)],
        (core, *ends),
    )


DIRECT = ""
MLP_ORDERS = ((4, 8, 2, "x"), ("x", 2, 4, 8))
HEAD_ORDERS = ((4, "x", 2, 8), (4, 2, "x", 8))
FORWARD = (
    ("own", 0),
    "a",
    ("own", 1),
    "a",
    "biases",
    "b",
    "up",
    ("other", 0),
    "out",
    "b",
    "down",
    ("other", 1),
    "out",
    "up",
    "project",
    "down",
    "up",
    "units",
    "down",
)
BACKWARD = (
    ("ub", 0),
    ("ub", 1),
    ("m", 0),
    ("m", 1),
    ("fb",),
    ("hb", 0),
    ("m", 0),
    ("h", 0),
    ("m", 1),
    ("hb", 1),
    ("m", 1),
    ("h", 0),
    ("m", 0),
    ("h", 1),
    ("m", 1),
    ("h", 0),
    ("m", 0),
    ("h", 0),
    ("m", 1),
    ("m", 0),
    ("h", 1),
    ("h", 0),
    ("m", 0),
    ("m", 1),
    ("h", 0),
    ("h", 1),
    ("h", 0),
    ("m", 1),
    ("h", 1),
    ("m", 0),
    ("h", 0),
    ("small",),
    ("h", 1),
    ("h", 0),
    ("m", 1),
    ("h", 1),
    ("m", 0),
    ("m", 1),
    ("h", 1),
    ("m", 0),
    ("h", 1),
    ("h", 1),
)


def whole_page_body(
    inputs,
    qkv_weight,
    qv_bias,
    out_weight,
    out_bias,
    norm_gain,
    norm_shift,
    up_weight,
    up_bias,
    down_weight,
    down_bias,
    cotangent,
):
    place = lax.axis_index("dp")
    core, beside, above = (bit_of(place, distance) for distance in (1, 2, 4))
    words = jnp.stack([place, core * 2 + beside, core * 4 + beside * 2 + above, core])
    words = words.astype(jnp.int32)
    core_word, quarter_word = words[3:4], words[1:2]
    nothing = jnp.zeros((1,), jnp.int32)
    quarter_order = {"own": nothing, "other": quarter_word}
    half_order = {"own": nothing, "other": core_word}
    width = qv_bias.shape[2]
    parts = width // GROUP
    rows, depth = inputs.shape
    units_here = up_bias.shape[1]
    clock = Clock()

    def qkv_block(part):
        return (qkv_weight, (1, 3, QUARTER, GROUP), lambda word: (0, 0, word[1], part))

    pieces_now = take_blocks(words, [qkv_block(0), qkv_block(1)])
    clock.tick(pieces_now[0])
    fetch = {name: FetchQuarters(clock, piece) for name, piece in zip("ab", pieces_now)}
    pieces_now = take_blocks(
        words,
        [
            (clock.hold(out_weight), (1, width, QUARTER), lambda word: (0, 0, word[1])),
            (up_weight, (1, depth // 8, units_here), lambda word: (0, word[2], 0)),
            (down_weight, (1, units_here, depth // 8), lambda word: (0, 0, word[2])),
        ],
    )
    clock.tick(pieces_now[0])
    fetch["out"] = FetchQuarters(clock, pieces_now[0])
    fetch["up"] = FetchHalves(clock, words, pieces_now[1], 1)
    fetch["down"] = FetchHalves(clock, words, pieces_now[2], 2)
    biases = jnp.concatenate([qv_bias[:, 0], qv_bias[:, 1], up_bias], 1)
    biases = {"own": biases}
    gains, shifts = norm_gain[0], norm_shift[0]
    saved = {"own": (), "other": ()}
    qkv_w = {("own", part): (qkv_weight,) for part in range(parts)}
    up_w, down_w, out_w = {"own": (up_weight,)}, {"own": (down_weight,)}, {"own": (out_weight,)}
    units = {}

    def run_heads(side, part):
        bias = biases[side] if side == "own" else clock.hold(biases[side])
        if side == "other":
            qkv_w[side, part] = fetch["ab"[part]].parts
        saved[side] = heads_forward(
            quarter_order[side],
            qkv_w[side, part],
            clock.hold(inputs),
            bias,
            part,
            parts,
            saved[side],
        )
        clock.tick(saved[side][1])

    def run_units(side):
        bias = biases[side] if side == "own" else clock.hold(biases[side])
        units[side] = units_forward(
            half_order[side], clock.hold(hidden_low), up_w[side], bias, down_w[side]
        )
        clock.tick(units[side][2])

    for action in FORWARD:
        if action == "biases":
            biases["other"] = swap(clock.hold(biases["own"]), 1, "mp")
        elif action == "project":
            out_w["other"] = fetch["out"].parts
            pre_first, hidden, hidden_low = project(
                quarter_word,
                (saved["own"][1], saved["other"][1]),
                out_weight,
                out_w["other"],
                clock.hold(inputs),
                out_bias,
                gains[0:1],
                shifts[0:1],
            )
            clock.tick(hidden_low)
        elif action == "units":
            run_units("own")
        elif isinstance(action, tuple):
            run_heads(*action)
        else:
            fetch[action].step()
    up_w["other"], down_w["other"] = fetch["up"].parts, fetch["down"].parts
    run_units("other")
    layer_out, grad_second, second_low, gain_two, shift_two, down_sum = turn(
        (units["own"][2], units["other"][2]),
        hidden,
        cotangent,
        down_bias,
        gains[1:2],
        shifts[1:2],
    )
    clock.tick(second_low)
    keep, received, totals, up_sums, head_sums = {}, {}, [], {}, {}
    state = {}

    def run_units_back(part):
        kept, sent, total, up_sums[part] = units_back(
            core_word,
            core_word,
            clock.hold(second_low),
            hidden_low,
            units,
            up_w,
            down_w,
            part,
            2,
        )
        keep["m", part], received["m", part] = kept, swap(sent, 1)
        totals.append(total)
        clock.tick(total)

    def run_first_back():
        state["first"] = first_back(totals, clock.hold(grad_second), pre_first, gains[0:1])
        state["grad_x"] = state["first"][0]
        clock.tick(state["first"][1])

    def run_heads_back(part):
        kept, sent, grad_x, head_sums[part] = heads_back(
            core_word,
            quarter_word,
            saved,
            part,
            inputs,
            clock.hold(state["first"][1]),
            {side: qkv_w[side, part] for side in ("own", "other")},
            out_w,
            state["grad_x"],
        )
        keep["h", part], received["h", part] = kept, swap(sent, 1)
        state["grad_x"] = grad_x
        clock.tick(grad_x)

    def gather_small():
        def small_of(side):
            sums = [head_sums[part][side, 0] for part in range(parts)]
            entries = [entry[:GROUP] for entry in sums] + [entry[2 * GROUP :] for entry in sums]
            for part in range(2):
                steps = up_sums[part].shape[0] // 2
                entries.append(up_sums[part][side * steps : (side + 1) * steps].reshape(-1))
            return jnp.concatenate(entries)

        gain_one, shift_one, out_sum = state["first"][2:]
        sums = (out_sum, gain_one, gain_two, shift_one, shift_two, down_sum)
        split = [small_of(0), small_of(1)]
        every = lax.all_gather(
            jnp.concatenate(split + [entry[0] for entry in sums]), ("dp", "mp"), axis=0
        )
        state["every"], state["split"] = every, split[0].shape[0]

    def add_small():
        every = clock.hold(state["every"])
        split_width = state["split"]
        odd = (lax.broadcasted_iota(jnp.int32, (every.shape[0], 1), 0) % 2) == 1
        same = [
            jnp.sum(jnp.where(odd == (number == 1), every, 0.0), axis=0) for number in range(2)
        ]
        straight = same[0][:split_width] + same[1][split_width : 2 * split_width]
        turned = same[1][:split_width] + same[0][split_width : 2 * split_width]
        split_sum = jnp.where(lax.axis_index("mp") == 0, straight, turned)
        shared = (same[0] + same[1])[2 * split_width :].reshape(6, -1)
        clock.tick(split_sum, shared)
        state["small"] = (
            split_sum[: 2 * width].reshape(1, 2, width),
            split_sum[2 * width :].reshape(1, -1),
            shared,
        )

    pieces = {}
    outcome = {}

    def run_piece(kind, number):
        key = (kind, number)
        if key not in pieces:
            orders = MLP_ORDERS if kind == "m" else HEAD_ORDERS

            def source(side):
                return [(keep[key], side), (received[key], side)]

            pieces[key] = Piece(clock, words, orders[number], source, 4, kind in DIRECT)
        pieces[key].step()
        both = [pieces.get((kind, other)) for other in range(2)]
        if kind not in outcome and all(piece and piece.complete for piece in both):
            ends = [array for piece in both for array in (piece.total, piece.flight[0])]
            ends[0] = clock.hold(ends[0])
            outcome[kind] = finish_units(core_word, ends) if kind == "m" else finish_heads(core_word, ends)
            clock.tick(outcome[kind][0])

    for action in BACKWARD:
        name, *rest = action
        if name == "ub":
            run_units_back(*rest)
        elif name == "fb":
            run_first_back()
        elif name == "hb":
            run_heads_back(*rest)
            if rest[0] == parts - 1:
                gather_small()
        elif name == "small":
            add_small()
        else:
            run_piece(*action)
    for kind in "mh":
        while kind not in outcome:
            for number in range(2):
                if not pieces[kind, number].complete:
                    run_piece(kind, number)
    grad_x = state["grad_x"]
    grad_down, grad_up = outcome["m"]
    grad_qkv, grad_out_w = outcome["h"]

    grad_qv_bias, grad_up_bias, shared = state["small"]
    return (
        layer_out,
        grad_x,
        grad_qkv[None],
        grad_qv_bias,
        grad_out_w[None],
        shared[0:1],
        shared[1:3][None],
        shared[3:5][None],
        grad_up[None],
        grad_up_bias,
        grad_down[None],
        shared[5:6],
    )


def body(inputs, *others):
    rows = inputs.shape[0]
    shared = lax.axis_size("mp") == 2 and lax.axis_size("dp") == 16
    if rows % PAGE == 0 and shared:
        return whole_page_body(inputs, *others)
    return spread_body(inputs, *others)


def solution(mesh):
    placed = (
        P(("dp", "mp"), None),
        P(None, None, None, "mp"),
        P(None, None, "mp"),
        P(None, "mp", None),
        P(),
        P(),
        P(),
        P(None, None, "mp"),
        P(None, "mp"),
        P(None, "mp", None),
        P(),
        P(("dp", "mp"), None),
    )
    return jax.shard_map(
        body,
        mesh=mesh,
        in_specs=placed,
        out_specs=(
            P(("dp", "mp"), None),
            P(("dp", "mp"), None),
            P(None, None, None, "mp"),
            P(None, None, "mp"),
            P(None, "mp", None),
            P(),
            P(),
            P(),
            P(None, None, "mp"),
            P(None, "mp"),
            P(None, "mp", None),
            P(),
        ),
        check_vma=False,
    )
```
